128 devices in a mesh: lat: 8 (over x, core), lon: 16 (over z, y).
Axes of the slice: x: 4, y: 4, z: 4, core: 2. Of those that a mesh axis runs over, the one named last changes fastest.
Arguments:
- spectra: bfloat16 [65536, 616], P(('lat', 'lon')), may hold values from -6 to 6
- owner: int32 [65536, 1], P(('lat', 'lon')), may hold values from 0 to 127; in each aligned block of 512 rows (0 to 511, 512 to 1023, ...) at most 8 rows name the same one
- cell: int32 [65536], P(('lat', 'lon')), may hold values from 0 to 2047
- w_in: bfloat16 [616, 512], replicated, may hold values from -0.25 to 0.25
- w_out: bfloat16 [512, 512], replicated, may hold values from -0.25 to 0.25
- w_point: bfloat16 [512, 512], replicated, may hold values from -0.25 to 0.25
- w_depth: float32 [9, 512], replicated, may hold values from -2 to 2
- cotangent: bfloat16 [128, 2048, 512], P('lat', 'lon'), may hold values from -6 to 6
Outputs:
- latent: bfloat16 [128, 2048, 512], P('lat', 'lon')
- grad_in: float32 [616, 512], replicated
- grad_out: float32 [512, 512], replicated
- grad_point: float32 [512, 512], replicated
- grad_depth: float32 [9, 512], replicated
The draws below stay inside these ranges and needn't reach their ends.
Inputs may be any that keep to these rules, and one draw needn't show every extreme that they name: `owner`: among the 512 rows of one device at most 8 name the same tile, a bound that some block reaches.
All inputs are finite; a program needn't handle non-finite values.
Results may differ from the reference program's by a relative error of at most 0.007.
Values may be sent and summed in bfloat16 or wider, within the bound.
A program may use at most 64 MiB of HBM per device.

```python
import math
import jax
import jax.numpy as jnp
import numpy as np
from jax import lax

SPEC = 616
HID = 512
C = 512
OBS_DEV = 512
CAP = 8
CLAT = 16
CLON = 128
TILES = 128
CELLS = 2048
OBS = 65536
LAT = 128
LON = 2048
N_LON = 16


def touch_ends(array, own_key, low, top_value):
    longest = array.shape.index(max(array.shape))
    spots = []
    for shift in (0, 1):
        where = [jax.random.randint(jax.random.fold_in(own_key, axis), (), 0, length) for axis, length in enumerate(array.shape)]
        where[longest] = (where[longest] + shift) % array.shape[longest]
        spots.append(tuple(where))
    return array.at[spots[0]].set(low).at[spots[1]].set(top_value)


def levels(key, dims, split, least, top_value):
    loudness, own = 1.0, jax.random.fold_in(key, 6)
    for position, shards_of in split:
        draws = jnp.exp(jax.random.uniform(jax.random.fold_in(own, position), (shards_of,), jnp.float32, least / len(split), top_value / len(split)))
        loudness = loudness * jnp.repeat(draws, dims[position] // shards_of).reshape([-1 if axis == position else 1 for axis in range(len(dims))])
    return loudness


def routed_block(stream_key, own, number, rows, number_of, top, reach, lean):
    order = jax.random.permutation(stream_key, number_of)
    heavy_load, common = load_shares(number_of, rows * top, reach, lean, True), load_shares(number_of, rows * top, reach, lean, False)
    places = jnp.arange(number_of)

    def named(sizes, rotation):
        used = int((sizes > 0).sum())
        fixed = max(1, used // 4)
        shifted = fixed + (places - fixed + rotation * (used - fixed)) % max(1, number_of - fixed)
        return jnp.zeros((number_of,), jnp.int32).at[order[jnp.where(places < fixed, places, shifted)]].set(jnp.asarray(sizes, jnp.int32))

    sizes = jnp.where(number % 4 == 0, named(heavy_load, number // 4), named(common, number - number // 4 - 1))
    mixed = jax.random.permutation(jax.random.fold_in(own, 3), number_of)
    giver, sink = mixed[0:number_of // 2 * 2:2], mixed[1:number_of // 2 * 2:2]
    slack = jnp.minimum(sizes[giver] - 1, reach - sizes[sink]) // 2
    slack = jnp.where((giver == order[0]) | (sink == order[0]) | (sizes[sink] == 0), 0, jnp.maximum(slack, 0))
    shifted = jax.random.randint(jax.random.fold_in(own, 4), (number_of // 2,), 0, 1 << 20) % (slack + 1)
    sizes = sizes.at[giver].add(-shifted).at[sink].add(shifted)
    labels = jnp.searchsorted(jnp.cumsum(sizes), jnp.arange(rows * top), side="right").astype(jnp.int32)
    table = labels.reshape(top, rows).T
    table = table[jax.random.permutation(jax.random.fold_in(own, 1), rows)]
    rotation = jax.random.randint(jax.random.fold_in(own, 2), (rows, 1), 0, top)
    return jnp.take_along_axis(table, (jnp.arange(top)[None, :] + rotation) % top, axis=1)


def load_shares(number_of, total, most, slope, full):
    weights = [(1 << 20) // math.isqrt(rank ** slope) + 1 for rank in range(1, number_of + 1)]
    largest = most if full else min(most, max(-(-total // number_of), total * weights[0] // sum(weights)))
    least = 1 if total - largest >= number_of - 1 else 0
    given, spare = [largest] + [least] * (number_of - 1), total - largest - least * (number_of - 1)
    while spare > 0:
        movable = [i for i in range(1, number_of) if given[i] < largest] or [i for i in range(1, number_of) if given[i] < most]
        pool, budget = sum([weights[i] for i in movable]), spare
        for i in movable:
            more = min(most - given[i], max(1, budget * weights[i] // pool), spare)
            given[i] = given[i] + more
            spare = spare - more
    return np.array(given)


def scatter_about(own_key, extent, deviation, most, split=(), kind=jnp.bfloat16):
    values = deviation * jax.random.normal(own_key, extent, jnp.float32)
    if split:
        values = values * levels(own_key, extent, split, -0.22, 0.18)
    return jnp.clip(values, -most, most).astype(kind)


def setup_inputs(seed: int = 0) -> dict:
    keys = jax.random.split(jax.random.key(seed), 9)
    spectra = scatter_about(keys[0], (OBS, SPEC), 1.0, 6.0, ((0, 128),))
    owner_keys = jax.random.split(jax.random.fold_in(keys[1], 1), OBS // OBS_DEV)
    owner_turns = jax.random.permutation(jax.random.fold_in(keys[1], 3), OBS // OBS_DEV)
    owner = jax.vmap(lambda own, number: routed_block(jax.random.fold_in(keys[1], 2), own, number, OBS_DEV, TILES, 1, CAP, 2))(owner_keys, owner_turns).reshape((OBS, 1))
    cell = touch_ends(jax.random.randint(keys[2], (OBS,), 0, CELLS), jax.random.fold_in(keys[2], 1), 0, CELLS - 1).astype(jnp.int32)
    w_in = scatter_about(keys[3], (SPEC, HID), SPEC ** -0.5, 0.25)
    w_out = scatter_about(keys[4], (HID, C), HID ** -0.5, 0.25)
    w_point = scatter_about(keys[5], (C, C), C ** -0.5, 0.25)
    w_depth = scatter_about(keys[6], (9, C), 9 ** -0.5, 2.0, (), jnp.float32)
    cotangent = scatter_about(keys[7], (LAT, LON, C), 1.0, 6.0, ((0, 8), (1, 16)))
    return dict(spectra=spectra, owner=owner, cell=cell, w_in=w_in, w_out=w_out, w_point=w_point, w_depth=w_depth, cotangent=cotangent)


offsets = [(a, b) for a in (-1, 0, 1) for b in (-1, 0, 1)]

def extend(field):
    wide = field.astype(jnp.float32)
    wide = jnp.concatenate([wide[:, -1:], wide, wide[:, :1]], axis=1)
    return jnp.pad(wide, ((1, 1), (0, 0), (0, 0)))

def reference(spectra, owner, cell, w_in, w_out, w_point, w_depth, cotangent):
    tile = owner[:, 0].astype(jnp.int32)
    grid_row = tile // N_LON * CLAT + cell // CLON
    grid_col = tile % N_LON * CLON + cell % CLON
    place = (grid_row * LON + grid_col).astype(jnp.int32)
    preact = jnp.dot(spectra, w_in, preferred_element_type=jnp.float32)
    hidden = jax.nn.silu(preact).astype(jnp.bfloat16)
    embedded = jnp.dot(hidden, w_out, preferred_element_type=jnp.float32).astype(jnp.bfloat16)
    grid = jax.ops.segment_sum(embedded.astype(jnp.float32), place, num_segments=LAT * LON)
    grid = grid.astype(jnp.bfloat16).reshape(LAT, LON, C)
    padded = extend(grid)
    mixed = jnp.zeros((LAT, LON, C), jnp.float32)
    for k, (a, b) in enumerate(offsets):
        mixed = mixed + w_depth[k] * padded[1 + a:1 + a + LAT, 1 + b:1 + b + LON]
    mixed = mixed.astype(jnp.bfloat16)
    mixed_rows = mixed.reshape(-1, C)
    latent = grid.astype(jnp.float32) + jnp.dot(mixed_rows, w_point, preferred_element_type=jnp.float32).reshape(LAT, LON, C)
    latent = latent.astype(jnp.bfloat16)
    cot_rows = cotangent.reshape(-1, C)
    grad_point = jnp.dot(mixed_rows.T, cot_rows, preferred_element_type=jnp.float32)
    g_mixed = jnp.dot(cot_rows, w_point.T, preferred_element_type=jnp.float32).astype(jnp.bfloat16).reshape(LAT, LON, C)
    g_mixed_f = g_mixed.astype(jnp.float32)
    grad_depth = jnp.stack([lax.optimization_barrier(jnp.sum(g_mixed_f * padded[1 + a:1 + a + LAT, 1 + b:1 + b + LON], axis=(0, 1))) for a, b in offsets])
    padded_g = extend(g_mixed)
    g_grid = cotangent.astype(jnp.float32)
    for k, (a, b) in enumerate(offsets):
        g_grid = g_grid + w_depth[k] * padded_g[1 - a:1 - a + LAT, 1 - b:1 - b + LON]
    g_grid = g_grid.astype(jnp.bfloat16).reshape(-1, C)
    g_embedded = g_grid[place]
    grad_out = jnp.dot(hidden.T, g_embedded, preferred_element_type=jnp.float32)
    g_hidden = jnp.dot(g_embedded, w_out.T, preferred_element_type=jnp.float32)
    sigmoid_pre = jax.nn.sigmoid(preact)
    g_preact = (g_hidden * sigmoid_pre * (1.0 + preact * (1.0 - sigmoid_pre))).astype(jnp.bfloat16)
    grad_in = jnp.dot(spectra.T, g_preact, preferred_element_type=jnp.float32)
    obs_scale = 1.0 / jnp.sqrt(jnp.float32(OBS))
    cell_scale = 1.0 / jnp.sqrt(jnp.float32(LAT * LON))
    return (latent, grad_in * obs_scale, grad_out * obs_scale, grad_point * cell_scale, grad_depth * cell_scale)
```

```python
import functools

import jax
import jax.numpy as jnp
from jax import lax
from jax.experimental import pallas as pl
from jax.experimental.pallas import tpu as pltpu
from jax.sharding import PartitionSpec as P

offsets = [(a, b) for a in (-1, 0, 1) for b in (-1, 0, 1)]
f32, bf16, i32 = jnp.float32, jnp.bfloat16, jnp.int32

N_LAT, N_LON, SIDE = 8, 16, 4
CHIPS = N_LAT // 2 * N_LON
CAP = 8
SLOT = 2 * CAP
SLOTS = CHIPS * SLOT
OBS = 512
C = 512
CLAT, CLON = 16, 128
CELLS = CLAT * CLON
SPEC = 616
META = 128
ROWS_IN = 624
ROWS = ROWS_IN + C + C + 16
BLOCKS = ROWS // 16
HALF = BLOCKS // 2
HALF_ROWS = HALF * 16

VMEM = pltpu.VMEM


def vmem():
    return pl.BlockSpec(memory_space=pltpu.VMEM)


def dot(a, b, dims):
    return lax.dot_general(a, b, (dims, ((), ())), preferred_element_type=f32)


class Place:
    def __init__(self):
        self.lat = lax.axis_index("lat")
        self.lon = lax.axis_index("lon")
        self.core = self.lat % 2
        self.x = self.lat // 2
        self.chip = self.x * N_LON + self.lon
        self.sibling = (self.x * 2 + 1 - self.core, self.lon)

    def peer(self, step):
        step = (step * 37) % CHIPS
        x = (self.x + step // N_LON) % (N_LAT // 2)
        z = (self.lon // SIDE + step // SIDE) % SIDE
        y = (self.lon + step) % SIDE
        lon = z * SIDE + y
        return x * N_LON + lon, (x * 2 + self.core, lon)

    def of_chip(self, chip):
        return (chip // N_LON * 2 + self.core, chip % N_LON)


def remote(src, dst, send, recv, device):
    return pltpu.make_async_remote_copy(
        src_ref=src,
        dst_ref=dst,
        send_sem=send,
        recv_sem=recv,
        device_id=device,
        device_id_type=pl.DeviceIdType.MESH,
    )


def greet(place, halo):
    barrier = pltpu.get_barrier_semaphore()

    def hello(device):
        pl.semaphore_signal(
            barrier, inc=1, device_id=device, device_id_type=pl.DeviceIdType.MESH
        )

    def one(step, carry):
        hello(place.peer(step)[1])
        return carry

    lax.fori_loop(1, CHIPS, one, 0)
    if not halo:
        hello(place.sibling)
        return barrier, CHIPS
    for side in (-1, 1):
        inside = (place.lat + side >= 0) & (place.lat + side < N_LAT)

        @pl.when(inside)
        def _(side=side):
            for turn in (-1, 0, 1):
                hello((place.lat + side, (place.lon + turn + N_LON) % N_LON))

    edges = (place.lat > 0).astype(i32) + (place.lat < N_LAT - 1).astype(i32)
    return barrier, CHIPS - 1 + 3 * edges


class Halo:
    def __init__(self, place, rows, cols, to_rows, to_cols, to_diag, send, recv):
        self.place = place
        self.outs = (to_rows, to_diag)
        lat, lon = place.lat, place.lon
        east, west = (lon + 1) % N_LON, (lon + N_LON - 1) % N_LON
        has_north, has_south = lat > 0, lat < N_LAT - 1
        south, north = jnp.minimum(lat + 1, N_LAT - 1), jnp.maximum(lat - 1, 0)
        plan = [
            (rows.at[1], to_rows.at[0], (south, lon), has_south, has_north),
            (rows.at[0], to_rows.at[1], (north, lon), has_north, has_south),
            (cols.at[1], to_cols.at[0], (lat, east), None, None),
            (cols.at[0], to_cols.at[1], (lat, west), None, None),
            (cols.at[1], to_diag.at[0], (south, east), has_south, has_north),
            (cols.at[0], to_diag.at[1], (south, west), has_south, has_north),
            (cols.at[1], to_diag.at[2], (north, east), has_north, has_south),
            (cols.at[0], to_diag.at[3], (north, west), has_north, has_south),
        ]
        self.plan = [
            (remote(src, dst, send.at[i], recv.at[i], device), sends, receives)
            for i, (src, dst, device, sends, receives) in enumerate(plan)
        ]

    def start(self):
        for copy, sends, _ in self.plan:
            if sends is None:
                copy.start()
            else:
                pl.when(sends)(copy.start)

    def wait(self):
        for copy, sends, receives in self.plan:
            if sends is None:
                copy.wait_send()
                copy.wait_recv()
            else:
                pl.when(sends)(copy.wait_send)
                pl.when(receives)(copy.wait_recv)

    def clear_outside(self):
        rows, diag = self.outs

        @pl.when(self.place.lat == 0)
        def _():
            rows[0] = jnp.zeros_like(rows[0])
            diag[0] = jnp.zeros_like(diag[0])
            diag[1] = jnp.zeros_like(diag[1])

        @pl.when(self.place.lat == N_LAT - 1)
        def _():
            rows[1] = jnp.zeros_like(rows[1])
            diag[2] = jnp.zeros_like(diag[2])
            diag[3] = jnp.zeros_like(diag[3])


HALO_OUT = [
    jax.ShapeDtypeStruct((2, CLON, C), bf16),
    jax.ShapeDtypeStruct((2, CLAT, C), bf16),
    jax.ShapeDtypeStruct((4, CLAT, C), bf16),
]


def encode_kernel(spec_t, rows, w_in, w_out, preact, hidden, emb, route):
    pre = dot(spec_t[...], w_in[...], ((0,), (0,)))
    preact[...] = pre
    hid = (pre * (1.0 / (1.0 + jnp.exp(-pre)))).astype(bf16)
    hidden[...] = hid
    emb[:, :C] = dot(hid, w_out[...], ((1,), (0,))).astype(bf16)
    values = rows[...]
    down = lax.broadcasted_iota(i32, (OBS, OBS), 0)
    across = lax.broadcasted_iota(i32, (OBS, OBS), 1)
    eye = (down == across).astype(f32).astype(bf16)
    columns = dot(eye, values, ((1,), (1,)))
    tile_col, high_col, low_col = columns[:, 0:1], columns[:, 1:2], columns[:, 2:3]
    tile_row = values[0:1, :].astype(f32)
    tiles = N_LAT * N_LON
    hits = (tile_col == lax.broadcasted_iota(i32, (OBS, tiles), 1).astype(f32)).astype(f32)
    lower = (across <= down).astype(f32).astype(bf16)
    count = dot(lower, hits.astype(bf16), ((1,), (0,)))
    pos_col = (jnp.sum(count * hits, axis=1, keepdims=True) - 1.0).astype(i32)
    hits_t = (tile_row == lax.broadcasted_iota(i32, (tiles, OBS), 0).astype(f32)).astype(f32)
    upper = (down <= across).astype(f32).astype(bf16)
    count_t = dot(hits_t.astype(bf16), upper, ((1,), (0,)))
    pos_row = (jnp.sum(count_t * hits_t, axis=0, keepdims=True) - 1.0).astype(i32)
    lane = lax.broadcasted_iota(i32, (OBS, META), 1)
    kind = lane // CAP
    value = jnp.where(kind == 0, high_col, jnp.where(kind == 1, low_col, 1.0))
    keep = (lane % CAP == pos_col) & (kind < 3)
    emb[:, C:] = jnp.where(keep, value, 0.0).astype(bf16)
    tile = tile_row.astype(i32)
    lat, lon = tile // N_LON, tile % N_LON
    chip = lat // 2 * N_LON + lon
    route[...] = jnp.concatenate(
        [chip * SLOT + pos_row, lat % 2, chip, jnp.zeros((5, OBS), i32)], axis=0
    )


def encode(spec_t, rows, w_in, w_out):
    return pl.pallas_call(
        encode_kernel,
        out_shape=[
            jax.ShapeDtypeStruct((OBS, C), f32),
            jax.ShapeDtypeStruct((OBS, C), bf16),
            jax.ShapeDtypeStruct((OBS, C + META), bf16),
            jax.ShapeDtypeStruct((8, OBS), i32),
        ],
        in_specs=[vmem()] * 4,
        out_specs=[vmem()] * 4,
        compiler_params=pltpu.CompilerParams(vmem_limit_bytes=40 << 20),
    )(spec_t, rows, w_in, w_out)


def slot_keys(route, mine, core):
    return jnp.where(route[1:2, :] == mine, route[0:1, :] + CAP * core, -1)


PART = 256


def forward_kernel(
    emb,
    route,
    rows,
    cols,
    arrived,
    places,
    route_sib,
    to_rows,
    to_cols,
    to_diag,
    emb_sib,
    outgoing,
    marks,
    local_sem,
    sib_send,
    sib_recv,
    data_send,
    data_recv,
    halo_send,
    halo_recv,
):
    place = Place()
    core = place.core
    barrier, count = greet(place, True)
    halo = Halo(place, rows, cols, to_rows, to_cols, to_diag, halo_send, halo_recv)
    halo.clear_outside()
    pl.semaphore_wait(barrier, count)
    swaps = [
        remote(emb, emb_sib, sib_send.at[0], sib_recv.at[0], place.sibling),
        remote(route, route_sib, sib_send.at[1], sib_recv.at[1], place.sibling),
    ]
    for copy in swaps:
        copy.start()
    halo.start()
    key = slot_keys(route[...], core, core)

    def own_part(i, carry):
        at = pl.multiple_of(i * PART, PART)
        index = lax.broadcasted_iota(i32, (PART, OBS), 0) + at
        pick = (index == key).astype(f32).astype(bf16)
        outgoing[pl.ds(at, PART), :] = dot(pick, emb[:, :C], ((1,), (0,))).astype(bf16)
        return carry

    lax.fori_loop(0, SLOTS // PART, own_part, 0)
    for copy in swaps:
        copy.wait()
    key_sib = slot_keys(route_sib[...], core, 1 - core)

    def sib_part(i, carry):
        at = pl.multiple_of(i * PART, PART)
        index = lax.broadcasted_iota(i32, (PART, OBS), 0) + at
        pick = (index == key_sib).astype(f32).astype(bf16)
        more = dot(pick, emb_sib[:, :C], ((1,), (0,)))
        outgoing[pl.ds(at, PART), :] = (
            outgoing[pl.ds(at, PART), :].astype(f32) + more
        ).astype(bf16)
        return carry

    lax.fori_loop(0, SLOTS // PART, sib_part, 0)
    chips = lax.broadcasted_iota(i32, (CHIPS, OBS), 0)

    def marked(info, values):
        wanted = (info[2:3, :] == chips) & (info[1:2, :] == core)
        return dot(wanted.astype(f32).astype(bf16), values[:, C:], ((1,), (0,)))

    own, other = marked(route, emb), marked(route_sib, emb_sib)
    marks[:, 0, :] = jnp.where(core == 0, own, other)
    marks[:, 1, :] = jnp.where(core == 0, other, own)

    def block(ref, chip):
        return ref.at[pl.ds(pl.multiple_of(chip * SLOT, SLOT), SLOT)]

    keep = [
        pltpu.make_async_copy(block(outgoing, place.chip), block(arrived, place.chip), local_sem.at[0]),
        pltpu.make_async_copy(marks.at[place.chip], places.at[place.chip], local_sem.at[1]),
    ]
    for copy in keep:
        copy.start()

    def send(step, carry):
        chip, device = place.peer(step)
        remote(
            marks.at[chip], places.at[place.chip], data_send.at[1], data_recv.at[1], device
        ).start()
        remote(
            block(outgoing, chip),
            block(arrived, place.chip),
            data_send.at[0],
            data_recv.at[0],
            device,
        ).start()
        return carry

    lax.fori_loop(1, CHIPS, send, 0)
    for copy in keep:
        copy.wait()
    halo.wait()
    some = pl.ds(0, (CHIPS - 1) * SLOT)
    whole = [
        remote(
            outgoing.at[some], arrived.at[some], data_send.at[0], data_recv.at[0], place.sibling
        ),
        remote(
            marks.at[pl.ds(0, CHIPS - 1)],
            places.at[pl.ds(0, CHIPS - 1)],
            data_send.at[1],
            data_recv.at[1],
            place.sibling,
        ),
    ]
    for copy in whole:
        copy.wait_recv()
        copy.wait_send()


def forward_exchange(emb, route, rows, cols):
    dma = pltpu.SemaphoreType.DMA
    return pl.pallas_call(
        forward_kernel,
        out_shape=[
            jax.ShapeDtypeStruct((SLOTS, C), bf16),
            jax.ShapeDtypeStruct((CHIPS, 2, META), f32),
            jax.ShapeDtypeStruct((8, OBS), i32),
        ]
        + HALO_OUT,
        in_specs=[vmem()] * 4,
        out_specs=[vmem()] * 6,
        scratch_shapes=[
            VMEM((OBS, C + META), bf16),
            VMEM((SLOTS, C), bf16),
            VMEM((CHIPS, 2, META), f32),
            dma((2,)),
            dma((2,)),
            dma((2,)),
            dma((2,)),
            dma((2,)),
            dma((8,)),
            dma((8,)),
        ],
        compiler_params=pltpu.CompilerParams(
            collective_id=0, has_side_effects=True, vmem_limit_bytes=40 << 20
        ),
    )(emb, route, rows, cols)


def backward_kernel(
    grads,
    route,
    route_sib,
    rows,
    cols,
    result,
    to_rows,
    to_cols,
    to_diag,
    returned,
    part,
    part_sib,
    local_sem,
    sib_send,
    sib_recv,
    data_send,
    data_recv,
    halo_send,
    halo_recv,
):
    place = Place()
    core = place.core
    barrier, count = greet(place, True)
    halo = Halo(place, rows, cols, to_rows, to_cols, to_diag, halo_send, halo_recv)
    halo.clear_outside()
    pl.semaphore_wait(barrier, count)
    halo.start()

    def block(ref, chip):
        return ref.at[pl.ds(pl.multiple_of(chip * SLOT, SLOT), SLOT)]

    keep = pltpu.make_async_copy(
        block(grads, place.chip), block(returned, place.chip), local_sem.at[0]
    )
    keep.start()

    def send(step, carry):
        chip, device = place.peer(step)
        remote(
            block(grads, chip),
            block(returned, place.chip),
            data_send.at[0],
            data_recv.at[0],
            device,
        ).start()
        return carry

    lax.fori_loop(1, CHIPS, send, 0)
    keep.wait()
    halo.wait()
    some = pl.ds(0, (CHIPS - 1) * SLOT)
    whole = remote(
        grads.at[some], returned.at[some], data_send.at[0], data_recv.at[0], place.sibling
    )
    whole.wait_recv()
    whole.wait_send()

    def gathered(key):
        total = jnp.zeros((OBS, C), f32)
        for at in range(0, SLOTS, PART):
            index = lax.broadcasted_iota(i32, (PART, OBS), 0) + at
            pick = (index == key).astype(f32).astype(bf16)
            total = total + dot(pick, returned[at : at + PART, :], ((0,), (0,)))
        return total

    part[...] = gathered(slot_keys(route_sib[...], core, 1 - core)).astype(bf16)
    swap = remote(part, part_sib, sib_send.at[0], sib_recv.at[0], place.sibling)
    swap.start()
    own = gathered(slot_keys(route[...], core, core))
    swap.wait()
    result[...] = (own + part_sib[...].astype(f32)).astype(bf16)


def backward_exchange(grads, route, route_sib, rows, cols):
    dma = pltpu.SemaphoreType.DMA
    return pl.pallas_call(
        backward_kernel,
        out_shape=[jax.ShapeDtypeStruct((OBS, C), bf16)] + HALO_OUT,
        in_specs=[vmem()] * 5,
        out_specs=[vmem()] * 4,
        scratch_shapes=[
            VMEM((SLOTS, C), bf16),
            VMEM((OBS, C), bf16),
            VMEM((OBS, C), bf16),
            dma((1,)),
            dma((1,)),
            dma((1,)),
            dma((1,)),
            dma((1,)),
            dma((8,)),
            dma((8,)),
        ],
        compiler_params=pltpu.CompilerParams(
            collective_id=1, has_side_effects=True, vmem_limit_bytes=40 << 20
        ),
    )(grads, route, route_sib, rows, cols)


def sum_kernel(
    parts,
    result,
    to_sib,
    from_sib,
    chip_sum,
    gather,
    owned,
    local_sem,
    sib_send,
    sib_recv,
    data_send,
    data_recv,
    share_send,
    share_recv,
):
    place = Place()
    core, me = place.core, place.chip
    mine = pl.ds(pl.multiple_of(core * HALF_ROWS, 16), HALF_ROWS)
    other = pl.ds(pl.multiple_of((1 - core) * HALF_ROWS, 16), HALF_ROWS)
    barrier, count = greet(place, False)
    to_sib[...] = parts[other, :].astype(bf16)
    pl.semaphore_wait(barrier, count)
    swap = remote(to_sib, from_sib, sib_send.at[0], sib_recv.at[0], place.sibling)
    swap.start()
    swap.wait()
    chip_sum[...] = (parts[mine, :] + from_sib[...].astype(f32)).astype(bf16)

    def block(ref, chip):
        return ref.at[pl.ds(pl.multiple_of(chip * 16, 16), 16)]

    @pl.when(me < HALF)
    def _():
        pltpu.make_async_copy(block(chip_sum, me), gather.at[me], local_sem.at[0]).start()

    def send(step, carry):
        chip, device = place.peer(step)

        @pl.when(chip < HALF)
        def _():
            remote(
                block(chip_sum, chip), gather.at[me], data_send.at[0], data_recv.at[0], device
            ).start()

        return carry

    lax.fori_loop(1, CHIPS, send, 0)
    base = core * HALF_ROWS

    def final(chip):
        return result.at[pl.ds(pl.multiple_of(base + chip * 16, 16), 16)]

    @pl.when(me < HALF)
    def _():
        pltpu.make_async_copy(block(chip_sum, me), gather.at[me], local_sem.at[0]).wait()
        some = pl.ds(0, CHIPS - 1)
        remote(gather.at[some], gather.at[some], data_send.at[0], data_recv.at[0], place.sibling).wait_recv()
        total = jnp.sum(gather[...].astype(f32), axis=0)
        owned[...] = total.astype(bf16)
        pltpu.make_async_copy(owned, final(me), local_sem.at[1]).start()

        def share(step, carry):
            _, device = place.peer(step)
            remote(owned, final(me), share_send.at[0], share_recv.at[0], device).start()
            return carry

        lax.fori_loop(1, CHIPS, share, 0)
        pltpu.make_async_copy(owned, final(me), local_sem.at[1]).wait()
        remote(gather.at[some], gather.at[some], share_send.at[0], share_recv.at[0], place.sibling).wait_send()
        few = pl.ds(0, (HALF - 1) * 16)
        remote(chip_sum.at[few], chip_sum.at[few], data_send.at[0], share_recv.at[0], place.sibling).wait_recv()
        remote(chip_sum.at[few], chip_sum.at[few], data_send.at[0], share_recv.at[0], place.sibling).wait_send()

    @pl.when(me >= HALF)
    def _():
        remote(chip_sum, chip_sum, data_send.at[0], share_recv.at[0], place.sibling).wait_recv()
        remote(chip_sum, chip_sum, data_send.at[0], share_recv.at[0], place.sibling).wait_send()

    last = remote(result.at[mine], result.at[mine], sib_send.at[1], sib_recv.at[1], place.sibling)
    last.start()
    last.wait()


def sum_everywhere(parts):
    dma = pltpu.SemaphoreType.DMA
    return pl.pallas_call(
        sum_kernel,
        out_shape=jax.ShapeDtypeStruct((ROWS, C), bf16),
        in_specs=[vmem()],
        out_specs=vmem(),
        scratch_shapes=[
            VMEM((HALF_ROWS, C), bf16),
            VMEM((HALF_ROWS, C), bf16),
            VMEM((HALF_ROWS, C), bf16),
            VMEM((CHIPS, 16, C), bf16),
            VMEM((16, C), bf16),
            dma((2,)),
            dma((2,)),
            dma((2,)),
            dma((1,)),
            dma((1,)),
            dma((1,)),
            dma((1,)),
        ],
        compiler_params=pltpu.CompilerParams(
            collective_id=2, has_side_effects=True, vmem_limit_bytes=40 << 20
        ),
    )(parts)


def edges(field):
    rows = jnp.stack([field[0], field[CLAT - 1]])
    cols = jnp.stack([field[:, 0], field[:, CLON - 1]])
    return rows, cols


def joined(field, rows, cols, diag):
    north = jnp.concatenate([diag[0, CLAT - 1 :], rows[0], diag[1, CLAT - 1 :]], axis=0)
    south = jnp.concatenate([diag[2, :1], rows[1], diag[3, :1]], axis=0)
    middle = jnp.concatenate([cols[0][:, None], field, cols[1][:, None]], axis=1)
    return jnp.concatenate([north[None], middle, south[None]], axis=0).astype(f32)


def on_device(spectra, owner, cell, w_in, w_out, w_point, w_depth, cotangent):
    cot_rows = cotangent.reshape(CELLS, C)
    target = owner[:, 0]
    zero = jnp.zeros((13, OBS), bf16)
    rows = jnp.concatenate(
        [jnp.stack([target, cell // 16, cell % 16]).astype(bf16), zero], axis=0
    )
    preact, hidden, emb, route = encode(spectra.T, rows, w_in, w_out)
    g_mixed = dot(cot_rows, w_point, ((1,), (1,))).astype(bf16).reshape(CLAT, CLON, C)
    arrived, marks, route_sib, g_rows, g_cols, g_diag = forward_exchange(emb, route, *edges(g_mixed))
    high, low, valid = (marks[:, :, i * CAP : (i + 1) * CAP] for i in range(3))
    places = (high * 16.0 + low + valid - 1.0).astype(i32).reshape(SLOTS)
    one_hot = (places[None, :] == jnp.arange(CELLS, dtype=i32)[:, None]).astype(bf16)
    grid_rows = jnp.dot(one_hot, arrived, preferred_element_type=f32).astype(bf16)
    grid = grid_rows.reshape(CLAT, CLON, C)
    padded_g = joined(g_mixed, g_rows, g_cols, g_diag)
    g_grid = cotangent.astype(f32)
    for k, (a, b) in enumerate(offsets):
        g_grid = g_grid + w_depth[k] * padded_g[1 - a : 1 - a + CLAT, 1 - b : 1 - b + CLON]
    g_grid = g_grid.astype(bf16).reshape(CELLS, C)
    g_arrived = dot(one_hot, g_grid, ((0,), (0,))).astype(bf16)
    g_embedded, x_rows, x_cols, x_diag = backward_exchange(g_arrived, route, route_sib, *edges(grid))
    padded = joined(grid, x_rows, x_cols, x_diag)
    mixed = jnp.zeros((CLAT, CLON, C), f32)
    for k, (a, b) in enumerate(offsets):
        mixed = mixed + w_depth[k] * padded[1 + a : 1 + a + CLAT, 1 + b : 1 + b + CLON]
    mixed_rows = mixed.astype(bf16).reshape(CELLS, C)
    latent = grid_rows.astype(f32) + jnp.dot(mixed_rows, w_point, preferred_element_type=f32)
    latent = latent.astype(bf16).reshape(CLAT, CLON, C)
    grad_point = dot(mixed_rows, cot_rows, ((0,), (0,)))
    g_mixed_f = g_mixed.astype(f32)
    grad_depth = jnp.stack(
        [
            jnp.sum(g_mixed_f * padded[1 + a : 1 + a + CLAT, 1 + b : 1 + b + CLON], axis=(0, 1))
            for a, b in offsets
        ]
    )
    grad_out = dot(hidden, g_embedded, ((0,), (0,)))
    g_hidden = dot(g_embedded, w_out, ((1,), (1,)))
    sig = jax.nn.sigmoid(preact)
    g_preact = (g_hidden * sig * (1.0 + preact * (1.0 - sig))).astype(bf16)
    grad_in = dot(spectra, g_preact, ((0,), (0,)))
    parts = jnp.concatenate(
        [
            grad_in,
            jnp.zeros((ROWS_IN - SPEC, C), f32),
            grad_out,
            grad_point,
            grad_depth,
            jnp.zeros((7, C), f32),
        ],
        axis=0,
    )
    total = sum_everywhere(parts).astype(f32)
    tiles = N_LAT * N_LON
    obs_scale = 1.0 / jnp.sqrt(f32(OBS * tiles))
    cell_scale = 1.0 / jnp.sqrt(f32(CELLS * tiles))
    at = ROWS_IN
    return (
        latent,
        total[:SPEC] * obs_scale,
        total[at : at + C] * obs_scale,
        total[at + C : at + 2 * C] * cell_scale,
        total[at + 2 * C : at + 2 * C + 9] * cell_scale,
    )


def solution(mesh):
    in_specs = (
        P(("lat", "lon"), None),
        P(("lat", "lon"), None),
        P(("lat", "lon")),
        P(),
        P(),
        P(),
        P(),
        P("lat", "lon", None),
    )
    out_specs = (P("lat", "lon", None), P(), P(), P(), P())
    return jax.shard_map(
        on_device, mesh=mesh, in_specs=in_specs, out_specs=out_specs, check_vma=False
    )
```

```python
import functools

import jax
import jax.numpy as jnp
from jax import lax
from jax.experimental import pallas as pl
from jax.experimental.pallas import tpu as pltpu
from jax.sharding import PartitionSpec as P

offsets = [(a, b) for a in (-1, 0, 1) for b in (-1, 0, 1)]
f32, bf16, i32 = jnp.float32, jnp.bfloat16, jnp.int32

N_LAT, N_LON, SIDE = 8, 16, 4
CHIPS = N_LAT // 2 * N_LON
CAP = 8
SLOT = 2 * CAP
SLOTS = CHIPS * SLOT
OBS = 512
C = 512
CLAT, CLON = 16, 128
CELLS = CLAT * CLON
SPEC = 616
META = 128
ROWS_IN = 624
PART = 256
CHUNK = 128

VMEM = pltpu.VMEM


def vmem():
    return pl.BlockSpec(memory_space=pltpu.VMEM)


def dot(a, b, dims):
    return lax.dot_general(a, b, (dims, ((), ())), preferred_element_type=f32)


class Place:
    def __init__(self):
        self.lat = lax.axis_index("lat")
        self.lon = lax.axis_index("lon")
        self.core = self.lat % 2
        self.x = self.lat // 2
        self.chip = self.x * N_LON + self.lon
        self.sibling = (self.x * 2 + 1 - self.core, self.lon)

    def peer(self, step):
        step = (step * 37) % CHIPS
        x = (self.x + step // N_LON) % (N_LAT // 2)
        z = (self.lon // SIDE + step // SIDE) % SIDE
        y = (self.lon + step) % SIDE
        lon = z * SIDE + y
        return x * N_LON + lon, (x * 2 + self.core, lon)

    def of_chip(self, chip):
        return (chip // N_LON * 2 + self.core, chip % N_LON)


def remote(src, dst, send, recv, device):
    return pltpu.make_async_remote_copy(
        src_ref=src,
        dst_ref=dst,
        send_sem=send,
        recv_sem=recv,
        device_id=device,
        device_id_type=pl.DeviceIdType.MESH,
    )


def greet(place, halo):
    barrier = pltpu.get_barrier_semaphore()

    def hello(device):
        pl.semaphore_signal(
            barrier, inc=1, device_id=device, device_id_type=pl.DeviceIdType.MESH
        )

    def one(step, carry):
        hello(place.peer(step)[1])
        return carry

    lax.fori_loop(1, CHIPS, one, 0)
    if not halo:
        hello(place.sibling)
        return barrier, CHIPS
    for side in (-1, 1):
        inside = (place.lat + side >= 0) & (place.lat + side < N_LAT)

        @pl.when(inside)
        def _(side=side):
            for turn in (-1, 0, 1):
                hello((place.lat + side, (place.lon + turn + N_LON) % N_LON))

    edges = (place.lat > 0).astype(i32) + (place.lat < N_LAT - 1).astype(i32)
    return barrier, CHIPS - 1 + 3 * edges


class Halo:
    def __init__(self, place, ext, cols, to_cols, to_diag, send, recv):
        self.place = place
        self.ext, self.to_diag = ext, to_diag
        lat, lon = place.lat, place.lon
        east, west = (lon + 1) % N_LON, (lon + N_LON - 1) % N_LON
        has_north, has_south = lat > 0, lat < N_LAT - 1
        south, north = jnp.minimum(lat + 1, N_LAT - 1), jnp.maximum(lat - 1, 0)
        plan = [
            (ext.at[CLAT], ext.at[0], (south, lon), has_south, has_north),
            (ext.at[1], ext.at[CLAT + 1], (north, lon), has_north, has_south),
            (cols.at[1], to_cols.at[0], (lat, east), None, None),
            (cols.at[0], to_cols.at[1], (lat, west), None, None),
            (cols.at[1], to_diag.at[0], (south, east), has_south, has_north),
            (cols.at[0], to_diag.at[1], (south, west), has_south, has_north),
            (cols.at[1], to_diag.at[2], (north, east), has_north, has_south),
            (cols.at[0], to_diag.at[3], (north, west), has_north, has_south),
        ]
        self.plan = [
            (remote(src, dst, send.at[i], recv.at[i], device), sends, receives)
            for i, (src, dst, device, sends, receives) in enumerate(plan)
        ]

    def start(self):
        for copy, sends, _ in self.plan:
            if sends is None:
                copy.start()
            else:
                pl.when(sends)(copy.start)

    def wait(self):
        for copy, sends, receives in self.plan:
            if sends is None:
                copy.wait_send()
                copy.wait_recv()
            else:
                pl.when(sends)(copy.wait_send)
                pl.when(receives)(copy.wait_recv)

    def clear_outside(self):
        @pl.when(self.place.lat == 0)
        def _():
            self.ext[0] = jnp.zeros((CLON, C), bf16)
            self.to_diag[0] = jnp.zeros((CLAT, C), bf16)
            self.to_diag[1] = jnp.zeros((CLAT, C), bf16)

        @pl.when(self.place.lat == N_LAT - 1)
        def _():
            self.ext[CLAT + 1] = jnp.zeros((CLON, C), bf16)
            self.to_diag[2] = jnp.zeros((CLAT, C), bf16)
            self.to_diag[3] = jnp.zeros((CLAT, C), bf16)


def vector_encode(spec_t, rows, w_in, w_out, preact, hidden, emb, route):
    pre = dot(spec_t[...], w_in[...], ((0,), (0,)))
    preact[...] = pre
    hid = (pre * (1.0 / (1.0 + jnp.exp(-pre)))).astype(bf16)
    hidden[...] = hid
    emb[:, :C] = dot(hid, w_out[...], ((1,), (0,))).astype(bf16)
    values = rows[...]
    down = lax.broadcasted_iota(i32, (OBS, OBS), 0)
    across = lax.broadcasted_iota(i32, (OBS, OBS), 1)
    eye = (down == across).astype(f32).astype(bf16)
    columns = dot(eye, values, ((1,), (1,)))
    tile_col, high_col, low_col = columns[:, 0:1], columns[:, 1:2], columns[:, 2:3]
    tile_row = values[0:1, :].astype(f32)
    tiles = N_LAT * N_LON
    hits = (tile_col == lax.broadcasted_iota(i32, (OBS, tiles), 1).astype(f32)).astype(f32)
    lower = (across <= down).astype(f32).astype(bf16)
    count = dot(lower, hits.astype(bf16), ((1,), (0,)))
    pos_col = (jnp.sum(count * hits, axis=1, keepdims=True) - 1.0).astype(i32)
    hits_t = (tile_row == lax.broadcasted_iota(i32, (tiles, OBS), 0).astype(f32)).astype(f32)
    upper = (down <= across).astype(f32).astype(bf16)
    count_t = dot(hits_t.astype(bf16), upper, ((1,), (0,)))
    pos_row = (jnp.sum(count_t * hits_t, axis=0, keepdims=True) - 1.0).astype(i32)
    lane = lax.broadcasted_iota(i32, (OBS, META), 1)
    kind = lane // CAP
    value = jnp.where(kind == 0, high_col, jnp.where(kind == 1, low_col, 1.0))
    keep = (lane % CAP == pos_col) & (kind < 3)
    emb[:, C:] = jnp.where(keep, value, 0.0).astype(bf16)
    tile = tile_row.astype(i32)
    lat, lon = tile // N_LON, tile % N_LON
    chip = lat // 2 * N_LON + lon
    route[...] = jnp.concatenate(
        [chip * SLOT + pos_row, lat % 2, chip, jnp.zeros((5, OBS), i32)], axis=0
    )


def slot_keys(route, mine, core):
    return jnp.where(route[1:2, :] == mine, route[0:1, :] + CAP * core, -1)


class Round:
    def __init__(self, first, count, owner):
        self.first, self.count, self.owner = first, count, owner
        self.half = count * 16


EARLY = Round(0, 36, 0)
LATE = Round(1152, 17, 36)
PARTS = 1152 + 544

SIB_EMB, SIB_ROUTE, MARK, DATA, BACK, SIB_PART = range(6)
ROUND_SEMS = ((6, 7, 8, 9), (10, 11, 12, 13))
SEMS = 14


def block(ref, chip, size=SLOT):
    return ref.at[pl.ds(pl.multiple_of(chip * size, size), size)]


def edge_columns(ext, cols):
    for side, (at, row) in enumerate(((0, 0), (CLON - 16, 15))):
        for i in range(CLAT):
            cols[side, i : i + 1, :] = ext[1 + i, at : at + 16, :].astype(f32)[row : row + 1]


def side_columns(to_cols, to_diag, west, east):
    for side, (into, above, below) in enumerate(((west, 0, 2), (east, 1, 3))):
        into[0:1, :] = to_diag[above].astype(f32)[CLAT - 1 : CLAT]
        into[1 : CLAT + 1, :] = to_cols[side].astype(f32)
        into[CLAT + 1 : CLAT + 2, :] = to_diag[below].astype(f32)[0:1]


def side_sums(west, east, weight, sides):
    for side, ref in ((0, west), (1, east)):
        b = 2 * side
        total = (
            weight(b) * ref[0:CLAT, :]
            + weight(3 + b) * ref[1 : CLAT + 1, :]
            + weight(6 + b) * ref[2 : CLAT + 2, :]
        )
        for i in range(CLAT):
            sides[side, i, 0:1, :] = total[i : i + 1, :]


def conv_part(rows, sides, i, lanes, weight):
    columns = [
        weight(b) * rows[0] + weight(3 + b) * rows[1] + weight(6 + b) * rows[2] for b in range(3)
    ]
    index = lax.broadcasted_iota(i32, (CLON, CHUNK), 0)
    left = jnp.where(index == 0, sides[0, i, 0:1, lanes], pltpu.roll(columns[0], 1, 0))
    right = jnp.where(
        index == CLON - 1, sides[1, i, 0:1, lanes], pltpu.roll(columns[2], CLON - 1, 0)
    )
    return columns[1] + left + right


def kernel(
    spec_in,
    rows,
    w_in_in,
    w_out_in,
    w_point_in,
    w_depth,
    cot_in,
    latent,
    result,
    spec_t,
    w_in,
    w_out,
    w_point,
    cot,
    preact,
    hidden,
    emb,
    emb_sib,
    route,
    route_sib,
    outgoing,
    arrived,
    marks,
    places,
    gm_ext,
    grid_ext,
    cols_f,
    cols,
    to_cols,
    to_diag,
    cols_x,
    to_cols_x,
    to_diag_x,
    west,
    east,
    sides,
    g_grid,
    g_arrived,
    returned,
    part,
    part_sib,
    g_emb,
    mixed,
    parts,
    swap_out,
    swap_in,
    chip_sum,
    gather,
    owned,
    load_sem,
    local_sem,
    send_sem,
    recv_sem,
    halo_send,
    halo_recv,
):
    place = Place()
    core, me = place.core, place.chip
    loads = [
        pltpu.make_async_copy(src, dst, load_sem.at[i])
        for i, (src, dst) in enumerate(
            (
                (spec_in, spec_t),
                (w_in_in, w_in),
                (w_out_in, w_out),
                (w_point_in, w_point),
                (cot_in, cot),
            )
        )
    ]
    for copy in loads:
        copy.start()
    barrier, count = greet(place, True)

    def cross(src, dst, index, device):
        return remote(src, dst, send_sem.at[index], recv_sem.at[index], device)

    halo_g = Halo(place, gm_ext, cols, to_cols, to_diag, halo_send.at[0], halo_recv.at[0])
    halo_x = Halo(place, grid_ext, cols_x, to_cols_x, to_diag_x, halo_send.at[1], halo_recv.at[1])
    halo_g.clear_outside()
    halo_x.clear_outside()
    for copy in loads[:3]:
        copy.wait()
    vector_encode(spec_t, rows, w_in, w_out, preact, hidden, emb, route)
    for copy in loads[3:]:
        copy.wait()

    def mix_back(i, carry):
        rows4 = cot[pl.ds(pl.multiple_of(i * 512, 512), 512), :]
        gm = dot(rows4, w_point[...], ((1,), (1,))).astype(bf16)
        gm_ext[pl.ds(1 + 4 * i, 4)] = gm.reshape(4, CLON, C)
        return carry

    lax.fori_loop(0, CLAT // 4, mix_back, 0)
    edge_columns(gm_ext, cols_f.at[pl.ds(0, 2)])
    cols[...] = cols_f[0:2].astype(bf16)
    pl.semaphore_wait(barrier, count)

    swaps = [
        cross(emb, emb_sib, SIB_EMB, place.sibling),
        cross(route, route_sib, SIB_ROUTE, place.sibling),
    ]
    for copy in swaps:
        copy.start()
    halo_g.start()

    def spread(key, values, more):
        def one(i, carry):
            at = pl.multiple_of(i * PART, PART)
            index = lax.broadcasted_iota(i32, (PART, OBS), 0) + at
            pick = (index == key).astype(f32).astype(bf16)
            new = dot(pick, values[:, :C], ((1,), (0,)))
            if more:
                new = new + outgoing[pl.ds(at, PART), :].astype(f32)
            outgoing[pl.ds(at, PART), :] = new.astype(bf16)
            return carry

        lax.fori_loop(0, SLOTS // PART, one, 0)

    chips = lax.broadcasted_iota(i32, (CHIPS, OBS), 0)

    def marked(info, values):
        wanted = (info[2:3, :] == chips) & (info[1:2, :] == core)
        return dot(wanted.astype(f32).astype(bf16), values[:, C:], ((1,), (0,)))

    spread(slot_keys(route[...], core, core), emb, False)
    own = marked(route, emb)
    for copy in swaps:
        copy.wait()
    other = marked(route_sib, emb_sib)
    marks[:, 0, :] = jnp.where(core == 0, own, other)
    marks[:, 1, :] = jnp.where(core == 0, other, own)
    spread(slot_keys(route_sib[...], core, 1 - core), emb_sib, True)
    keep = [
        pltpu.make_async_copy(marks.at[me], places.at[me], local_sem.at[0]),
        pltpu.make_async_copy(block(outgoing, me), block(arrived, me), local_sem.at[1]),
    ]
    for copy in keep:
        copy.start()

    def send_marks(step, carry):
        chip, device = place.peer(step)
        cross(marks.at[chip], places.at[me], MARK, device).start()
        return carry

    lax.fori_loop(1, CHIPS, send_marks, 0)

    def send_data(step, carry):
        chip, device = place.peer(step)
        cross(block(outgoing, chip), block(arrived, me), DATA, device).start()
        return carry

    lax.fori_loop(1, CHIPS, send_data, 0)
    some = pl.ds(0, (CHIPS - 1) * SLOT)
    few = pl.ds(0, CHIPS - 1)

    halo_g.wait()
    side_columns(to_cols, to_diag, west, east)
    side_sums(west, east, lambda k: w_depth[8 - k : 9 - k, :], sides)

    def conv_back(i, carry):
        for chunk in range(C // CHUNK):
            lanes = slice(chunk * CHUNK, (chunk + 1) * CHUNK)
            three = [gm_ext[i + a, :, lanes].astype(f32) for a in range(3)]
            acc = conv_part(three, sides, i, lanes, lambda k: w_depth[8 - k : 9 - k, lanes])
            at = pl.ds(pl.multiple_of(i * CLON, CLON), CLON)
            g_grid[at, lanes] = (cot[at, lanes].astype(f32) + acc).astype(bf16)
        return carry

    lax.fori_loop(0, CLAT, conv_back, 0)

    for copy in keep:
        copy.wait()
    all_marks = cross(marks.at[few], places.at[few], MARK, place.sibling)
    all_marks.wait_recv()
    tables = [places[:, k, :].astype(bf16) for k in range(2)]
    down = lax.broadcasted_iota(i32, (SLOTS, CHIPS), 0)
    expand = (down // SLOT == lax.broadcasted_iota(i32, (SLOTS, CHIPS), 1)).astype(f32).astype(bf16)
    slot = lax.broadcasted_iota(i32, (SLOTS, META), 0)
    lane = lax.broadcasted_iota(i32, (SLOTS, META), 1)
    wide = [dot(expand, table, ((1,), (0,))) for table in tables]
    mine = jnp.where((slot // CAP) % 2 == 0, wide[0], wide[1])
    factor = jnp.where(lane < CAP, 16.0, 1.0)
    place_col = (
        jnp.sum(jnp.where(lane % CAP == slot % CAP, mine * factor, 0.0), axis=1, keepdims=True) - 1.0
    ).astype(i32)
    across = lax.broadcasted_iota(i32, (CHIPS, SLOTS), 1)
    expand_t = (across // SLOT == lax.broadcasted_iota(i32, (CHIPS, SLOTS), 0)).astype(f32).astype(bf16)
    slot_t = lax.broadcasted_iota(i32, (META, SLOTS), 1)
    lane_t = lax.broadcasted_iota(i32, (META, SLOTS), 0)
    wide_t = [dot(table, expand_t, ((0,), (0,))) for table in tables]
    mine_t = jnp.where((slot_t // CAP) % 2 == 0, wide_t[0], wide_t[1])
    factor_t = jnp.where(lane_t < CAP, 16.0, 1.0)
    place_row = (
        jnp.sum(jnp.where(lane_t % CAP == slot_t % CAP, mine_t * factor_t, 0.0), axis=0, keepdims=True)
        - 1.0
    ).astype(i32)
    cells = lax.broadcasted_iota(i32, (PART, CELLS), 1)
    for at in range(0, SLOTS, PART):
        pick = (place_col[at : at + PART] == cells).astype(f32).astype(bf16)
        g_arrived[at : at + PART, :] = dot(pick, g_grid[...], ((1,), (0,))).astype(bf16)
    keep_back = pltpu.make_async_copy(block(g_arrived, me), block(returned, me), local_sem.at[2])
    keep_back.start()

    def send_back(step, carry):
        chip, device = place.peer(step)
        cross(block(g_arrived, chip), block(returned, me), BACK, device).start()
        return carry

    lax.fori_loop(1, CHIPS, send_back, 0)

    all_data = cross(outgoing.at[some], arrived.at[some], DATA, place.sibling)
    all_data.wait_recv()

    def bin_rows(i, carry):
        index = lax.broadcasted_iota(i32, (PART, SLOTS), 0) + i * PART
        pick = (index == place_row).astype(f32).astype(bf16)
        cells_here = dot(pick, arrived[...], ((1,), (0,))).astype(bf16)
        grid_ext[pl.ds(1 + 2 * i, 2)] = cells_here.reshape(2, CLON, C)
        return carry

    lax.fori_loop(0, CELLS // PART, bin_rows, 0)
    edge_columns(grid_ext, cols_f.at[pl.ds(2, 2)])
    cols_x[...] = cols_f[2:4].astype(bf16)
    halo_x.start()
    halo_x.wait()
    side_columns(to_cols_x, to_diag_x, west, east)
    side_sums(west, east, lambda k: w_depth[k : k + 1, :], sides)
    depth = LATE.first + C
    for chunk in range(C // CHUNK):
        lanes = slice(chunk * CHUNK, (chunk + 1) * CHUNK)

        def conv_forward(i, sums, lanes=lanes):
            three = [grid_ext[i + a, :, lanes].astype(f32) for a in range(3)]
            acc = conv_part(three, sides, i, lanes, lambda k: w_depth[k : k + 1, lanes])
            at = pl.ds(pl.multiple_of(i * CLON, CLON), CLON)
            mixed[at, lanes] = acc.astype(bf16)
            middle = gm_ext[i + 1, :, lanes].astype(f32)
            index = lax.broadcasted_iota(i32, (CLON, CHUNK), 0)
            shifted = [
                jnp.where(index == CLON - 1, 0.0, pltpu.roll(middle, CLON - 1, 0)),
                middle,
                jnp.where(index == 0, 0.0, pltpu.roll(middle, 1, 0)),
            ]
            return tuple(
                sums[3 * a + b] + jnp.sum((shifted[b] * three[a]).reshape(16, 8, CHUNK), axis=0)
                for a in range(3)
                for b in range(3)
            )

        sums = lax.fori_loop(0, CLAT, conv_forward, tuple(jnp.zeros((8, CHUNK), f32) for _ in range(9)))
        for k, (a, b) in enumerate(offsets):
            total = jnp.sum(sums[k], axis=0, keepdims=True)
            if b:
                side = (west if b < 0 else east)[1 + a : 1 + a + CLAT, lanes]
                edge = cols_f[0 if b < 0 else 1, :, lanes].astype(bf16).astype(f32)
                total = total + jnp.sum(side * edge, axis=0, keepdims=True)
            parts[depth + k : depth + k + 1, lanes] = total
    parts[SPEC:ROWS_IN, :] = jnp.zeros((ROWS_IN - SPEC, C), f32)
    parts[ROWS_IN + C : LATE.first, :] = jnp.zeros((LATE.first - ROWS_IN - C, C), f32)
    parts[depth + 9 : PARTS, :] = jnp.zeros((PARTS - depth - 9, C), f32)

    keep_back.wait()
    all_back = cross(g_arrived.at[some], returned.at[some], BACK, place.sibling)
    all_back.wait_recv()

    def gathered(key):
        total = jnp.zeros((OBS, C), f32)
        for at in range(0, SLOTS, PART):
            index = lax.broadcasted_iota(i32, (PART, OBS), 0) + at
            pick = (index == key).astype(f32).astype(bf16)
            total = total + dot(pick, returned[at : at + PART, :], ((0,), (0,)))
        return total

    part[...] = gathered(slot_keys(route_sib[...], core, 1 - core)).astype(bf16)
    swap = cross(part, part_sib, SIB_PART, place.sibling)
    swap.start()
    own = gathered(slot_keys(route[...], core, core))
    parts[LATE.first : LATE.first + C, :] = dot(mixed[...], cot[...], ((0,), (0,)))
    swap.wait()
    g_emb[...] = (own + part_sib[...].astype(f32)).astype(bf16)
    parts[ROWS_IN : ROWS_IN + C, :] = dot(hidden[...], g_emb[...], ((0,), (0,)))
    g_hidden = dot(g_emb[...], w_out[...], ((1,), (1,)))
    pre = preact[...]
    sig = 1.0 / (1.0 + jnp.exp(-pre))
    g_pre = (g_hidden * sig * (1.0 + pre * (1.0 - sig))).astype(bf16)
    parts[0:SPEC, :] = dot(spec_t[...], g_pre, ((1,), (0,)))

    base = {EARLY: 0, LATE: EARLY.half}
    sems = {EARLY: ROUND_SEMS[0], LATE: ROUND_SEMS[1]}

    def half_of(r, which):
        return pl.ds(pl.multiple_of(r.first + which * r.half, 16), r.half)

    def local_half(r):
        return pl.ds(base[r], r.half)

    def swap_halves(r):
        swap_out[local_half(r), :] = parts[half_of(r, 1 - core), :].astype(bf16)
        copy = cross(swap_out.at[local_half(r)], swap_in.at[local_half(r)], sems[r][0], place.sibling)
        copy.start()
        return copy

    def owns(r, chip):
        return (chip >= r.owner) & (chip < r.owner + r.count)

    def send_blocks(r):
        rows_here = local_half(r)
        chip_sum[rows_here, :] = (
            parts[half_of(r, core), :] + swap_in[rows_here, :].astype(f32)
        ).astype(bf16)

        def own_block(chip):
            return chip_sum.at[pl.ds(pl.multiple_of(base[r] + (chip - r.owner) * 16, 16), 16)]

        def send(step, carry):
            chip, device = place.peer(step)

            @pl.when(owns(r, chip))
            def _():
                cross(own_block(chip), gather.at[me], sems[r][1], device).start()

            return carry

        lax.fori_loop(1, CHIPS, send, 0)

        @pl.when(owns(r, me))
        def _():
            pltpu.make_async_copy(own_block(me), gather.at[me], local_sem.at[3]).start()

    def share_sum(r):
        @pl.when(owns(r, me))
        def _():
            pltpu.make_async_copy(gather.at[me], gather.at[me], local_sem.at[3]).wait()
            cross(gather.at[few], gather.at[few], sems[r][1], place.sibling).wait_recv()
            owned[...] = jnp.sum(gather[...].astype(f32), axis=0).astype(bf16)
            here = pl.ds(
                pl.multiple_of(r.first + core * r.half + (me - r.owner) * 16, 16), 16
            )
            pltpu.make_async_copy(owned, result.at[here], local_sem.at[4]).start()

            def share(step, carry):
                _, device = place.peer(step)
                cross(owned, result.at[here], sems[r][2], device).start()
                return carry

            lax.fori_loop(1, CHIPS, share, 0)

    def collect(r):
        def waits(blocks):
            rows_here = pl.ds(0, blocks * 16)
            cross(chip_sum.at[rows_here], chip_sum.at[rows_here], sems[r][2], place.sibling).wait_recv()
            cross(chip_sum.at[rows_here], chip_sum.at[rows_here], sems[r][1], place.sibling).wait_send()

        @pl.when(owns(r, me))
        def _():
            pltpu.make_async_copy(owned, owned, local_sem.at[4]).wait()
            cross(gather.at[few], gather.at[few], sems[r][2], place.sibling).wait_send()
            waits(r.count - 1)

        @pl.when(jnp.logical_not(owns(r, me)))
        def _():
            waits(r.count)

        copy = cross(result.at[half_of(r, core)], result.at[half_of(r, core)], sems[r][3], place.sibling)
        copy.start()
        return copy

    early = swap_halves(EARLY)
    late = swap_halves(LATE)

    def point(i, carry):
        at = pl.ds(pl.multiple_of(i * 512, 512), 512)
        here = grid_ext[pl.ds(1 + 4 * i, 4)].astype(f32).reshape(512, C)
        latent[at, :] = (here + dot(mixed[at, :], w_point[...], ((1,), (0,)))).astype(bf16)
        return carry

    early.wait()
    send_blocks(EARLY)
    late.wait()
    send_blocks(LATE)
    lax.fori_loop(0, CLAT // 4, point, 0)
    share_sum(EARLY)
    share_sum(LATE)
    last = [collect(EARLY), collect(LATE)]
    for copy in (all_marks, all_data, all_back):
        copy.wait_send()
    for copy in last:
        copy.wait()


def run(spec_t, rows, w_in, w_out, w_point, w_depth, cot):
    dma = pltpu.SemaphoreType.DMA
    anywhere = pl.BlockSpec(memory_space=pl.ANY)
    field = VMEM((CLAT + 2, CLON, C), bf16)
    half = VMEM((EARLY.half + LATE.half, C), bf16)
    return pl.pallas_call(
        kernel,
        out_shape=[
            jax.ShapeDtypeStruct((CELLS, C), bf16),
            jax.ShapeDtypeStruct((PARTS, C), bf16),
        ],
        in_specs=[anywhere, vmem(), anywhere, anywhere, anywhere, vmem(), anywhere],
        out_specs=[vmem()] * 2,
        scratch_shapes=[
            VMEM((SPEC, OBS), bf16),
            VMEM((SPEC, C), bf16),
            VMEM((C, C), bf16),
            VMEM((C, C), bf16),
            VMEM((CELLS, C), bf16),
            VMEM((OBS, C), f32),
            VMEM((OBS, C), bf16),
            VMEM((OBS, C + META), bf16),
            VMEM((OBS, C + META), bf16),
            VMEM((8, OBS), i32),
            VMEM((8, OBS), i32),
            VMEM((SLOTS, C), bf16),
            VMEM((SLOTS, C), bf16),
            VMEM((CHIPS, 2, META), f32),
            VMEM((CHIPS, 2, META), f32),
            field,
            field,
            VMEM((4, CLAT, C), f32),
            VMEM((2, CLAT, C), bf16),
            VMEM((2, CLAT, C), bf16),
            VMEM((4, CLAT, C), bf16),
            VMEM((2, CLAT, C), bf16),
            VMEM((2, CLAT, C), bf16),
            VMEM((4, CLAT, C), bf16),
            VMEM((24, C), f32),
            VMEM((24, C), f32),
            VMEM((2, CLAT, 8, C), f32),
            VMEM((CELLS, C), bf16),
            VMEM((SLOTS, C), bf16),
            VMEM((SLOTS, C), bf16),
            VMEM((OBS, C), bf16),
            VMEM((OBS, C), bf16),
            VMEM((OBS, C), bf16),
            VMEM((CELLS, C), bf16),
            VMEM((PARTS, C), f32),
            half,
            half,
            half,
            VMEM((CHIPS, 16, C), bf16),
            VMEM((16, C), bf16),
            dma((5,)),
            dma((5,)),
            dma((SEMS,)),
            dma((SEMS,)),
            dma((2, 8)),
            dma((2, 8)),
        ],
        compiler_params=pltpu.CompilerParams(
            collective_id=0, has_side_effects=True, vmem_limit_bytes=60 << 20
        ),
    )(spec_t, rows, w_in, w_out, w_point, w_depth, cot)


def on_device(spectra, owner, cell, w_in, w_out, w_point, w_depth, cotangent):
    zero = jnp.zeros((13, OBS), bf16)
    rows = jnp.concatenate(
        [jnp.stack([owner[:, 0], cell // 16, cell % 16]).astype(bf16), zero], axis=0
    )
    latent, total = run(
        spectra.T, rows, w_in, w_out, w_point, w_depth, cotangent.reshape(CELLS, C)
    )
    total = total.astype(f32)
    tiles = N_LAT * N_LON
    obs_scale = 1.0 / jnp.sqrt(f32(OBS * tiles))
    cell_scale = 1.0 / jnp.sqrt(f32(CELLS * tiles))
    at = ROWS_IN
    late = LATE.first
    return (
        latent.reshape(CLAT, CLON, C),
        total[:SPEC] * obs_scale,
        total[at : at + C] * obs_scale,
        total[late : late + C] * cell_scale,
        total[late + C : late + C + 9] * cell_scale,
    )


def solution(mesh):
    in_specs = (
        P(("lat", "lon"), None),
        P(("lat", "lon"), None),
        P(("lat", "lon")),
        P(),
        P(),
        P(),
        P(),
        P("lat", "lon", None),
    )
    out_specs = (P("lat", "lon", None), P(), P(), P(), P())
    return jax.shard_map(
        on_device, mesh=mesh, in_specs=in_specs, out_specs=out_specs, check_vma=False
    )
```

```python
import math

import jax
import jax.numpy as jnp
from jax import lax
from jax.experimental import pallas as pl
from jax.experimental.pallas import tpu as pltpu
from jax.sharding import PartitionSpec as P

offsets = [(a, b) for a in (-1, 0, 1) for b in (-1, 0, 1)]
f32, bf16, i32 = jnp.float32, jnp.bfloat16, jnp.int32

N_LAT, N_LON, SIDE = 8, 16, 4
CHIPS = N_LAT // 2 * N_LON
CAP = 8
SLOT = 2 * CAP
SLOTS = CHIPS * SLOT
OBS = 512
C = 512
CLAT, CLON = 16, 128
CELLS = CLAT * CLON
SPEC = 616
META = 128
ROWS_IN = 640
PART = 256
CHUNK = 128

VMEM = pltpu.VMEM


def vmem():
    return pl.BlockSpec(memory_space=pltpu.VMEM)


def dot(a, b, dims):
    return lax.dot_general(a, b, (dims, ((), ())), preferred_element_type=f32)


class Place:
    def __init__(self):
        self.lat = lax.axis_index("lat")
        self.lon = lax.axis_index("lon")
        self.core = self.lat % 2
        self.x = self.lat // 2
        self.chip = self.x * N_LON + self.lon
        self.sibling = (self.x * 2 + 1 - self.core, self.lon)

    def peer(self, step):
        step = (step * 37) % CHIPS
        x = (self.x + step // N_LON) % (N_LAT // 2)
        z = (self.lon // SIDE + step // SIDE) % SIDE
        y = (self.lon + step) % SIDE
        lon = z * SIDE + y
        return x * N_LON + lon, (x * 2 + self.core, lon)

    def of_chip(self, chip):
        return (chip // N_LON * 2 + self.core, chip % N_LON)


def remote(src, dst, send, recv, device):
    return pltpu.make_async_remote_copy(
        src_ref=src,
        dst_ref=dst,
        send_sem=send,
        recv_sem=recv,
        device_id=device,
        device_id_type=pl.DeviceIdType.MESH,
    )


def greet(place):
    barrier = pltpu.get_barrier_semaphore()

    def hello(device):
        pl.semaphore_signal(
            barrier, inc=1, device_id=device, device_id_type=pl.DeviceIdType.MESH
        )

    def one(step, carry):
        hello(place.peer(step)[1])
        return carry

    lax.fori_loop(1, CHIPS, one, 0)
    others = N_LAT // 2
    for x in range(others):
        hello((2 * x + 1 - place.core, place.lon))
    for side in (-1, 1):
        inside = (place.lat + side >= 0) & (place.lat + side < N_LAT)

        @pl.when(inside)
        def _(side=side):
            for turn in (-1, 1):
                hello((place.lat + side, (place.lon + turn + N_LON) % N_LON))

    edges = (place.lat > 0).astype(i32) + (place.lat < N_LAT - 1).astype(i32)
    return barrier, CHIPS - 1 + others + 2 * edges


class Halo:
    def __init__(self, place, ext, cols, to_cols, to_diag, send, recv):
        self.place = place
        self.ext, self.to_diag = ext, to_diag
        lat, lon = place.lat, place.lon
        east, west = (lon + 1) % N_LON, (lon + N_LON - 1) % N_LON
        has_north, has_south = lat > 0, lat < N_LAT - 1
        south, north = jnp.minimum(lat + 1, N_LAT - 1), jnp.maximum(lat - 1, 0)
        plan = [
            (ext.at[CLAT], ext.at[0], (south, lon), has_south, has_north),
            (ext.at[1], ext.at[CLAT + 1], (north, lon), has_north, has_south),
            (cols.at[1], to_cols.at[0], (lat, east), None, None),
            (cols.at[0], to_cols.at[1], (lat, west), None, None),
            (cols.at[1], to_diag.at[0], (south, east), has_south, has_north),
            (cols.at[0], to_diag.at[1], (south, west), has_south, has_north),
            (cols.at[1], to_diag.at[2], (north, east), has_north, has_south),
            (cols.at[0], to_diag.at[3], (north, west), has_north, has_south),
        ]
        self.plan = [
            (remote(src, dst, send.at[i], recv.at[i], device), sends, receives)
            for i, (src, dst, device, sends, receives) in enumerate(plan)
        ]

    def start(self):
        for copy, sends, _ in self.plan:
            if sends is None:
                copy.start()
            else:
                pl.when(sends)(copy.start)

    def wait(self):
        for copy, sends, receives in self.plan:
            if sends is None:
                copy.wait_send()
                copy.wait_recv()
            else:
                pl.when(sends)(copy.wait_send)
                pl.when(receives)(copy.wait_recv)

    def clear_outside(self):
        @pl.when(self.place.lat == 0)
        def _():
            self.ext[0] = jnp.zeros((CLON, C), bf16)
            self.to_diag[0] = jnp.zeros((CLAT, C), bf16)
            self.to_diag[1] = jnp.zeros((CLAT, C), bf16)

        @pl.when(self.place.lat == N_LAT - 1)
        def _():
            self.ext[CLAT + 1] = jnp.zeros((CLON, C), bf16)
            self.to_diag[2] = jnp.zeros((CLAT, C), bf16)
            self.to_diag[3] = jnp.zeros((CLAT, C), bf16)


def vector_encode(spec_t, owner, cell, w_in, w_out, preact, hidden, emb, route, table):
    pre = dot(spec_t[...], w_in[...], ((0,), (0,)))
    preact[...] = pre
    hid = (pre * (1.0 / (1.0 + jnp.exp(-pre)))).astype(bf16)
    hidden[...] = hid
    emb[:, :C] = dot(hid, w_out[...], ((1,), (0,))).astype(bf16)
    places = cell[...]
    values = jnp.concatenate(
        [owner[...], places // 16, places % 16, jnp.zeros((13, OBS), i32)], axis=0
    ).astype(f32).astype(bf16)
    down = lax.broadcasted_iota(i32, (OBS, OBS), 0)
    across = lax.broadcasted_iota(i32, (OBS, OBS), 1)
    eye = (down == across).astype(f32).astype(bf16)
    columns = dot(eye, values, ((1,), (1,)))
    tile_col, high_col, low_col = columns[:, 0:1], columns[:, 1:2], columns[:, 2:3]
    tile_row = values[0:1, :].astype(f32)
    tiles = N_LAT * N_LON
    hits = (tile_col == lax.broadcasted_iota(i32, (OBS, tiles), 1).astype(f32)).astype(f32)
    lower = (across <= down).astype(f32).astype(bf16)
    count = dot(lower, hits.astype(bf16), ((1,), (0,)))
    pos_col = (jnp.sum(count * hits, axis=1, keepdims=True) - 1.0).astype(i32)
    hits_t = (tile_row == lax.broadcasted_iota(i32, (tiles, OBS), 0).astype(f32)).astype(f32)
    upper = (down <= across).astype(f32).astype(bf16)
    count_t = dot(hits_t.astype(bf16), upper, ((1,), (0,)))
    pos_row = (jnp.sum(count_t * hits_t, axis=0, keepdims=True) - 1.0).astype(i32)
    lane = lax.broadcasted_iota(i32, (OBS, META), 1)
    kind = lane // CAP
    value = jnp.where(kind == 0, high_col, jnp.where(kind == 1, low_col, 1.0))
    keep = (lane % CAP == pos_col) & (kind < 3)
    emb[:, C:] = jnp.where(keep, value, 0.0).astype(bf16)
    table[...] = dot(hits_t.astype(bf16), emb[:, C:], ((1,), (0,))).reshape(N_LAT, N_LON, META)
    tile = tile_row.astype(i32)
    lat, lon = tile // N_LON, tile % N_LON
    chip = lat // 2 * N_LON + lon
    route[...] = jnp.concatenate(
        [chip * SLOT + pos_row, lat % 2, chip, jnp.zeros((5, OBS), i32)], axis=0
    )


def slot_keys(route, mine, core):
    return jnp.where(route[1:2, :] == mine, route[0:1, :] + CAP * core, -1)


class Round:
    def __init__(self, number, axis, first, quarter, width):
        self.axis, self.first, self.quarter, self.width = axis, first, quarter, width
        self.half = 4 * quarter
        self.base = first // 2
        self.across = C // width
        self.count = quarter // 16 * self.across
        self.sems = range(7 + 6 * number, 13 + 6 * number)

    def line(self, place):
        x, z, y, core = place.x, place.lon // SIDE, place.lon % SIDE, place.core
        if self.axis == "x":
            return x, lambda q: (2 * q + core, place.lon)
        if self.axis == "y":
            return y, lambda q: (place.lat, z * SIDE + q)
        return z, lambda q: (place.lat, q * SIDE + y)

    def plane(self, place):
        x, z, y, core = place.x, place.lon // SIDE, place.lon % SIDE, place.core
        if self.axis == "x":
            return place.lon, lambda m: (place.lat, m)
        if self.axis == "y":
            return x * SIDE + z, lambda m: (2 * (m // SIDE) + core, m % SIDE * SIDE + y)
        return x * SIDE + y, lambda m: (2 * (m // SIDE) + core, z * SIDE + m % SIDE)


IN = Round(0, "z", 0, 80, 256)
OUT = Round(1, "y", 640, 64, 128)
POINT = Round(2, "x", 1152, 64, 128)
PARTS = 1664
DEPTH = 624

SIB_EMB, SIB_ROUTE, MARK_LAT, MARK_LON, DATA, BACK, SIB_PART = range(7)
SEMS = 7 + 18


def block(ref, chip, size=SLOT):
    return ref.at[pl.ds(pl.multiple_of(chip * size, size), size)]


def edge_columns(ext, cols):
    for side, (at, row) in enumerate(((0, 0), (CLON - 16, 15))):
        for i in range(CLAT):
            cols[side, i : i + 1, :] = ext[1 + i, at : at + 16, :].astype(f32)[row : row + 1]


def side_columns(to_cols, to_diag, west, east):
    for side, (into, above, below) in enumerate(((west, 0, 2), (east, 1, 3))):
        into[0:1, :] = to_diag[above].astype(f32)[CLAT - 1 : CLAT]
        into[1 : CLAT + 1, :] = to_cols[side].astype(f32)
        into[CLAT + 1 : CLAT + 2, :] = to_diag[below].astype(f32)[0:1]


def side_sums(west, east, weight, sides):
    for side, ref in ((0, west), (1, east)):
        b = 2 * side
        total = (
            weight(b) * ref[0:CLAT, :]
            + weight(3 + b) * ref[1 : CLAT + 1, :]
            + weight(6 + b) * ref[2 : CLAT + 2, :]
        )
        for i in range(CLAT):
            sides[side, i, 0:1, :] = total[i : i + 1, :]


def conv_part(rows, sides, i, lanes, weight):
    columns = [
        weight(b) * rows[0] + weight(3 + b) * rows[1] + weight(6 + b) * rows[2] for b in range(3)
    ]
    index = lax.broadcasted_iota(i32, (CLON, CHUNK), 0)
    left = jnp.where(index == 0, sides[0, i, 0:1, lanes], pltpu.roll(columns[0], 1, 0))
    right = jnp.where(
        index == CLON - 1, sides[1, i, 0:1, lanes], pltpu.roll(columns[2], CLON - 1, 0)
    )
    return columns[1] + left + right


def kernel(
    spec_in,
    owner,
    cell,
    w_in_in,
    w_out_in,
    w_point_in,
    w_depth,
    cot_in,
    latent,
    result,
    spec_t,
    w_in,
    w_out,
    w_point,
    cot,
    preact,
    hidden,
    emb,
    emb_sib,
    route,
    route_sib,
    outgoing,
    arrived,
    table,
    table_lat,
    marks,
    places,
    gm_ext,
    grid_ext,
    cols_f,
    cols,
    to_cols,
    to_diag,
    cols_x,
    to_cols_x,
    to_diag_x,
    west,
    east,
    sides,
    g_grid,
    g_arrived,
    returned,
    part,
    part_sib,
    g_emb,
    mixed,
    parts,
    swap_out,
    swap_in,
    chip_sum,
    lines_in,
    lines_out,
    lines_point,
    quarter_in,
    quarter_out,
    quarter_point,
    gather_in,
    gather_out,
    gather_point,
    latent_here,
    load_sem,
    local_sem,
    send_sem,
    recv_sem,
    halo_send,
    halo_recv,
):
    place = Place()
    core, me = place.core, place.chip
    loads = [
        pltpu.make_async_copy(src, dst, load_sem.at[i])
        for i, (src, dst) in enumerate(
            (
                (spec_in, spec_t),
                (w_in_in, w_in),
                (w_out_in, w_out),
                (w_point_in, w_point),
                (cot_in, cot),
            )
        )
    ]
    for copy in loads:
        copy.start()
    barrier, count = greet(place)

    def cross(src, dst, index, device):
        return remote(src, dst, send_sem.at[index], recv_sem.at[index], device)

    halo_g = Halo(place, gm_ext, cols, to_cols, to_diag, halo_send.at[0], halo_recv.at[0])
    halo_x = Halo(place, grid_ext, cols_x, to_cols_x, to_diag_x, halo_send.at[1], halo_recv.at[1])
    halo_g.clear_outside()
    halo_x.clear_outside()
    for copy in loads[:3]:
        copy.wait()
    vector_encode(spec_t, owner, cell, w_in, w_out, preact, hidden, emb, route, table)
    for copy in loads[3:]:
        copy.wait()

    def mix_back(i, carry):
        rows4 = cot[pl.ds(pl.multiple_of(i * 512, 512), 512), :]
        gm = dot(rows4, w_point[...], ((1,), (1,))).astype(bf16)
        gm_ext[pl.ds(1 + 4 * i, 4)] = gm.reshape(4, CLON, C)
        return carry

    lax.fori_loop(0, CLAT // 4, mix_back, 0)
    edge_columns(gm_ext, cols_f.at[pl.ds(0, 2)])
    cols[...] = cols_f[0:2].astype(bf16)
    pl.semaphore_wait(barrier, count)

    swaps = [
        cross(emb, emb_sib, SIB_EMB, place.sibling),
        cross(route, route_sib, SIB_ROUTE, place.sibling),
    ]
    for copy in swaps:
        copy.start()
    keep_lat = pltpu.make_async_copy(
        table.at[place.lat], table_lat.at[place.lat], local_sem.at[5]
    )
    keep_lat.start()
    for step in range(1, N_LAT):
        lat = (place.lat + step) % N_LAT
        cross(table.at[lat], table_lat.at[place.lat], MARK_LAT, (lat, place.lon)).start()
    halo_g.start()

    def spread(key, values, more):
        def one(i, carry):
            at = pl.multiple_of(i * PART, PART)
            index = lax.broadcasted_iota(i32, (PART, OBS), 0) + at
            pick = (index == key).astype(f32).astype(bf16)
            new = dot(pick, values[:, :C], ((1,), (0,)))
            if more:
                new = new + outgoing[pl.ds(at, PART), :].astype(f32)
            outgoing[pl.ds(at, PART), :] = new.astype(bf16)
            return carry

        lax.fori_loop(0, SLOTS // PART, one, 0)

    spread(slot_keys(route[...], core, core), emb, False)
    keep_lat.wait()
    lat_row = pl.ds(0, N_LAT - 1)
    lat_marks = cross(table.at[lat_row], table_lat.at[lat_row], MARK_LAT, place.sibling)
    lat_marks.wait_recv()
    for lon in range(N_LON):
        marks[lon] = table_lat[:, lon, :]
    keep_lon = pltpu.make_async_copy(marks.at[place.lon], places.at[place.lon], local_sem.at[0])
    keep_lon.start()
    for step in range(1, N_LON):
        lon = (place.lon + step) % N_LON
        cross(marks.at[lon], places.at[place.lon], MARK_LON, (place.lat, lon)).start()
    for copy in swaps:
        copy.wait()
    spread(slot_keys(route_sib[...], core, 1 - core), emb_sib, True)
    keep = pltpu.make_async_copy(block(outgoing, me), block(arrived, me), local_sem.at[1])
    keep.start()

    def send_data(step, carry):
        chip, device = place.peer(step)
        cross(block(outgoing, chip), block(arrived, me), DATA, device).start()
        return carry

    lax.fori_loop(1, CHIPS, send_data, 0)
    some = pl.ds(0, (CHIPS - 1) * SLOT)
    few = pl.ds(0, CHIPS - 1)

    halo_g.wait()
    side_columns(to_cols, to_diag, west, east)
    side_sums(west, east, lambda k: w_depth[8 - k : 9 - k, :], sides)

    def conv_back(i, carry):
        for chunk in range(C // CHUNK):
            lanes = slice(chunk * CHUNK, (chunk + 1) * CHUNK)
            three = [gm_ext[i + a, :, lanes].astype(f32) for a in range(3)]
            acc = conv_part(three, sides, i, lanes, lambda k: w_depth[8 - k : 9 - k, lanes])
            at = pl.ds(pl.multiple_of(i * CLON, CLON), CLON)
            g_grid[at, lanes] = (cot[at, lanes].astype(f32) + acc).astype(bf16)
        return carry

    lax.fori_loop(0, CLAT, conv_back, 0)

    keep_lon.wait()
    lon_row = pl.ds(0, N_LON - 1)
    lon_marks = cross(marks.at[lon_row], places.at[lon_row], MARK_LON, place.sibling)
    lon_marks.wait_recv()
    tiles = N_LAT * N_LON
    known = places[...].reshape(tiles, META).astype(bf16)

    def sender(slot):
        chip = slot // SLOT
        return chip % N_LON * N_LAT + chip // N_LON * 2 + slot // CAP % 2

    def cells_of(axis):
        shape = (SLOTS, tiles) if axis == 0 else (tiles, SLOTS)
        slot = lax.broadcasted_iota(i32, shape, axis)
        other = lax.broadcasted_iota(i32, shape, 1 - axis)
        expand = (sender(slot) == other).astype(f32).astype(bf16)
        if axis == 0:
            wide = dot(expand, known, ((1,), (0,)))
        else:
            wide = dot(known, expand, ((0,), (0,)))
        value = jnp.where(other < CAP, 16.0, 1.0) * wide
        keep = jnp.where(other % CAP == slot % CAP, value, 0.0)
        return (jnp.sum(keep, axis=1 - axis, keepdims=True) - 1.0).astype(i32)

    place_col, place_row = cells_of(0), cells_of(1)
    cells = lax.broadcasted_iota(i32, (PART, CELLS), 1)
    for at in range(0, SLOTS, PART):
        pick = (place_col[at : at + PART] == cells).astype(f32).astype(bf16)
        g_arrived[at : at + PART, :] = dot(pick, g_grid[...], ((1,), (0,))).astype(bf16)
    keep_back = pltpu.make_async_copy(block(g_arrived, me), block(returned, me), local_sem.at[2])
    keep_back.start()

    def send_back(step, carry):
        chip, device = place.peer(step)
        cross(block(g_arrived, chip), block(returned, me), BACK, device).start()
        return carry

    lax.fori_loop(1, CHIPS, send_back, 0)

    all_data = cross(outgoing.at[some], arrived.at[some], DATA, place.sibling)
    all_data.wait_recv()
    keep.wait()

    def bin_rows(i, carry):
        index = lax.broadcasted_iota(i32, (PART, SLOTS), 0) + i * PART
        pick = (index == place_row).astype(f32).astype(bf16)
        cells_here = dot(pick, arrived[...], ((1,), (0,))).astype(bf16)
        grid_ext[pl.ds(1 + 2 * i, 2)] = cells_here.reshape(2, CLON, C)
        return carry

    lax.fori_loop(0, CELLS // PART, bin_rows, 0)
    edge_columns(grid_ext, cols_f.at[pl.ds(2, 2)])
    cols_x[...] = cols_f[2:4].astype(bf16)
    halo_x.start()
    halo_x.wait()
    side_columns(to_cols_x, to_diag_x, west, east)
    side_sums(west, east, lambda k: w_depth[k : k + 1, :], sides)
    for chunk in range(C // CHUNK):
        lanes = slice(chunk * CHUNK, (chunk + 1) * CHUNK)

        def conv_forward(i, sums, lanes=lanes):
            three = [grid_ext[i + a, :, lanes].astype(f32) for a in range(3)]
            acc = conv_part(three, sides, i, lanes, lambda k: w_depth[k : k + 1, lanes])
            at = pl.ds(pl.multiple_of(i * CLON, CLON), CLON)
            mixed[at, lanes] = acc.astype(bf16)
            middle = gm_ext[i + 1, :, lanes].astype(f32)
            index = lax.broadcasted_iota(i32, (CLON, CHUNK), 0)
            shifted = [
                jnp.where(index == CLON - 1, 0.0, pltpu.roll(middle, CLON - 1, 0)),
                middle,
                jnp.where(index == 0, 0.0, pltpu.roll(middle, 1, 0)),
            ]
            return tuple(
                sums[3 * a + b] + jnp.sum((shifted[b] * three[a]).reshape(16, 8, CHUNK), axis=0)
                for a in range(3)
                for b in range(3)
            )

        sums = lax.fori_loop(0, CLAT, conv_forward, tuple(jnp.zeros((8, CHUNK), f32) for _ in range(9)))
        for k, (a, b) in enumerate(offsets):
            total = jnp.sum(sums[k], axis=0, keepdims=True)
            if b:
                side = (west if b < 0 else east)[1 + a : 1 + a + CLAT, lanes]
                edge = cols_f[0 if b < 0 else 1, :, lanes].astype(bf16).astype(f32)
                total = total + jnp.sum(side * edge, axis=0, keepdims=True)
            parts[DEPTH + k : DEPTH + k + 1, lanes] = total
    parts[SPEC:DEPTH, :] = jnp.zeros((DEPTH - SPEC, C), f32)
    parts[DEPTH + 9 : ROWS_IN, :] = jnp.zeros((ROWS_IN - DEPTH - 9, C), f32)
    parts[POINT.first : PARTS, :] = dot(mixed[...], cot[...], ((0,), (0,)))

    lines = {IN: lines_in, OUT: lines_out, POINT: lines_point}
    quarter = {IN: quarter_in, OUT: quarter_out, POINT: quarter_point}
    gathers = {IN: gather_in, OUT: gather_out, POINT: gather_point}

    def half_of(r, which):
        return pl.ds(pl.multiple_of(r.first + which * r.half, 16), r.half)

    def local_half(r):
        return pl.ds(r.base, r.half)

    def swap_halves(r):
        swap_out[local_half(r), :] = parts[half_of(r, 1 - core), :].astype(bf16)
        copy = cross(swap_out.at[local_half(r)], swap_in.at[local_half(r)], r.sems[0], place.sibling)
        copy.start()
        return copy

    def rows_at(start, size):
        return pl.ds(pl.multiple_of(start, 16), size)

    def send_line(r):
        here = local_half(r)
        chip_sum[here, :] = (
            parts[half_of(r, core), :] + swap_in[here, :].astype(f32)
        ).astype(bf16)
        at, device = r.line(place)
        for step in range(1, 4):
            q = (at + step) % 4
            src = chip_sum.at[rows_at(r.base + q * r.quarter, r.quarter)]
            cross(src, lines[r].at[at], r.sems[1], device(q)).start()

    def piece(r, start, index):
        rows_here = rows_at(start + index // r.across * 16, 16)
        return rows_here, pl.ds(pl.multiple_of(index % r.across * r.width, 128), r.width)

    def waiting(r, size, sem):
        some = gathers[r].at[pl.ds(0, size)]
        return cross(some, some, r.sems[sem], place.sibling)

    def waiting_line(r, sem):
        some = lines[r].at[pl.ds(0, 3)]
        return cross(some, some, r.sems[sem], place.sibling)

    def send_plane(r):
        waiting_line(r, 1).wait_recv()
        at, _ = r.line(place)
        total = chip_sum[rows_at(r.base + at * r.quarter, r.quarter), :].astype(f32)
        for step in range(1, 4):
            total = total + lines[r][(at + step) % 4].astype(f32)
        quarter[r][...] = total.astype(bf16)
        me_here, device = r.plane(place)

        def send(step, carry):
            index = (me_here + step) % 16

            @pl.when(index < r.count)
            def _():
                where = piece(r, 0, index)
                cross(quarter[r].at[where], gathers[r].at[me_here], r.sems[2], device(index)).start()

            return carry

        lax.fori_loop(1, 16, send, 0)

    def result_rows(r):
        return r.first + core * r.half + r.line(place)[0] * r.quarter

    def share_plane(r):
        me_here, device = r.plane(place)

        @pl.when(me_here < r.count)
        def _():
            waiting(r, 15, 2).wait_recv()
            total = quarter[r][piece(r, 0, me_here)].astype(f32)
            for step in range(1, 16):
                total = total + gathers[r][(me_here + step) % 16].astype(f32)
            where = piece(r, result_rows(r), me_here)
            result[where] = total.astype(bf16)

            def share(step, carry):
                index = (me_here + step) % 16
                cross(result.at[where], result.at[where], r.sems[3], device(index)).start()
                return carry

            lax.fori_loop(1, 16, share, 0)

    def share_line(r):
        me_here, _ = r.plane(place)
        if r.count == 16:
            waiting(r, 15, 3).wait_recv()
        else:
            pl.when(me_here < r.count)(lambda: waiting(r, r.count - 1, 3).wait_recv())
            pl.when(me_here >= r.count)(lambda: waiting(r, r.count, 3).wait_recv())
        at, device = r.line(place)
        here = result.at[rows_at(result_rows(r), r.quarter)]
        for step in range(1, 4):
            cross(here, here, r.sems[4], device((at + step) % 4)).start()

    def last_swap(r):
        waiting_line(r, 4).wait_recv()
        half = result.at[half_of(r, core)]
        copy = cross(half, half, r.sems[5], place.sibling)
        copy.start()
        return copy

    def sent(r):
        waiting_line(r, 1).wait_send()
        waiting_line(r, 4).wait_send()
        me_here, _ = r.plane(place)

        def owner():
            waiting(r, r.count - 1, 2).wait_send()
            waiting(r, 15, 3).wait_send()

        if r.count == 16:
            owner()
        else:
            pl.when(me_here < r.count)(owner)
            pl.when(me_here >= r.count)(lambda: waiting(r, r.count, 2).wait_send())

    def point(i):
        at = slice(i * 512, (i + 1) * 512)
        here = grid_ext[1 + 4 * i : 5 + 4 * i].astype(f32).reshape(512, C)
        latent_here[at, :] = (here + dot(mixed[at, :], w_point[...], ((1,), (0,)))).astype(bf16)

    point_swap = swap_halves(POINT)

    keep_back.wait()
    all_back = cross(g_arrived.at[some], returned.at[some], BACK, place.sibling)
    all_back.wait_recv()

    def gathered(key):
        total = jnp.zeros((OBS, C), f32)
        for at in range(0, SLOTS, PART):
            index = lax.broadcasted_iota(i32, (PART, OBS), 0) + at
            pick = (index == key).astype(f32).astype(bf16)
            total = total + dot(pick, returned[at : at + PART, :], ((0,), (0,)))
        return total

    part[...] = gathered(slot_keys(route_sib[...], core, 1 - core)).astype(bf16)
    swap = cross(part, part_sib, SIB_PART, place.sibling)
    swap.start()
    own = gathered(slot_keys(route[...], core, core))
    swap.wait()
    g_emb[...] = (own + part_sib[...].astype(f32)).astype(bf16)
    parts[OUT.first : OUT.first + C, :] = dot(hidden[...], g_emb[...], ((0,), (0,)))
    out_swap = swap_halves(OUT)
    g_hidden = dot(g_emb[...], w_out[...], ((1,), (1,)))
    pre = preact[...]
    sig = 1.0 / (1.0 + jnp.exp(-pre))
    g_pre = (g_hidden * sig * (1.0 + pre * (1.0 - sig))).astype(bf16)
    parts[0:SPEC, :] = dot(spec_t[...], g_pre, ((1,), (0,)))
    in_swap = swap_halves(IN)
    point_swap.wait()
    send_line(POINT)
    out_swap.wait()
    send_line(OUT)
    in_swap.wait()
    send_line(IN)
    point(0)
    send_plane(POINT)
    send_plane(OUT)
    send_plane(IN)
    point(1)
    share_plane(POINT)
    share_plane(OUT)
    share_plane(IN)
    point(2)
    share_line(POINT)
    share_line(OUT)
    share_line(IN)
    point(3)
    store = pltpu.make_async_copy(latent_here, latent, local_sem.at[6])
    store.start()
    last = [last_swap(POINT), last_swap(OUT), last_swap(IN)]
    for r in (POINT, OUT, IN):
        sent(r)
    store.wait()
    for copy in (lat_marks, lon_marks, all_data, all_back):
        copy.wait_send()
    for copy in last:
        copy.wait()


def run(spec_t, owner, cell, w_in, w_out, w_point, w_depth, cot):
    dma = pltpu.SemaphoreType.DMA
    anywhere = pl.BlockSpec(memory_space=pl.ANY)
    field = VMEM((CLAT + 2, CLON, C), bf16)
    half = VMEM((PARTS // 2, C), bf16)
    return pl.pallas_call(
        kernel,
        out_shape=[
            jax.ShapeDtypeStruct((CELLS, C), bf16),
            jax.ShapeDtypeStruct((PARTS, C), bf16),
        ],
        in_specs=[anywhere, vmem(), vmem(), anywhere, anywhere, anywhere, vmem(), anywhere],
        out_specs=[anywhere, vmem()],
        scratch_shapes=[
            VMEM((SPEC, OBS), bf16),
            VMEM((SPEC, C), bf16),
            VMEM((C, C), bf16),
            VMEM((C, C), bf16),
            VMEM((CELLS, C), bf16),
            VMEM((OBS, C), f32),
            VMEM((OBS, C), bf16),
            VMEM((OBS, C + META), bf16),
            VMEM((OBS, C + META), bf16),
            VMEM((8, OBS), i32),
            VMEM((8, OBS), i32),
            VMEM((SLOTS, C), bf16),
            VMEM((SLOTS, C), bf16),
            VMEM((N_LAT, N_LON, META), f32),
            VMEM((N_LAT, N_LON, META), f32),
            VMEM((N_LON, N_LAT, META), f32),
            VMEM((N_LON, N_LAT, META), f32),
            field,
            field,
            VMEM((4, CLAT, C), f32),
            VMEM((2, CLAT, C), bf16),
            VMEM((2, CLAT, C), bf16),
            VMEM((4, CLAT, C), bf16),
            VMEM((2, CLAT, C), bf16),
            VMEM((2, CLAT, C), bf16),
            VMEM((4, CLAT, C), bf16),
            VMEM((24, C), f32),
            VMEM((24, C), f32),
            VMEM((2, CLAT, 8, C), f32),
            VMEM((CELLS, C), bf16),
            VMEM((SLOTS, C), bf16),
            VMEM((SLOTS, C), bf16),
            VMEM((OBS, C), bf16),
            VMEM((OBS, C), bf16),
            VMEM((OBS, C), bf16),
            VMEM((CELLS, C), bf16),
            VMEM((PARTS, C), f32),
            half,
            half,
            half,
        ]
        + [VMEM((4, r.quarter, C), bf16) for r in (IN, OUT, POINT)]
        + [VMEM((r.quarter, C), bf16) for r in (IN, OUT, POINT)]
        + [VMEM((16, 16, r.width), bf16) for r in (IN, OUT, POINT)]
        + [
            VMEM((CELLS, C), bf16),
            dma((5,)),
            dma((7,)),
            dma((SEMS,)),
            dma((SEMS,)),
            dma((2, 8)),
            dma((2, 8)),
        ],
        compiler_params=pltpu.CompilerParams(
            collective_id=0, has_side_effects=True, vmem_limit_bytes=60 << 20
        ),
    )(spec_t, owner, cell, w_in, w_out, w_point, w_depth, cot)


def finish_kernel(
    latent_in, total_in, latent, g_in, g_out, g_point, g_depth, total, in_f, out_f, point_f, latent_here, sem
):
    obs_scale = 1.0 / math.sqrt(OBS * N_LAT * N_LON)
    cell_scale = 1.0 / math.sqrt(CELLS * N_LAT * N_LON)
    plan = (
        (in_f, g_in, IN.first, 640, obs_scale),
        (out_f, g_out, OUT.first, C, obs_scale),
        (point_f, g_point, POINT.first, C, cell_scale),
    )
    loads = []
    for i, (_, _, first, size, _) in enumerate(plan):
        rows = pl.ds(first, size)
        loads.append(pltpu.make_async_copy(total_in.at[rows], total.at[rows], sem.at[i]))
    loads.append(pltpu.make_async_copy(latent_in, latent_here, sem.at[3]))
    for copy in loads:
        copy.start()
    copies = []
    for i, (values, target, first, _, scale) in enumerate(plan):
        loads[i].wait()
        values[...] = total[first : first + values.shape[0], :].astype(f32) * scale
        copies.append(pltpu.make_async_copy(values, target, sem.at[4 + i]))
        copies[-1].start()
        if i == 0:
            g_depth[...] = total[DEPTH : DEPTH + 16, :].astype(f32)[0:9] * cell_scale
    loads[3].wait()
    copies.append(pltpu.make_async_copy(latent_here, latent, sem.at[7]))
    copies[-1].start()
    for copy in copies:
        copy.wait()


def finish(latent, total):
    anywhere = pl.BlockSpec(memory_space=pl.ANY)
    shapes = [(SPEC, C), (C, C), (C, C), (9, C)]
    return pl.pallas_call(
        finish_kernel,
        out_shape=[jax.ShapeDtypeStruct((CELLS, C), bf16)]
        + [jax.ShapeDtypeStruct(shape, f32) for shape in shapes],
        in_specs=[anywhere, anywhere],
        out_specs=[anywhere] * 4 + [vmem()],
        scratch_shapes=[VMEM((PARTS, C), bf16)]
        + [VMEM(shape, f32) for shape in shapes[:3]]
        + [VMEM((CELLS, C), bf16), pltpu.SemaphoreType.DMA((8,))],
        compiler_params=pltpu.CompilerParams(vmem_limit_bytes=62 << 20),
    )(latent, total)


def on_device(spectra, owner, cell, w_in, w_out, w_point, w_depth, cotangent):
    latent, total = run(
        spectra.T,
        owner.reshape(1, OBS),
        cell.reshape(1, OBS),
        w_in,
        w_out,
        w_point,
        w_depth,
        cotangent.reshape(CELLS, C),
    )
    latent, *grads = finish(latent, total)
    return (latent.reshape(CLAT, CLON, C), *grads)


def solution(mesh):
    in_specs = (
        P(("lat", "lon"), None),
        P(("lat", "lon"), None),
        P(("lat", "lon")),
        P(),
        P(),
        P(),
        P(),
        P("lat", "lon", None),
    )
    out_specs = (P("lat", "lon", None), P(), P(), P(), P())
    return jax.shard_map(
        on_device, mesh=mesh, in_specs=in_specs, out_specs=out_specs, check_vma=False
    )
```

```python
import math

import jax
import jax.numpy as jnp
from jax import lax
from jax.experimental import pallas as pl
from jax.experimental.pallas import tpu as pltpu
from jax.sharding import PartitionSpec as P

offsets = [(a, b) for a in (-1, 0, 1) for b in (-1, 0, 1)]
f32, bf16, i32 = jnp.float32, jnp.bfloat16, jnp.int32

N_LAT, N_LON, SIDE = 8, 16, 4
CHIPS = N_LAT // 2 * N_LON
CAP = 8
SLOT = 2 * CAP
SLOTS = CHIPS * SLOT
OBS = 512
C = 512
CLAT, CLON = 16, 128
CELLS = CLAT * CLON
SPEC = 616
META = 128
ROWS_IN = 640
PART = 256
CHUNK = 128

VMEM = pltpu.VMEM


def vmem():
    return pl.BlockSpec(memory_space=pltpu.VMEM)


def dot(a, b, dims):
    return lax.dot_general(a, b, (dims, ((), ())), preferred_element_type=f32)


class Place:
    def __init__(self):
        self.lat = lax.axis_index("lat")
        self.lon = lax.axis_index("lon")
        self.core = self.lat % 2
        self.x = self.lat // 2
        self.chip = self.x * N_LON + self.lon
        self.sibling = (self.x * 2 + 1 - self.core, self.lon)

    def peer(self, step):
        step = (step * 37) % CHIPS
        x = (self.x + step // N_LON) % (N_LAT // 2)
        z = (self.lon // SIDE + step // SIDE) % SIDE
        y = (self.lon + step) % SIDE
        lon = z * SIDE + y
        return x * N_LON + lon, (x * 2 + self.core, lon)

    def of_chip(self, chip):
        return (chip // N_LON * 2 + self.core, chip % N_LON)


def remote(src, dst, send, recv, device):
    return pltpu.make_async_remote_copy(
        src_ref=src,
        dst_ref=dst,
        send_sem=send,
        recv_sem=recv,
        device_id=device,
        device_id_type=pl.DeviceIdType.MESH,
    )


def greet(place):
    barrier = pltpu.get_barrier_semaphore()

    def hello(device):
        pl.semaphore_signal(
            barrier, inc=1, device_id=device, device_id_type=pl.DeviceIdType.MESH
        )

    def one(step, carry):
        hello(place.peer(step)[1])
        return carry

    lax.fori_loop(1, CHIPS, one, 0)
    others = N_LAT // 2
    for x in range(others):
        hello((2 * x + 1 - place.core, place.lon))
    for side in (-1, 1):
        inside = (place.lat + side >= 0) & (place.lat + side < N_LAT)

        @pl.when(inside)
        def _(side=side):
            for turn in (-1, 1):
                hello((place.lat + side, (place.lon + turn + N_LON) % N_LON))

    edges = (place.lat > 0).astype(i32) + (place.lat < N_LAT - 1).astype(i32)
    return barrier, CHIPS - 1 + others + 2 * edges


class Halo:
    def __init__(self, place, ext, cols, to_cols, to_diag, send, recv):
        self.place = place
        self.ext, self.to_diag = ext, to_diag
        lat, lon = place.lat, place.lon
        east, west = (lon + 1) % N_LON, (lon + N_LON - 1) % N_LON
        has_north, has_south = lat > 0, lat < N_LAT - 1
        south, north = jnp.minimum(lat + 1, N_LAT - 1), jnp.maximum(lat - 1, 0)
        plan = [
            (ext.at[CLAT], ext.at[0], (south, lon), has_south, has_north),
            (ext.at[1], ext.at[CLAT + 1], (north, lon), has_north, has_south),
            (cols.at[1], to_cols.at[0], (lat, east), None, None),
            (cols.at[0], to_cols.at[1], (lat, west), None, None),
            (cols.at[1], to_diag.at[0], (south, east), has_south, has_north),
            (cols.at[0], to_diag.at[1], (south, west), has_south, has_north),
            (cols.at[1], to_diag.at[2], (north, east), has_north, has_south),
            (cols.at[0], to_diag.at[3], (north, west), has_north, has_south),
        ]
        self.plan = [
            (remote(src, dst, send.at[i], recv.at[i], device), sends, receives)
            for i, (src, dst, device, sends, receives) in enumerate(plan)
        ]

    def start(self):
        for copy, sends, _ in self.plan:
            if sends is None:
                copy.start()
            else:
                pl.when(sends)(copy.start)

    def wait(self):
        for copy, sends, receives in self.plan:
            if sends is None:
                copy.wait_send()
                copy.wait_recv()
            else:
                pl.when(sends)(copy.wait_send)
                pl.when(receives)(copy.wait_recv)

    def clear_outside(self):
        @pl.when(self.place.lat == 0)
        def _():
            self.ext[0] = jnp.zeros((CLON, C), bf16)
            self.to_diag[0] = jnp.zeros((CLAT, C), bf16)
            self.to_diag[1] = jnp.zeros((CLAT, C), bf16)

        @pl.when(self.place.lat == N_LAT - 1)
        def _():
            self.ext[CLAT + 1] = jnp.zeros((CLON, C), bf16)
            self.to_diag[2] = jnp.zeros((CLAT, C), bf16)
            self.to_diag[3] = jnp.zeros((CLAT, C), bf16)


def vector_encode(spec_t, owner, cell, w_in, w_out, preact, hidden, emb, route, table):
    pre = dot(spec_t[...], w_in[...], ((0,), (0,)))
    preact[...] = pre
    hid = (pre * (1.0 / (1.0 + jnp.exp(-pre)))).astype(bf16)
    hidden[...] = hid
    emb[:, :C] = dot(hid, w_out[...], ((1,), (0,))).astype(bf16)
    places = cell[...]
    values = jnp.concatenate(
        [owner[...], places // 16, places % 16, jnp.zeros((13, OBS), i32)], axis=0
    ).astype(f32).astype(bf16)
    down = lax.broadcasted_iota(i32, (OBS, OBS), 0)
    across = lax.broadcasted_iota(i32, (OBS, OBS), 1)
    eye = (down == across).astype(f32).astype(bf16)
    columns = dot(eye, values, ((1,), (1,)))
    tile_col, high_col, low_col = columns[:, 0:1], columns[:, 1:2], columns[:, 2:3]
    tile_row = values[0:1, :].astype(f32)
    tiles = N_LAT * N_LON
    hits = (tile_col == lax.broadcasted_iota(i32, (OBS, tiles), 1).astype(f32)).astype(f32)
    lower = (across <= down).astype(f32).astype(bf16)
    count = dot(lower, hits.astype(bf16), ((1,), (0,)))
    pos_col = (jnp.sum(count * hits, axis=1, keepdims=True) - 1.0).astype(i32)
    hits_t = (tile_row == lax.broadcasted_iota(i32, (tiles, OBS), 0).astype(f32)).astype(f32)
    upper = (down <= across).astype(f32).astype(bf16)
    count_t = dot(hits_t.astype(bf16), upper, ((1,), (0,)))
    pos_row = (jnp.sum(count_t * hits_t, axis=0, keepdims=True) - 1.0).astype(i32)
    lane = lax.broadcasted_iota(i32, (OBS, META), 1)
    kind = lane // CAP
    value = jnp.where(kind == 0, high_col, jnp.where(kind == 1, low_col, 1.0))
    keep = (lane % CAP == pos_col) & (kind < 3)
    emb[:, C:] = jnp.where(keep, value, 0.0).astype(bf16)
    table[...] = dot(hits_t.astype(bf16), emb[:, C:], ((1,), (0,))).reshape(N_LAT, N_LON, META)
    tile = tile_row.astype(i32)
    lat, lon = tile // N_LON, tile % N_LON
    chip = lat // 2 * N_LON + lon
    route[...] = jnp.concatenate(
        [chip * SLOT + pos_row, lat % 2, chip, jnp.zeros((5, OBS), i32)], axis=0
    )


def slot_keys(route, mine, core):
    return jnp.where(route[1:2, :] == mine, route[0:1, :] + CAP * core, -1)


class Round:
    def __init__(self, number, axis, first, quarter, width):
        self.axis, self.first, self.quarter, self.width = axis, first, quarter, width
        self.half = 4 * quarter
        self.base = first // 2
        self.across = C // width
        self.count = quarter // 16 * self.across
        self.sems = range(7 + 6 * number, 13 + 6 * number)

    def line(self, place):
        x, z, y, core = place.x, place.lon // SIDE, place.lon % SIDE, place.core
        if self.axis == "x":
            return x, lambda q: (2 * q + core, place.lon)
        if self.axis == "y":
            return y, lambda q: (place.lat, z * SIDE + q)
        return z, lambda q: (place.lat, q * SIDE + y)

    def plane(self, place):
        x, z, y, core = place.x, place.lon // SIDE, place.lon % SIDE, place.core
        if self.axis == "x":
            return place.lon, lambda m: (place.lat, m)
        if self.axis == "y":
            return x * SIDE + z, lambda m: (2 * (m // SIDE) + core, m % SIDE * SIDE + y)
        return x * SIDE + y, lambda m: (2 * (m // SIDE) + core, z * SIDE + m % SIDE)


IN = Round(0, "z", 0, 80, 256)
OUT = Round(1, "y", 640, 64, 128)
POINT = Round(2, "x", 1152, 64, 128)
PARTS = 1664
DEPTH = 624

SIB_EMB, SIB_ROUTE, MARK_LAT, MARK_LON, DATA, BACK, SIB_PART = range(7)
SEMS = 7 + 18


def block(ref, chip, size=SLOT):
    return ref.at[pl.ds(pl.multiple_of(chip * size, size), size)]


def edge_columns(ext, cols):
    for side, (at, row) in enumerate(((0, 0), (CLON - 16, 15))):
        for i in range(CLAT):
            cols[side, i : i + 1, :] = ext[1 + i, at : at + 16, :].astype(f32)[row : row + 1]


def side_columns(to_cols, to_diag, west, east):
    for side, (into, above, below) in enumerate(((west, 0, 2), (east, 1, 3))):
        into[0:1, :] = to_diag[above].astype(f32)[CLAT - 1 : CLAT]
        into[1 : CLAT + 1, :] = to_cols[side].astype(f32)
        into[CLAT + 1 : CLAT + 2, :] = to_diag[below].astype(f32)[0:1]


def side_sums(west, east, weight, sides):
    for side, ref in ((0, west), (1, east)):
        b = 2 * side
        total = (
            weight(b) * ref[0:CLAT, :]
            + weight(3 + b) * ref[1 : CLAT + 1, :]
            + weight(6 + b) * ref[2 : CLAT + 2, :]
        )
        for i in range(CLAT):
            sides[side, i, 0:1, :] = total[i : i + 1, :]


def conv_part(rows, first, last, weight):
    columns = [
        weight(b) * rows[0] + weight(3 + b) * rows[1] + weight(6 + b) * rows[2] for b in range(3)
    ]
    index = lax.broadcasted_iota(i32, (CLON, CHUNK), 0)
    left = jnp.where(index == 0, first, pltpu.roll(columns[0], 1, 0))
    right = jnp.where(index == CLON - 1, last, pltpu.roll(columns[2], CLON - 1, 0))
    return columns[1] + left + right


def kernel(
    spec_in,
    owner,
    cell,
    w_in_in,
    w_out_in,
    w_point_in,
    w_depth,
    cot_in,
    latent,
    sums_out,
    spec_t,
    w_in,
    w_out,
    w_point,
    cot,
    preact,
    hidden,
    emb,
    emb_sib,
    route,
    route_sib,
    outgoing,
    arrived,
    table,
    table_lat,
    marks,
    places,
    gm_ext,
    grid_ext,
    cols_f,
    cols,
    to_cols,
    to_diag,
    cols_x,
    to_cols_x,
    to_diag_x,
    west,
    east,
    sides,
    ends,
    depth_sums,
    g_grid,
    g_arrived,
    returned,
    part,
    part_sib,
    g_emb,
    mixed,
    parts,
    swap_out,
    swap_in,
    chip_sum,
    lines_in,
    lines_out,
    lines_point,
    quarter_in,
    quarter_out,
    quarter_point,
    gather_in,
    gather_out,
    gather_point,
    latent_here,
    result,
    out_sem,
    load_sem,
    local_sem,
    send_sem,
    recv_sem,
    halo_send,
    halo_recv,
):
    place = Place()
    core, me = place.core, place.chip
    loads = [
        pltpu.make_async_copy(src, dst, load_sem.at[i])
        for i, (src, dst) in enumerate(
            (
                (spec_in, spec_t),
                (w_in_in, w_in),
                (w_out_in, w_out),
                (w_point_in, w_point),
                (cot_in, cot),
            )
        )
    ]
    for copy in loads:
        copy.start()
    barrier, count = greet(place)

    def cross(src, dst, index, device):
        return remote(src, dst, send_sem.at[index], recv_sem.at[index], device)

    halo_g = Halo(place, gm_ext, cols, to_cols, to_diag, halo_send.at[0], halo_recv.at[0])
    halo_x = Halo(place, grid_ext, cols_x, to_cols_x, to_diag_x, halo_send.at[1], halo_recv.at[1])
    halo_g.clear_outside()
    halo_x.clear_outside()
    for copy in loads[:3]:
        copy.wait()
    vector_encode(spec_t, owner, cell, w_in, w_out, preact, hidden, emb, route, table)
    for copy in loads[3:]:
        copy.wait()

    def mix_back(i, carry):
        rows4 = cot[pl.ds(pl.multiple_of(i * 512, 512), 512), :]
        gm = dot(rows4, w_point[...], ((1,), (1,))).astype(bf16)
        gm_ext[pl.ds(1 + 4 * i, 4)] = gm.reshape(4, CLON, C)
        return carry

    lax.fori_loop(0, CLAT // 4, mix_back, 0)
    edge_columns(gm_ext, cols_f.at[pl.ds(0, 2)])
    cols[...] = cols_f[0:2].astype(bf16)
    pl.semaphore_wait(barrier, count)

    swaps = [
        cross(emb, emb_sib, SIB_EMB, place.sibling),
        cross(route, route_sib, SIB_ROUTE, place.sibling),
    ]
    for copy in swaps:
        copy.start()
    keep_lat = pltpu.make_async_copy(
        table.at[place.lat], table_lat.at[place.lat], local_sem.at[5]
    )
    keep_lat.start()
    for step in range(1, N_LAT):
        lat = (place.lat + step) % N_LAT
        cross(table.at[lat], table_lat.at[place.lat], MARK_LAT, (lat, place.lon)).start()
    halo_g.start()

    def spread(key, values, more):
        def one(i, carry):
            at = pl.multiple_of(i * PART, PART)
            index = lax.broadcasted_iota(i32, (PART, OBS), 0) + at
            pick = (index == key).astype(f32).astype(bf16)
            new = dot(pick, values[:, :C], ((1,), (0,)))
            if more:
                new = new + outgoing[pl.ds(at, PART), :].astype(f32)
            outgoing[pl.ds(at, PART), :] = new.astype(bf16)
            return carry

        lax.fori_loop(0, SLOTS // PART, one, 0)

    spread(slot_keys(route[...], core, core), emb, False)
    keep_lat.wait()
    lat_row = pl.ds(0, N_LAT - 1)
    lat_marks = cross(table.at[lat_row], table_lat.at[lat_row], MARK_LAT, place.sibling)
    lat_marks.wait_recv()
    for lon in range(N_LON):
        marks[lon] = table_lat[:, lon, :]
    keep_lon = pltpu.make_async_copy(marks.at[place.lon], places.at[place.lon], local_sem.at[0])
    keep_lon.start()
    for step in range(1, N_LON):
        lon = (place.lon + step) % N_LON
        cross(marks.at[lon], places.at[place.lon], MARK_LON, (place.lat, lon)).start()
    for copy in swaps:
        copy.wait()
    spread(slot_keys(route_sib[...], core, 1 - core), emb_sib, True)
    keep = pltpu.make_async_copy(block(outgoing, me), block(arrived, me), local_sem.at[1])
    keep.start()

    def send_data(step, carry):
        chip, device = place.peer(step)
        cross(block(outgoing, chip), block(arrived, me), DATA, device).start()
        return carry

    lax.fori_loop(1, CHIPS, send_data, 0)
    some = pl.ds(0, (CHIPS - 1) * SLOT)
    few = pl.ds(0, CHIPS - 1)

    halo_g.wait()
    side_columns(to_cols, to_diag, west, east)
    side_sums(west, east, lambda k: w_depth[8 - k : 9 - k, :], sides)

    def conv_back(i, carry):
        for chunk in range(C // CHUNK):
            lanes = slice(chunk * CHUNK, (chunk + 1) * CHUNK)
            three = [gm_ext[i + a, :, lanes].astype(f32) for a in range(3)]
            first, last = sides[0, i, 0:1, lanes], sides[1, i, 0:1, lanes]
            acc = conv_part(three, first, last, lambda k: w_depth[8 - k : 9 - k, lanes])
            at = pl.ds(pl.multiple_of(i * CLON, CLON), CLON)
            g_grid[at, lanes] = (cot[at, lanes].astype(f32) + acc).astype(bf16)
        return carry

    lax.fori_loop(0, CLAT, conv_back, 0)

    keep_lon.wait()
    lon_row = pl.ds(0, N_LON - 1)
    lon_marks = cross(marks.at[lon_row], places.at[lon_row], MARK_LON, place.sibling)
    lon_marks.wait_recv()
    tiles = N_LAT * N_LON
    known = places[...].reshape(tiles, META).astype(bf16)

    def sender(slot):
        chip = slot // SLOT
        return chip % N_LON * N_LAT + chip // N_LON * 2 + slot // CAP % 2

    def cells_of(axis):
        shape = (SLOTS, tiles) if axis == 0 else (tiles, SLOTS)
        slot = lax.broadcasted_iota(i32, shape, axis)
        other = lax.broadcasted_iota(i32, shape, 1 - axis)
        expand = (sender(slot) == other).astype(f32).astype(bf16)
        if axis == 0:
            wide = dot(expand, known, ((1,), (0,)))
        else:
            wide = dot(known, expand, ((0,), (0,)))
        value = jnp.where(other < CAP, 16.0, 1.0) * wide
        keep = jnp.where(other % CAP == slot % CAP, value, 0.0)
        return (jnp.sum(keep, axis=1 - axis, keepdims=True) - 1.0).astype(i32)

    place_col, place_row = cells_of(0), cells_of(1)
    cells = lax.broadcasted_iota(i32, (PART, CELLS), 1)
    for at in range(0, SLOTS, PART):
        pick = (place_col[at : at + PART] == cells).astype(f32).astype(bf16)
        g_arrived[at : at + PART, :] = dot(pick, g_grid[...], ((1,), (0,))).astype(bf16)
    keep_back = pltpu.make_async_copy(block(g_arrived, me), block(returned, me), local_sem.at[2])
    keep_back.start()

    def send_back(step, carry):
        chip, device = place.peer(step)
        cross(block(g_arrived, chip), block(returned, me), BACK, device).start()
        return carry

    lax.fori_loop(1, CHIPS, send_back, 0)

    all_data = cross(outgoing.at[some], arrived.at[some], DATA, place.sibling)
    all_data.wait_recv()
    keep.wait()

    def bin_rows(i, carry):
        index = lax.broadcasted_iota(i32, (PART, SLOTS), 0) + i * PART
        pick = (index == place_row).astype(f32).astype(bf16)
        cells_here = dot(pick, arrived[...], ((1,), (0,))).astype(bf16)
        grid_ext[pl.ds(1 + 2 * i, 2)] = cells_here.reshape(2, CLON, C)
        return carry

    lax.fori_loop(0, CELLS // PART, bin_rows, 0)
    edge_columns(grid_ext, cols_f.at[pl.ds(2, 2)])
    cols_x[...] = cols_f[2:4].astype(bf16)
    halo_x.start()

    def conv_rows(low, high, chunk, sums):
        lanes = slice(chunk * CHUNK, (chunk + 1) * CHUNK)

        def one(i, sums):
            three = [grid_ext[i + a, :, lanes].astype(f32) for a in range(3)]
            acc = conv_part(three, 0.0, 0.0, lambda k: w_depth[k : k + 1, lanes])
            at = pl.ds(pl.multiple_of(i * CLON, CLON), CLON)
            mixed[at, lanes] = acc.astype(bf16)
            ends[0, i, 0:1, lanes] = acc[0:1]
            ends[1, i, 0:1, lanes] = acc[CLON - 1 : CLON]
            middle = gm_ext[i + 1, :, lanes].astype(f32)
            index = lax.broadcasted_iota(i32, (CLON, CHUNK), 0)
            shifted = [
                jnp.where(index == CLON - 1, 0.0, pltpu.roll(middle, CLON - 1, 0)),
                middle,
                jnp.where(index == 0, 0.0, pltpu.roll(middle, 1, 0)),
            ]
            return tuple(
                sums[3 * a + b] + jnp.sum((shifted[b] * three[a]).reshape(16, 8, CHUNK), axis=0)
                for a in range(3)
                for b in range(3)
            )

        return lax.fori_loop(low, high, one, sums)

    for chunk in range(C // CHUNK):
        sums = conv_rows(1, CLAT - 1, chunk, tuple(jnp.zeros((8, CHUNK), f32) for _ in range(9)))
        for k in range(9):
            depth_sums[chunk, k] = sums[k]
    halo_x.wait()
    side_columns(to_cols_x, to_diag_x, west, east)
    side_sums(west, east, lambda k: w_depth[k : k + 1, :], sides)
    for chunk in range(C // CHUNK):
        lanes = slice(chunk * CHUNK, (chunk + 1) * CHUNK)
        sums = conv_rows(0, 1, chunk, tuple(depth_sums[chunk, k] for k in range(9)))
        sums = conv_rows(CLAT - 1, CLAT, chunk, sums)
        for k, (a, b) in enumerate(offsets):
            total = jnp.sum(sums[k], axis=0, keepdims=True)
            if b:
                side = (west if b < 0 else east)[1 + a : 1 + a + CLAT, lanes]
                edge = cols_f[0 if b < 0 else 1, :, lanes].astype(bf16).astype(f32)
                total = total + jnp.sum(side * edge, axis=0, keepdims=True)
            parts[DEPTH + k : DEPTH + k + 1, lanes] = total

    def side_rows(i, carry):
        index = lax.broadcasted_iota(i32, (16, C), 0)
        for side, row in ((0, 0), (1, CLON - 16)):
            at = pl.ds(pl.multiple_of(i * CLON + row, 16), 16)
            whole = (ends[side, i, 0:1, :] + sides[side, i, 0:1, :]).astype(bf16).astype(f32)
            old = mixed[at, :].astype(f32)
            mixed[at, :] = jnp.where(index == 15 * side, whole, old).astype(bf16)
        return carry

    lax.fori_loop(0, CLAT, side_rows, 0)
    parts[SPEC:DEPTH, :] = jnp.zeros((DEPTH - SPEC, C), f32)
    parts[DEPTH + 9 : ROWS_IN, :] = jnp.zeros((ROWS_IN - DEPTH - 9, C), f32)
    parts[POINT.first : PARTS, :] = dot(mixed[...], cot[...], ((0,), (0,)))

    lines = {IN: lines_in, OUT: lines_out, POINT: lines_point}
    quarter = {IN: quarter_in, OUT: quarter_out, POINT: quarter_point}
    gathers = {IN: gather_in, OUT: gather_out, POINT: gather_point}

    def half_of(r, which):
        return pl.ds(pl.multiple_of(r.first + which * r.half, 16), r.half)

    def local_half(r):
        return pl.ds(r.base, r.half)

    def swap_halves(r):
        swap_out[local_half(r), :] = parts[half_of(r, 1 - core), :].astype(bf16)
        copy = cross(swap_out.at[local_half(r)], swap_in.at[local_half(r)], r.sems[0], place.sibling)
        copy.start()
        return copy

    def rows_at(start, size):
        return pl.ds(pl.multiple_of(start, 16), size)

    def send_line(r):
        here = local_half(r)
        chip_sum[here, :] = (
            parts[half_of(r, core), :] + swap_in[here, :].astype(f32)
        ).astype(bf16)
        at, device = r.line(place)
        for step in range(1, 4):
            q = (at + step) % 4
            src = chip_sum.at[rows_at(r.base + q * r.quarter, r.quarter)]
            cross(src, lines[r].at[at], r.sems[1], device(q)).start()

    def piece(r, start, index):
        rows_here = rows_at(start + index // r.across * 16, 16)
        return rows_here, pl.ds(pl.multiple_of(index % r.across * r.width, 128), r.width)

    def waiting(r, size, sem):
        some = gathers[r].at[pl.ds(0, size)]
        return cross(some, some, r.sems[sem], place.sibling)

    def waiting_line(r, sem):
        some = lines[r].at[pl.ds(0, 3)]
        return cross(some, some, r.sems[sem], place.sibling)

    def send_plane(r):
        waiting_line(r, 1).wait_recv()
        at, _ = r.line(place)
        total = chip_sum[rows_at(r.base + at * r.quarter, r.quarter), :].astype(f32)
        for step in range(1, 4):
            total = total + lines[r][(at + step) % 4].astype(f32)
        quarter[r][...] = total.astype(bf16)
        me_here, device = r.plane(place)

        def send(step, carry):
            index = (me_here + step) % 16

            @pl.when(index < r.count)
            def _():
                where = piece(r, 0, index)
                cross(quarter[r].at[where], gathers[r].at[me_here], r.sems[2], device(index)).start()

            return carry

        lax.fori_loop(1, 16, send, 0)

    def result_rows(r):
        return r.first + core * r.half + r.line(place)[0] * r.quarter

    def share_plane(r):
        me_here, device = r.plane(place)

        @pl.when(me_here < r.count)
        def _():
            waiting(r, 15, 2).wait_recv()
            total = quarter[r][piece(r, 0, me_here)].astype(f32)
            for step in range(1, 16):
                total = total + gathers[r][(me_here + step) % 16].astype(f32)
            where = piece(r, result_rows(r), me_here)
            result[where] = total.astype(bf16)

            def share(step, carry):
                index = (me_here + step) % 16
                cross(result.at[where], result.at[where], r.sems[3], device(index)).start()
                return carry

            lax.fori_loop(1, 16, share, 0)

    def share_line(r):
        me_here, _ = r.plane(place)
        if r.count == 16:
            waiting(r, 15, 3).wait_recv()
        else:
            pl.when(me_here < r.count)(lambda: waiting(r, r.count - 1, 3).wait_recv())
            pl.when(me_here >= r.count)(lambda: waiting(r, r.count, 3).wait_recv())
        at, device = r.line(place)
        here = result.at[rows_at(result_rows(r), r.quarter)]
        for step in range(1, 4):
            cross(here, here, r.sems[4], device((at + step) % 4)).start()

    def last_swap(r):
        waiting_line(r, 4).wait_recv()
        half = result.at[half_of(r, core)]
        copy = cross(half, half, r.sems[5], place.sibling)
        copy.start()
        return copy

    def sent(r):
        waiting_line(r, 1).wait_send()
        waiting_line(r, 4).wait_send()
        me_here, _ = r.plane(place)

        def owner():
            waiting(r, r.count - 1, 2).wait_send()
            waiting(r, 15, 3).wait_send()

        if r.count == 16:
            owner()
        else:
            pl.when(me_here < r.count)(owner)
            pl.when(me_here >= r.count)(lambda: waiting(r, r.count, 2).wait_send())

    def point(i):
        at = slice(i * 512, (i + 1) * 512)
        here = grid_ext[1 + 4 * i : 5 + 4 * i].astype(f32).reshape(512, C)
        latent_here[at, :] = (here + dot(mixed[at, :], w_point[...], ((1,), (0,)))).astype(bf16)

    point_swap = swap_halves(POINT)

    keep_back.wait()
    all_back = cross(g_arrived.at[some], returned.at[some], BACK, place.sibling)
    all_back.wait_recv()

    def gathered(key):
        total = jnp.zeros((OBS, C), f32)
        for at in range(0, SLOTS, PART):
            index = lax.broadcasted_iota(i32, (PART, OBS), 0) + at
            pick = (index == key).astype(f32).astype(bf16)
            total = total + dot(pick, returned[at : at + PART, :], ((0,), (0,)))
        return total

    part[...] = gathered(slot_keys(route_sib[...], core, 1 - core)).astype(bf16)
    swap = cross(part, part_sib, SIB_PART, place.sibling)
    swap.start()
    own = gathered(slot_keys(route[...], core, core))
    swap.wait()
    g_emb[...] = (own + part_sib[...].astype(f32)).astype(bf16)
    parts[OUT.first : OUT.first + C, :] = dot(hidden[...], g_emb[...], ((0,), (0,)))
    out_swap = swap_halves(OUT)
    g_hidden = dot(g_emb[...], w_out[...], ((1,), (1,)))
    pre = preact[...]
    sig = 1.0 / (1.0 + jnp.exp(-pre))
    g_pre = (g_hidden * sig * (1.0 + pre * (1.0 - sig))).astype(bf16)
    parts[0:SPEC, :] = dot(spec_t[...], g_pre, ((1,), (0,)))
    in_swap = swap_halves(IN)
    point_swap.wait()
    send_line(POINT)
    out_swap.wait()
    send_line(OUT)
    in_swap.wait()
    send_line(IN)
    point(0)
    send_plane(POINT)
    send_plane(OUT)
    send_plane(IN)
    point(1)
    share_plane(POINT)
    share_plane(OUT)
    share_plane(IN)
    point(2)
    share_line(POINT)
    share_line(OUT)
    share_line(IN)
    point(3)
    store = pltpu.make_async_copy(latent_here, latent, local_sem.at[6])
    store.start()
    rounds = (POINT, OUT, IN)

    def leave(r, which, index):
        half = half_of(r, which)
        return pltpu.make_async_copy(result.at[half], sums_out.at[half], out_sem.at[index])

    last, leaving = [], []
    for i, r in enumerate(rounds):
        last.append(last_swap(r))
        leaving.append(leave(r, core, i))
        leaving[-1].start()
    for r in rounds:
        sent(r)
    store.wait()
    for copy in (lat_marks, lon_marks, all_data, all_back):
        copy.wait_send()
    for i, r in enumerate(rounds):
        last[i].wait()
        leaving.append(leave(r, 1 - core, 3 + i))
        leaving[-1].start()
    for copy in leaving:
        copy.wait()


def run(spec_t, owner, cell, w_in, w_out, w_point, w_depth, cot):
    dma = pltpu.SemaphoreType.DMA
    anywhere = pl.BlockSpec(memory_space=pl.ANY)
    field = VMEM((CLAT + 2, CLON, C), bf16)
    half = VMEM((PARTS // 2, C), bf16)
    return pl.pallas_call(
        kernel,
        out_shape=[
            pltpu.VMEM((CELLS, C), bf16),
            pltpu.VMEM((PARTS, C), bf16),
        ],
        in_specs=[anywhere, vmem(), vmem(), anywhere, anywhere, anywhere, vmem(), anywhere],
        out_specs=[anywhere, anywhere],
        scratch_shapes=[
            VMEM((SPEC, OBS), bf16),
            VMEM((SPEC, C), bf16),
            VMEM((C, C), bf16),
            VMEM((C, C), bf16),
            VMEM((CELLS, C), bf16),
            VMEM((OBS, C), f32),
            VMEM((OBS, C), bf16),
            VMEM((OBS, C + META), bf16),
            VMEM((OBS, C + META), bf16),
            VMEM((8, OBS), i32),
            VMEM((8, OBS), i32),
            VMEM((SLOTS, C), bf16),
            VMEM((SLOTS, C), bf16),
            VMEM((N_LAT, N_LON, META), f32),
            VMEM((N_LAT, N_LON, META), f32),
            VMEM((N_LON, N_LAT, META), f32),
            VMEM((N_LON, N_LAT, META), f32),
            field,
            field,
            VMEM((4, CLAT, C), f32),
            VMEM((2, CLAT, C), bf16),
            VMEM((2, CLAT, C), bf16),
            VMEM((4, CLAT, C), bf16),
            VMEM((2, CLAT, C), bf16),
            VMEM((2, CLAT, C), bf16),
            VMEM((4, CLAT, C), bf16),
            VMEM((24, C), f32),
            VMEM((24, C), f32),
            VMEM((2, CLAT, 8, C), f32),
            VMEM((2, CLAT, 8, C), f32),
            VMEM((C // CHUNK, 9, 8, CHUNK), f32),
            VMEM((CELLS, C), bf16),
            VMEM((SLOTS, C), bf16),
            VMEM((SLOTS, C), bf16),
            VMEM((OBS, C), bf16),
            VMEM((OBS, C), bf16),
            VMEM((OBS, C), bf16),
            VMEM((CELLS, C), bf16),
            VMEM((PARTS, C), f32),
            half,
            half,
            half,
        ]
        + [VMEM((4, r.quarter, C), bf16) for r in (IN, OUT, POINT)]
        + [VMEM((r.quarter, C), bf16) for r in (IN, OUT, POINT)]
        + [VMEM((16, 16, r.width), bf16) for r in (IN, OUT, POINT)]
        + [
            VMEM((CELLS, C), bf16),
            VMEM((PARTS, C), bf16),
            dma((6,)),
            dma((5,)),
            dma((7,)),
            dma((SEMS,)),
            dma((SEMS,)),
            dma((2, 8)),
            dma((2, 8)),
        ],
        compiler_params=pltpu.CompilerParams(
            collective_id=0, has_side_effects=True, vmem_limit_bytes=51 << 20
        ),
    )(spec_t, owner, cell, w_in, w_out, w_point, w_depth, cot)


def finish_kernel(latent_in, total, latent, g_in, g_out, g_point, g_depth, in_f, out_f, point_f, sem):
    obs_scale = 1.0 / math.sqrt(OBS * N_LAT * N_LON)
    cell_scale = 1.0 / math.sqrt(CELLS * N_LAT * N_LON)
    copies = [pltpu.make_async_copy(latent_in, latent, sem.at[3])]
    copies[0].start()
    plan = (
        (in_f, g_in, IN.first, obs_scale),
        (out_f, g_out, OUT.first, obs_scale),
        (point_f, g_point, POINT.first, cell_scale),
    )
    for i, (values, target, first, scale) in enumerate(plan):
        values[...] = total[first : first + values.shape[0], :].astype(f32) * scale
        copies.append(pltpu.make_async_copy(values, target, sem.at[i]))
        copies[-1].start()
    g_depth[...] = total[DEPTH : DEPTH + 16, :].astype(f32)[0:9] * cell_scale
    for copy in copies:
        copy.wait()


def finish(latent, total):
    anywhere = pl.BlockSpec(memory_space=pl.ANY)
    shapes = [(SPEC, C), (C, C), (C, C), (9, C)]
    return pl.pallas_call(
        finish_kernel,
        out_shape=[jax.ShapeDtypeStruct((CELLS, C), bf16)]
        + [jax.ShapeDtypeStruct(shape, f32) for shape in shapes],
        in_specs=[vmem(), vmem()],
        out_specs=[anywhere] * 4 + [vmem()],
        scratch_shapes=[VMEM(shape, f32) for shape in shapes[:3]] + [pltpu.SemaphoreType.DMA((4,))],
        compiler_params=pltpu.CompilerParams(vmem_limit_bytes=12 << 20),
    )(latent, total)


def on_device(spectra, owner, cell, w_in, w_out, w_point, w_depth, cotangent):
    latent, total = run(
        spectra.T,
        owner.reshape(1, OBS),
        cell.reshape(1, OBS),
        w_in,
        w_out,
        w_point,
        w_depth,
        cotangent.reshape(CELLS, C),
    )
    latent, *grads = finish(latent, total)
    return (latent.reshape(CLAT, CLON, C), *grads)


def solution(mesh):
    in_specs = (
        P(("lat", "lon"), None),
        P(("lat", "lon"), None),
        P(("lat", "lon")),
        P(),
        P(),
        P(),
        P(),
        P("lat", "lon", None),
    )
    out_specs = (P("lat", "lon", None), P(), P(), P(), P())
    return jax.shard_map(
        on_device, mesh=mesh, in_specs=in_specs, out_specs=out_specs, check_vma=False
    )
```

```python
import math

import jax
import jax.numpy as jnp
from jax import lax
from jax.experimental import pallas as pl
from jax.experimental.pallas import tpu as pltpu
from jax.sharding import PartitionSpec as P

offsets = [(a, b) for a in (-1, 0, 1) for b in (-1, 0, 1)]
f32, bf16, i32 = jnp.float32, jnp.bfloat16, jnp.int32

N_LAT, N_LON, SIDE = 8, 16, 4
CHIPS = N_LAT // 2 * N_LON
CAP = 8
SLOT = 2 * CAP
SLOTS = CHIPS * SLOT
OBS = 512
C = 512
CLAT, CLON = 16, 128
CELLS = CLAT * CLON
SPEC = 616
META = 128
ROWS_IN = 640
PART = 256
CHUNK = 128

VMEM = pltpu.VMEM


def vmem():
    return pl.BlockSpec(memory_space=pltpu.VMEM)


def dot(a, b, dims):
    return lax.dot_general(a, b, (dims, ((), ())), preferred_element_type=f32)


class Place:
    def __init__(self):
        self.lat = lax.axis_index("lat")
        self.lon = lax.axis_index("lon")
        self.core = self.lat % 2
        self.x = self.lat // 2
        self.chip = self.x * N_LON + self.lon
        self.sibling = (self.x * 2 + 1 - self.core, self.lon)

    def peer(self, step):
        step = (step * 37) % CHIPS
        x = (self.x + step // N_LON) % (N_LAT // 2)
        z = (self.lon // SIDE + step // SIDE) % SIDE
        y = (self.lon + step) % SIDE
        lon = z * SIDE + y
        return x * N_LON + lon, (x * 2 + self.core, lon)

    def of_chip(self, chip):
        return (chip // N_LON * 2 + self.core, chip % N_LON)


def remote(src, dst, send, recv, device):
    return pltpu.make_async_remote_copy(
        src_ref=src,
        dst_ref=dst,
        send_sem=send,
        recv_sem=recv,
        device_id=device,
        device_id_type=pl.DeviceIdType.MESH,
    )


def greet(place):
    barrier = pltpu.get_barrier_semaphore()

    def hello(device):
        pl.semaphore_signal(
            barrier, inc=1, device_id=device, device_id_type=pl.DeviceIdType.MESH
        )

    def one(step, carry):
        hello(place.peer(step)[1])
        return carry

    lax.fori_loop(1, CHIPS, one, 0)
    others = N_LAT // 2
    for x in range(others):
        hello((2 * x + 1 - place.core, place.lon))
    for side in (-1, 1):
        inside = (place.lat + side >= 0) & (place.lat + side < N_LAT)

        @pl.when(inside)
        def _(side=side):
            for turn in (-1, 1):
                hello((place.lat + side, (place.lon + turn + N_LON) % N_LON))

    edges = (place.lat > 0).astype(i32) + (place.lat < N_LAT - 1).astype(i32)
    return barrier, CHIPS - 1 + others + 2 * edges


class Halo:
    def __init__(self, place, ext, cols, to_cols, to_diag, send, recv):
        self.place = place
        self.ext, self.to_diag = ext, to_diag
        lat, lon = place.lat, place.lon
        east, west = (lon + 1) % N_LON, (lon + N_LON - 1) % N_LON
        has_north, has_south = lat > 0, lat < N_LAT - 1
        south, north = jnp.minimum(lat + 1, N_LAT - 1), jnp.maximum(lat - 1, 0)
        plan = [
            (ext.at[CLAT], ext.at[0], (south, lon), has_south, has_north),
            (ext.at[1], ext.at[CLAT + 1], (north, lon), has_north, has_south),
            (cols.at[1], to_cols.at[0], (lat, east), None, None),
            (cols.at[0], to_cols.at[1], (lat, west), None, None),
            (cols.at[1], to_diag.at[0], (south, east), has_south, has_north),
            (cols.at[0], to_diag.at[1], (south, west), has_south, has_north),
            (cols.at[1], to_diag.at[2], (north, east), has_north, has_south),
            (cols.at[0], to_diag.at[3], (north, west), has_north, has_south),
        ]
        self.plan = [
            (remote(src, dst, send.at[i], recv.at[i], device), sends, receives)
            for i, (src, dst, device, sends, receives) in enumerate(plan)
        ]

    def start(self):
        for copy, sends, _ in self.plan:
            if sends is None:
                copy.start()
            else:
                pl.when(sends)(copy.start)

    def wait(self):
        for copy, sends, receives in self.plan:
            if sends is None:
                copy.wait_send()
                copy.wait_recv()
            else:
                pl.when(sends)(copy.wait_send)
                pl.when(receives)(copy.wait_recv)

    def clear_outside(self):
        @pl.when(self.place.lat == 0)
        def _():
            self.ext[0] = jnp.zeros((CLON, C), bf16)
            self.to_diag[0] = jnp.zeros((CLAT, C), bf16)
            self.to_diag[1] = jnp.zeros((CLAT, C), bf16)

        @pl.when(self.place.lat == N_LAT - 1)
        def _():
            self.ext[CLAT + 1] = jnp.zeros((CLON, C), bf16)
            self.to_diag[2] = jnp.zeros((CLAT, C), bf16)
            self.to_diag[3] = jnp.zeros((CLAT, C), bf16)


def vector_encode(spec_t, owner, cell, w_in, w_out, preact, hidden, emb, route, table):
    pre = dot(spec_t[...], w_in[...], ((0,), (0,)))
    preact[...] = pre
    hid = (pre * (1.0 / (1.0 + jnp.exp(-pre)))).astype(bf16)
    hidden[...] = hid
    emb[:, :C] = dot(hid, w_out[...], ((1,), (0,))).astype(bf16)
    places = cell[...]
    values = jnp.concatenate(
        [owner[...], places // 16, places % 16, jnp.zeros((13, OBS), i32)], axis=0
    ).astype(f32).astype(bf16)
    down = lax.broadcasted_iota(i32, (OBS, OBS), 0)
    across = lax.broadcasted_iota(i32, (OBS, OBS), 1)
    eye = (down == across).astype(f32).astype(bf16)
    columns = dot(eye, values, ((1,), (1,)))
    tile_col, high_col, low_col = columns[:, 0:1], columns[:, 1:2], columns[:, 2:3]
    tile_row = values[0:1, :].astype(f32)
    tiles = N_LAT * N_LON
    hits = (tile_col == lax.broadcasted_iota(i32, (OBS, tiles), 1).astype(f32)).astype(f32)
    lower = (across <= down).astype(f32).astype(bf16)
    count = dot(lower, hits.astype(bf16), ((1,), (0,)))
    pos_col = (jnp.sum(count * hits, axis=1, keepdims=True) - 1.0).astype(i32)
    hits_t = (tile_row == lax.broadcasted_iota(i32, (tiles, OBS), 0).astype(f32)).astype(f32)
    upper = (down <= across).astype(f32).astype(bf16)
    count_t = dot(hits_t.astype(bf16), upper, ((1,), (0,)))
    pos_row = (jnp.sum(count_t * hits_t, axis=0, keepdims=True) - 1.0).astype(i32)
    lane = lax.broadcasted_iota(i32, (OBS, META), 1)
    kind = lane // CAP
    value = jnp.where(kind == 0, high_col, jnp.where(kind == 1, low_col, 1.0))
    keep = (lane % CAP == pos_col) & (kind < 3)
    emb[:, C:] = jnp.where(keep, value, 0.0).astype(bf16)
    table[...] = dot(hits_t.astype(bf16), emb[:, C:], ((1,), (0,))).reshape(N_LAT, N_LON, META)
    tile = tile_row.astype(i32)
    lat, lon = tile // N_LON, tile % N_LON
    chip = lat // 2 * N_LON + lon
    route[...] = jnp.concatenate(
        [chip * SLOT + pos_row, lat % 2, chip, jnp.zeros((5, OBS), i32)], axis=0
    )


def slot_keys(route, mine, core):
    return jnp.where(route[1:2, :] == mine, route[0:1, :] + CAP * core, -1)


class Round:
    def __init__(self, number, axis, first, quarter, width):
        self.axis, self.first, self.quarter, self.width = axis, first, quarter, width
        self.half = 4 * quarter
        self.base = first // 2
        self.across = C // width
        self.count = quarter // 16 * self.across
        self.sems = range(7 + 6 * number, 13 + 6 * number)

    def line(self, place):
        x, z, y, core = place.x, place.lon // SIDE, place.lon % SIDE, place.core
        if self.axis == "x":
            return x, lambda q: (2 * q + core, place.lon)
        if self.axis == "y":
            return y, lambda q: (place.lat, z * SIDE + q)
        return z, lambda q: (place.lat, q * SIDE + y)

    def plane(self, place):
        x, z, y, core = place.x, place.lon // SIDE, place.lon % SIDE, place.core
        if self.axis == "x":
            return place.lon, lambda m: (place.lat, m)
        if self.axis == "y":
            return x * SIDE + z, lambda m: (2 * (m // SIDE) + core, m % SIDE * SIDE + y)
        return x * SIDE + y, lambda m: (2 * (m // SIDE) + core, z * SIDE + m % SIDE)


IN = Round(0, "z", 0, 80, 256)
OUT = Round(1, "y", 640, 64, 128)
POINT = Round(2, "x", 1152, 64, 128)
PARTS = 1664
DEPTH = 624

SIB_EMB, SIB_ROUTE, MARK_LAT, MARK_LON, DATA, BACK, SIB_PART = range(7)
SEMS = 7 + 18


def block(ref, chip, size=SLOT):
    return ref.at[pl.ds(pl.multiple_of(chip * size, size), size)]


def keep_ends(ends, row, values):
    for r in range(values.shape[0] // CLON):
        at = r * CLON
        ends[0, row + r, 0:1, :] = values[at : at + 1]
        ends[1, row + r, 0:1, :] = values[at + CLON - 1 : at + CLON]


def edge_columns(ends, cols):
    for side in range(2):
        cols[side] = ends[side, :, 0, :].astype(bf16)


def side_columns(to_cols, to_diag, west, east):
    for side, (into, above, below) in enumerate(((west, 0, 2), (east, 1, 3))):
        into[0:1, :] = to_diag[above].astype(f32)[CLAT - 1 : CLAT]
        into[1 : CLAT + 1, :] = to_cols[side].astype(f32)
        into[CLAT + 1 : CLAT + 2, :] = to_diag[below].astype(f32)[0:1]


def side_sums(west, east, weight, sides):
    for side, ref in ((0, west), (1, east)):
        b = 2 * side
        total = (
            weight(b) * ref[0:CLAT, :]
            + weight(3 + b) * ref[1 : CLAT + 1, :]
            + weight(6 + b) * ref[2 : CLAT + 2, :]
        )
        for i in range(CLAT):
            sides[side, i, 0:1, :] = total[i : i + 1, :]


def conv_part(rows, first, last, weight):
    columns = [
        weight(b) * rows[0] + weight(3 + b) * rows[1] + weight(6 + b) * rows[2] for b in range(3)
    ]
    index = lax.broadcasted_iota(i32, (CLON, CHUNK), 0)
    left = jnp.where(index == 0, first, pltpu.roll(columns[0], 1, 0))
    right = jnp.where(index == CLON - 1, last, pltpu.roll(columns[2], CLON - 1, 0))
    return columns[1] + left + right


def kernel(
    spec_in,
    owner,
    cell,
    w_in_in,
    w_out_in,
    w_point_in,
    w_depth,
    cot_in,
    latent,
    sums_out,
    spec_t,
    w_in,
    w_out,
    w_point,
    cot,
    preact,
    hidden,
    emb,
    emb_sib,
    route,
    route_sib,
    outgoing,
    arrived,
    table,
    table_lat,
    marks,
    places,
    gm_ext,
    grid_ext,
    cols,
    to_cols,
    to_diag,
    cols_x,
    to_cols_x,
    to_diag_x,
    west,
    east,
    sides,
    ends,
    depth_sums,
    g_grid,
    g_arrived,
    returned,
    part,
    part_sib,
    g_emb,
    mixed,
    parts,
    swap_out,
    swap_in,
    chip_sum,
    lines_in,
    lines_out,
    lines_point,
    quarter_in,
    quarter_out,
    quarter_point,
    gather_in,
    gather_out,
    gather_point,
    latent_here,
    result,
    out_sem,
    load_sem,
    local_sem,
    send_sem,
    recv_sem,
    halo_send,
    halo_recv,
):
    place = Place()
    core, me = place.core, place.chip
    loads = [
        pltpu.make_async_copy(src, dst, load_sem.at[i])
        for i, (src, dst) in enumerate(
            (
                (spec_in, spec_t),
                (w_in_in, w_in),
                (w_out_in, w_out),
                (w_point_in, w_point),
                (cot_in, cot),
            )
        )
    ]
    for copy in loads:
        copy.start()
    barrier, count = greet(place)

    def cross(src, dst, index, device):
        return remote(src, dst, send_sem.at[index], recv_sem.at[index], device)

    halo_g = Halo(place, gm_ext, cols, to_cols, to_diag, halo_send.at[0], halo_recv.at[0])
    halo_x = Halo(place, grid_ext, cols_x, to_cols_x, to_diag_x, halo_send.at[1], halo_recv.at[1])
    halo_g.clear_outside()
    halo_x.clear_outside()
    for copy in loads[:3]:
        copy.wait()
    vector_encode(spec_t, owner, cell, w_in, w_out, preact, hidden, emb, route, table)
    pl.semaphore_wait(barrier, count)

    swaps = [
        cross(emb, emb_sib, SIB_EMB, place.sibling),
        cross(route, route_sib, SIB_ROUTE, place.sibling),
    ]
    for copy in swaps:
        copy.start()
    keep_lat = pltpu.make_async_copy(
        table.at[place.lat], table_lat.at[place.lat], local_sem.at[5]
    )
    keep_lat.start()
    for step in range(1, N_LAT):
        lat = (place.lat + step) % N_LAT
        cross(table.at[lat], table_lat.at[place.lat], MARK_LAT, (lat, place.lon)).start()
    def spread(key, values, more):
        def one(i, carry):
            at = pl.multiple_of(i * PART, PART)
            index = lax.broadcasted_iota(i32, (PART, OBS), 0) + at
            pick = (index == key).astype(f32).astype(bf16)
            new = dot(pick, values[:, :C], ((1,), (0,)))
            if more:
                new = new + outgoing[pl.ds(at, PART), :].astype(f32)
            outgoing[pl.ds(at, PART), :] = new.astype(bf16)
            return carry

        lax.fori_loop(0, SLOTS // PART, one, 0)

    spread(slot_keys(route[...], core, core), emb, False)
    for copy in loads[3:]:
        copy.wait()

    def mix_back(i, carry):
        rows4 = cot[pl.ds(pl.multiple_of(i * 512, 512), 512), :]
        gm = dot(rows4, w_point[...], ((1,), (1,)))
        gm_ext[pl.ds(1 + 4 * i, 4)] = gm.astype(bf16).reshape(4, CLON, C)
        keep_ends(ends, 4 * i, gm)
        return carry

    lax.fori_loop(0, CLAT // 4, mix_back, 0)
    edge_columns(ends, cols)
    halo_g.start()
    keep_lat.wait()
    lat_row = pl.ds(0, N_LAT - 1)
    lat_marks = cross(table.at[lat_row], table_lat.at[lat_row], MARK_LAT, place.sibling)
    lat_marks.wait_recv()
    for lon in range(N_LON):
        marks[lon] = table_lat[:, lon, :]
    keep_lon = pltpu.make_async_copy(marks.at[place.lon], places.at[place.lon], local_sem.at[0])
    keep_lon.start()
    for step in range(1, N_LON):
        lon = (place.lon + step) % N_LON
        cross(marks.at[lon], places.at[place.lon], MARK_LON, (place.lat, lon)).start()
    for copy in swaps:
        copy.wait()
    spread(slot_keys(route_sib[...], core, 1 - core), emb_sib, True)
    keep = pltpu.make_async_copy(block(outgoing, me), block(arrived, me), local_sem.at[1])
    keep.start()

    def send_data(step, carry):
        chip, device = place.peer(step)
        cross(block(outgoing, chip), block(arrived, me), DATA, device).start()
        return carry

    lax.fori_loop(1, CHIPS, send_data, 0)
    some = pl.ds(0, (CHIPS - 1) * SLOT)
    few = pl.ds(0, CHIPS - 1)

    halo_g.wait()
    side_columns(to_cols, to_diag, west, east)
    side_sums(west, east, lambda k: w_depth[8 - k : 9 - k, :], sides)

    def conv_back(i, carry):
        for chunk in range(C // CHUNK):
            lanes = slice(chunk * CHUNK, (chunk + 1) * CHUNK)
            three = [gm_ext[i + a, :, lanes].astype(f32) for a in range(3)]
            first, last = sides[0, i, 0:1, lanes], sides[1, i, 0:1, lanes]
            acc = conv_part(three, first, last, lambda k: w_depth[8 - k : 9 - k, lanes])
            at = pl.ds(pl.multiple_of(i * CLON, CLON), CLON)
            g_grid[at, lanes] = (cot[at, lanes].astype(f32) + acc).astype(bf16)
        return carry

    lax.fori_loop(0, CLAT, conv_back, 0)

    keep_lon.wait()
    lon_row = pl.ds(0, N_LON - 1)
    lon_marks = cross(marks.at[lon_row], places.at[lon_row], MARK_LON, place.sibling)
    lon_marks.wait_recv()
    tiles = N_LAT * N_LON
    known = places[...].reshape(tiles, META).astype(bf16)

    def sender(slot):
        chip = slot // SLOT
        return chip % N_LON * N_LAT + chip // N_LON * 2 + slot // CAP % 2

    def cells_of(axis):
        shape = (SLOTS, tiles) if axis == 0 else (tiles, SLOTS)
        slot = lax.broadcasted_iota(i32, shape, axis)
        other = lax.broadcasted_iota(i32, shape, 1 - axis)
        expand = (sender(slot) == other).astype(f32).astype(bf16)
        if axis == 0:
            wide = dot(expand, known, ((1,), (0,)))
        else:
            wide = dot(known, expand, ((0,), (0,)))
        value = jnp.where(other < CAP, 16.0, 1.0) * wide
        keep = jnp.where(other % CAP == slot % CAP, value, 0.0)
        return (jnp.sum(keep, axis=1 - axis, keepdims=True) - 1.0).astype(i32)

    place_col, place_row = cells_of(0), cells_of(1)
    cells = lax.broadcasted_iota(i32, (PART, CELLS), 1)
    for at in range(0, SLOTS, PART):
        pick = (place_col[at : at + PART] == cells).astype(f32).astype(bf16)
        g_arrived[at : at + PART, :] = dot(pick, g_grid[...], ((1,), (0,))).astype(bf16)
    keep_back = pltpu.make_async_copy(block(g_arrived, me), block(returned, me), local_sem.at[2])
    keep_back.start()

    def send_back(step, carry):
        chip, device = place.peer(step)
        cross(block(g_arrived, chip), block(returned, me), BACK, device).start()
        return carry

    lax.fori_loop(1, CHIPS, send_back, 0)

    all_data = cross(outgoing.at[some], arrived.at[some], DATA, place.sibling)
    all_data.wait_recv()
    keep.wait()

    def bin_rows(i, carry):
        index = lax.broadcasted_iota(i32, (PART, SLOTS), 0) + i * PART
        pick = (index == place_row).astype(f32).astype(bf16)
        cells_here = dot(pick, arrived[...], ((1,), (0,)))
        grid_ext[pl.ds(1 + 2 * i, 2)] = cells_here.astype(bf16).reshape(2, CLON, C)
        keep_ends(ends, 2 * i, cells_here)
        return carry

    lax.fori_loop(0, CELLS // PART, bin_rows, 0)
    edge_columns(ends, cols_x)
    halo_x.start()

    def conv_rows(low, high, chunk, sums):
        lanes = slice(chunk * CHUNK, (chunk + 1) * CHUNK)

        def one(i, sums):
            three = [grid_ext[i + a, :, lanes].astype(f32) for a in range(3)]
            acc = conv_part(three, 0.0, 0.0, lambda k: w_depth[k : k + 1, lanes])
            at = pl.ds(pl.multiple_of(i * CLON, CLON), CLON)
            mixed[at, lanes] = acc.astype(bf16)
            ends[0, i, 0:1, lanes] = acc[0:1]
            ends[1, i, 0:1, lanes] = acc[CLON - 1 : CLON]
            middle = gm_ext[i + 1, :, lanes].astype(f32)
            index = lax.broadcasted_iota(i32, (CLON, CHUNK), 0)
            shifted = [
                jnp.where(index == CLON - 1, 0.0, pltpu.roll(middle, CLON - 1, 0)),
                middle,
                jnp.where(index == 0, 0.0, pltpu.roll(middle, 1, 0)),
            ]
            return tuple(
                sums[3 * a + b] + jnp.sum((shifted[b] * three[a]).reshape(16, 8, CHUNK), axis=0)
                for a in range(3)
                for b in range(3)
            )

        return lax.fori_loop(low, high, one, sums)

    for chunk in range(C // CHUNK):
        sums = conv_rows(1, CLAT - 1, chunk, tuple(jnp.zeros((8, CHUNK), f32) for _ in range(9)))
        for k in range(9):
            depth_sums[chunk, k] = sums[k]
    halo_x.wait()
    side_columns(to_cols_x, to_diag_x, west, east)
    side_sums(west, east, lambda k: w_depth[k : k + 1, :], sides)
    for chunk in range(C // CHUNK):
        lanes = slice(chunk * CHUNK, (chunk + 1) * CHUNK)
        sums = conv_rows(0, 1, chunk, tuple(depth_sums[chunk, k] for k in range(9)))
        sums = conv_rows(CLAT - 1, CLAT, chunk, sums)
        for k, (a, b) in enumerate(offsets):
            total = jnp.sum(sums[k], axis=0, keepdims=True)
            if b:
                side = (west if b < 0 else east)[1 + a : 1 + a + CLAT, lanes]
                edge = cols[0 if b < 0 else 1, :, lanes].astype(f32)
                total = total + jnp.sum(side * edge, axis=0, keepdims=True)
            parts[DEPTH + k : DEPTH + k + 1, lanes] = total

    def side_rows(i, carry):
        index = lax.broadcasted_iota(i32, (16, C), 0)
        for side, row in ((0, 0), (1, CLON - 16)):
            at = pl.ds(pl.multiple_of(i * CLON + row, 16), 16)
            whole = (ends[side, i, 0:1, :] + sides[side, i, 0:1, :]).astype(bf16).astype(f32)
            old = mixed[at, :].astype(f32)
            mixed[at, :] = jnp.where(index == 15 * side, whole, old).astype(bf16)
        return carry

    lax.fori_loop(0, CLAT, side_rows, 0)
    parts[SPEC:DEPTH, :] = jnp.zeros((DEPTH - SPEC, C), f32)
    parts[DEPTH + 9 : ROWS_IN, :] = jnp.zeros((ROWS_IN - DEPTH - 9, C), f32)

    lines = {IN: lines_in, OUT: lines_out, POINT: lines_point}
    quarter = {IN: quarter_in, OUT: quarter_out, POINT: quarter_point}
    gathers = {IN: gather_in, OUT: gather_out, POINT: gather_point}

    def half_of(r, which):
        return pl.ds(pl.multiple_of(r.first + which * r.half, 16), r.half)

    def local_half(r):
        return pl.ds(r.base, r.half)

    def swap_halves(r):
        swap_out[local_half(r), :] = parts[half_of(r, 1 - core), :].astype(bf16)
        copy = cross(swap_out.at[local_half(r)], swap_in.at[local_half(r)], r.sems[0], place.sibling)
        copy.start()
        return copy

    def rows_at(start, size):
        return pl.ds(pl.multiple_of(start, 16), size)

    def send_line(r):
        here = local_half(r)
        chip_sum[here, :] = (
            parts[half_of(r, core), :] + swap_in[here, :].astype(f32)
        ).astype(bf16)
        at, device = r.line(place)
        for step in range(1, 4):
            q = (at + step) % 4
            src = chip_sum.at[rows_at(r.base + q * r.quarter, r.quarter)]
            cross(src, lines[r].at[at], r.sems[1], device(q)).start()

    def piece(r, start, index):
        rows_here = rows_at(start + index // r.across * 16, 16)
        return rows_here, pl.ds(pl.multiple_of(index % r.across * r.width, 128), r.width)

    def waiting(r, size, sem):
        some = gathers[r].at[pl.ds(0, size)]
        return cross(some, some, r.sems[sem], place.sibling)

    def waiting_line(r, sem):
        some = lines[r].at[pl.ds(0, 3)]
        return cross(some, some, r.sems[sem], place.sibling)

    def send_plane(r):
        waiting_line(r, 1).wait_recv()
        at, _ = r.line(place)
        total = chip_sum[rows_at(r.base + at * r.quarter, r.quarter), :].astype(f32)
        for step in range(1, 4):
            total = total + lines[r][(at + step) % 4].astype(f32)
        quarter[r][...] = total.astype(bf16)
        me_here, device = r.plane(place)

        def send(step, carry):
            index = (me_here + step) % 16

            @pl.when(index < r.count)
            def _():
                where = piece(r, 0, index)
                cross(quarter[r].at[where], gathers[r].at[me_here], r.sems[2], device(index)).start()

            return carry

        lax.fori_loop(1, 16, send, 0)

    def result_rows(r):
        return r.first + core * r.half + r.line(place)[0] * r.quarter

    def share_plane(r):
        me_here, device = r.plane(place)

        @pl.when(me_here < r.count)
        def _():
            waiting(r, 15, 2).wait_recv()
            total = quarter[r][piece(r, 0, me_here)].astype(f32)
            for step in range(1, 16):
                total = total + gathers[r][(me_here + step) % 16].astype(f32)
            where = piece(r, result_rows(r), me_here)
            result[where] = total.astype(bf16)

            def share(step, carry):
                index = (me_here + step) % 16
                cross(result.at[where], result.at[where], r.sems[3], device(index)).start()
                return carry

            lax.fori_loop(1, 16, share, 0)

    def share_line(r):
        me_here, _ = r.plane(place)
        if r.count == 16:
            waiting(r, 15, 3).wait_recv()
        else:
            pl.when(me_here < r.count)(lambda: waiting(r, r.count - 1, 3).wait_recv())
            pl.when(me_here >= r.count)(lambda: waiting(r, r.count, 3).wait_recv())
        at, device = r.line(place)
        here = result.at[rows_at(result_rows(r), r.quarter)]
        for step in range(1, 4):
            cross(here, here, r.sems[4], device((at + step) % 4)).start()

    def last_swap(r):
        waiting_line(r, 4).wait_recv()
        half = result.at[half_of(r, core)]
        copy = cross(half, half, r.sems[5], place.sibling)
        copy.start()
        return copy

    def sent(r):
        waiting_line(r, 1).wait_send()
        waiting_line(r, 4).wait_send()
        me_here, _ = r.plane(place)

        def owner():
            waiting(r, r.count - 1, 2).wait_send()
            waiting(r, 15, 3).wait_send()

        if r.count == 16:
            owner()
        else:
            pl.when(me_here < r.count)(owner)
            pl.when(me_here >= r.count)(lambda: waiting(r, r.count, 2).wait_send())

    def point(i):
        at = slice(i * 512, (i + 1) * 512)
        here = grid_ext[1 + 4 * i : 5 + 4 * i].astype(f32).reshape(512, C)
        latent_here[at, :] = (here + dot(mixed[at, :], w_point[...], ((1,), (0,)))).astype(bf16)


    keep_back.wait()
    all_back = cross(g_arrived.at[some], returned.at[some], BACK, place.sibling)
    all_back.wait_recv()

    def gathered(key):
        total = jnp.zeros((OBS, C), f32)
        for at in range(0, SLOTS, PART):
            index = lax.broadcasted_iota(i32, (PART, OBS), 0) + at
            pick = (index == key).astype(f32).astype(bf16)
            total = total + dot(pick, returned[at : at + PART, :], ((0,), (0,)))
        return total

    part[...] = gathered(slot_keys(route_sib[...], core, 1 - core)).astype(bf16)
    swap = cross(part, part_sib, SIB_PART, place.sibling)
    swap.start()
    parts[POINT.first : PARTS, :] = dot(mixed[...], cot[...], ((0,), (0,)))
    point_swap = swap_halves(POINT)
    own = gathered(slot_keys(route[...], core, core))
    swap.wait()
    g_emb[...] = (own + part_sib[...].astype(f32)).astype(bf16)
    parts[OUT.first : OUT.first + C, :] = dot(hidden[...], g_emb[...], ((0,), (0,)))
    out_swap = swap_halves(OUT)
    g_hidden = dot(g_emb[...], w_out[...], ((1,), (1,)))
    pre = preact[...]
    sig = 1.0 / (1.0 + jnp.exp(-pre))
    g_pre = (g_hidden * sig * (1.0 + pre * (1.0 - sig))).astype(bf16)
    parts[0:SPEC, :] = dot(spec_t[...], g_pre, ((1,), (0,)))
    in_swap = swap_halves(IN)
    point_swap.wait()
    send_line(POINT)
    out_swap.wait()
    send_line(OUT)
    in_swap.wait()
    send_line(IN)
    point(0)
    send_plane(POINT)
    send_plane(OUT)
    send_plane(IN)
    point(1)
    share_plane(POINT)
    share_plane(OUT)
    share_plane(IN)
    point(2)
    share_line(POINT)
    share_line(OUT)
    share_line(IN)
    point(3)
    store = pltpu.make_async_copy(latent_here, latent, local_sem.at[6])
    store.start()
    rounds = (POINT, OUT, IN)

    def leave(r, which, index):
        half = half_of(r, which)
        return pltpu.make_async_copy(result.at[half], sums_out.at[half], out_sem.at[index])

    last, leaving = [], []
    for i, r in enumerate(rounds):
        last.append(last_swap(r))
        leaving.append(leave(r, core, i))
        leaving[-1].start()
    for r in rounds:
        sent(r)
    store.wait()
    for copy in (lat_marks, lon_marks, all_data, all_back):
        copy.wait_send()
    for i, r in enumerate(rounds):
        last[i].wait()
        leaving.append(leave(r, 1 - core, 3 + i))
        leaving[-1].start()
    for copy in leaving:
        copy.wait()


def run(spec_t, owner, cell, w_in, w_out, w_point, w_depth, cot):
    dma = pltpu.SemaphoreType.DMA
    anywhere = pl.BlockSpec(memory_space=pl.ANY)
    field = VMEM((CLAT + 2, CLON, C), bf16)
    half = VMEM((PARTS // 2, C), bf16)
    return pl.pallas_call(
        kernel,
        out_shape=[
            pltpu.VMEM((CELLS, C), bf16),
            pltpu.VMEM((PARTS, C), bf16),
        ],
        in_specs=[anywhere, vmem(), vmem(), anywhere, anywhere, anywhere, vmem(), anywhere],
        out_specs=[anywhere, anywhere],
        scratch_shapes=[
            VMEM((SPEC, OBS), bf16),
            VMEM((SPEC, C), bf16),
            VMEM((C, C), bf16),
            VMEM((C, C), bf16),
            VMEM((CELLS, C), bf16),
            VMEM((OBS, C), f32),
            VMEM((OBS, C), bf16),
            VMEM((OBS, C + META), bf16),
            VMEM((OBS, C + META), bf16),
            VMEM((8, OBS), i32),
            VMEM((8, OBS), i32),
            VMEM((SLOTS, C), bf16),
            VMEM((SLOTS, C), bf16),
            VMEM((N_LAT, N_LON, META), f32),
            VMEM((N_LAT, N_LON, META), f32),
            VMEM((N_LON, N_LAT, META), f32),
            VMEM((N_LON, N_LAT, META), f32),
            field,
            field,
            VMEM((2, CLAT, C), bf16),
            VMEM((2, CLAT, C), bf16),
            VMEM((4, CLAT, C), bf16),
            VMEM((2, CLAT, C), bf16),
            VMEM((2, CLAT, C), bf16),
            VMEM((4, CLAT, C), bf16),
            VMEM((24, C), f32),
            VMEM((24, C), f32),
            VMEM((2, CLAT, 8, C), f32),
            VMEM((2, CLAT, 8, C), f32),
            VMEM((C // CHUNK, 9, 8, CHUNK), f32),
            VMEM((CELLS, C), bf16),
            VMEM((SLOTS, C), bf16),
            VMEM((SLOTS, C), bf16),
            VMEM((OBS, C), bf16),
            VMEM((OBS, C), bf16),
            VMEM((OBS, C), bf16),
            VMEM((CELLS, C), bf16),
            VMEM((PARTS, C), f32),
            half,
            half,
            half,
        ]
        + [VMEM((4, r.quarter, C), bf16) for r in (IN, OUT, POINT)]
        + [VMEM((r.quarter, C), bf16) for r in (IN, OUT, POINT)]
        + [VMEM((16, 16, r.width), bf16) for r in (IN, OUT, POINT)]
        + [
            VMEM((CELLS, C), bf16),
            VMEM((PARTS, C), bf16),
            dma((6,)),
            dma((5,)),
            dma((7,)),
            dma((SEMS,)),
            dma((SEMS,)),
            dma((2, 8)),
            dma((2, 8)),
        ],
        compiler_params=pltpu.CompilerParams(
            collective_id=0, has_side_effects=True, vmem_limit_bytes=51 << 20
        ),
    )(spec_t, owner, cell, w_in, w_out, w_point, w_depth, cot)


def finish_kernel(latent_in, total, latent, g_in, g_out, g_point, g_depth, in_f, out_f, point_f, sem):
    obs_scale = 1.0 / math.sqrt(OBS * N_LAT * N_LON)
    cell_scale = 1.0 / math.sqrt(CELLS * N_LAT * N_LON)
    copies = [pltpu.make_async_copy(latent_in, latent, sem.at[3])]
    copies[0].start()
    plan = (
        (in_f, g_in, IN.first, obs_scale),
        (out_f, g_out, OUT.first, obs_scale),
        (point_f, g_point, POINT.first, cell_scale),
    )
    for i, (values, target, first, scale) in enumerate(plan):
        values[...] = total[first : first + values.shape[0], :].astype(f32) * scale
        copies.append(pltpu.make_async_copy(values, target, sem.at[i]))
        copies[-1].start()
    g_depth[...] = total[DEPTH : DEPTH + 16, :].astype(f32)[0:9] * cell_scale
    for copy in copies:
        copy.wait()


def finish(latent, total):
    anywhere = pl.BlockSpec(memory_space=pl.ANY)
    shapes = [(SPEC, C), (C, C), (C, C), (9, C)]
    return pl.pallas_call(
        finish_kernel,
        out_shape=[jax.ShapeDtypeStruct((CELLS, C), bf16)]
        + [jax.ShapeDtypeStruct(shape, f32) for shape in shapes],
        in_specs=[vmem(), vmem()],
        out_specs=[anywhere] * 4 + [vmem()],
        scratch_shapes=[VMEM(shape, f32) for shape in shapes[:3]] + [pltpu.SemaphoreType.DMA((4,))],
        compiler_params=pltpu.CompilerParams(vmem_limit_bytes=12 << 20),
    )(latent, total)


def on_device(spectra, owner, cell, w_in, w_out, w_point, w_depth, cotangent):
    latent, total = run(
        spectra.T,
        owner.reshape(1, OBS),
        cell.reshape(1, OBS),
        w_in,
        w_out,
        w_point,
        w_depth,
        cotangent.reshape(CELLS, C),
    )
    latent, *grads = finish(latent, total)
    return (latent.reshape(CLAT, CLON, C), *grads)


def solution(mesh):
    in_specs = (
        P(("lat", "lon"), None),
        P(("lat", "lon"), None),
        P(("lat", "lon")),
        P(),
        P(),
        P(),
        P(),
        P("lat", "lon", None),
    )
    out_specs = (P("lat", "lon", None), P(), P(), P(), P())
    return jax.shard_map(
        on_device, mesh=mesh, in_specs=in_specs, out_specs=out_specs, check_vma=False
    )
```

```python
import math

import jax
import jax.numpy as jnp
from jax import lax
from jax.experimental import pallas as pl
from jax.experimental.pallas import tpu as pltpu
from jax.sharding import PartitionSpec as P

offsets = [(a, b) for a in (-1, 0, 1) for b in (-1, 0, 1)]
f32, bf16, i32 = jnp.float32, jnp.bfloat16, jnp.int32

N_LAT, N_LON, SIDE = 8, 16, 4
CHIPS = N_LAT // 2 * N_LON
CAP = 8
SLOT = 2 * CAP
SLOTS = CHIPS * SLOT
OBS = 512
C = 512
CLAT, CLON = 16, 128
CELLS = CLAT * CLON
SPEC = 616
META = 128
ROWS_IN = 640
PART = 256
CHUNK = 128

VMEM = pltpu.VMEM


def vmem():
    return pl.BlockSpec(memory_space=pltpu.VMEM)


def dot(a, b, dims):
    return lax.dot_general(a, b, (dims, ((), ())), preferred_element_type=f32)


class Place:
    def __init__(self):
        self.lat = lax.axis_index("lat")
        self.lon = lax.axis_index("lon")
        self.core = self.lat % 2
        self.x = self.lat // 2
        self.chip = self.x * N_LON + self.lon
        self.sibling = (self.x * 2 + 1 - self.core, self.lon)

    def peer(self, step):
        step = (step * 37) % CHIPS
        x = (self.x + step // N_LON) % (N_LAT // 2)
        z = (self.lon // SIDE + step // SIDE) % SIDE
        y = (self.lon + step) % SIDE
        lon = z * SIDE + y
        return x * N_LON + lon, (x * 2 + self.core, lon)

    def of_chip(self, chip):
        return (chip // N_LON * 2 + self.core, chip % N_LON)


def remote(src, dst, send, recv, device):
    return pltpu.make_async_remote_copy(
        src_ref=src,
        dst_ref=dst,
        send_sem=send,
        recv_sem=recv,
        device_id=device,
        device_id_type=pl.DeviceIdType.MESH,
    )


def greet(place):
    barrier = pltpu.get_barrier_semaphore()

    def hello(device):
        pl.semaphore_signal(
            barrier, inc=1, device_id=device, device_id_type=pl.DeviceIdType.MESH
        )

    def one(step, carry):
        hello(place.peer(step)[1])
        return carry

    lax.fori_loop(1, CHIPS, one, 0)
    others = N_LAT // 2
    for x in range(others):
        hello((2 * x + 1 - place.core, place.lon))
    for side in (-1, 1):
        inside = (place.lat + side >= 0) & (place.lat + side < N_LAT)

        @pl.when(inside)
        def _(side=side):
            for turn in (-1, 1):
                hello((place.lat + side, (place.lon + turn + N_LON) % N_LON))

    edges = (place.lat > 0).astype(i32) + (place.lat < N_LAT - 1).astype(i32)
    return barrier, CHIPS - 1 + others + 2 * edges


class Halo:
    def __init__(self, place, ext, cols, to_cols, to_diag, send, recv):
        self.place = place
        self.ext, self.to_diag = ext, to_diag
        lat, lon = place.lat, place.lon
        east, west = (lon + 1) % N_LON, (lon + N_LON - 1) % N_LON
        has_north, has_south = lat > 0, lat < N_LAT - 1
        south, north = jnp.minimum(lat + 1, N_LAT - 1), jnp.maximum(lat - 1, 0)
        plan = [
            (ext.at[CLAT], ext.at[0], (south, lon), has_south, has_north),
            (ext.at[1], ext.at[CLAT + 1], (north, lon), has_north, has_south),
            (cols.at[1], to_cols.at[0], (lat, east), None, None),
            (cols.at[0], to_cols.at[1], (lat, west), None, None),
            (cols.at[1], to_diag.at[0], (south, east), has_south, has_north),
            (cols.at[0], to_diag.at[1], (south, west), has_south, has_north),
            (cols.at[1], to_diag.at[2], (north, east), has_north, has_south),
            (cols.at[0], to_diag.at[3], (north, west), has_north, has_south),
        ]
        self.plan = [
            (remote(src, dst, send.at[i], recv.at[i], device), sends, receives)
            for i, (src, dst, device, sends, receives) in enumerate(plan)
        ]

    def start(self):
        for copy, sends, _ in self.plan:
            if sends is None:
                copy.start()
            else:
                pl.when(sends)(copy.start)

    def wait(self):
        for copy, sends, receives in self.plan:
            if sends is None:
                copy.wait_send()
                copy.wait_recv()
            else:
                pl.when(sends)(copy.wait_send)
                pl.when(receives)(copy.wait_recv)

    def clear_outside(self):
        @pl.when(self.place.lat == 0)
        def _():
            self.ext[0] = jnp.zeros((CLON, C), bf16)
            self.to_diag[0] = jnp.zeros((CLAT, C), bf16)
            self.to_diag[1] = jnp.zeros((CLAT, C), bf16)

        @pl.when(self.place.lat == N_LAT - 1)
        def _():
            self.ext[CLAT + 1] = jnp.zeros((CLON, C), bf16)
            self.to_diag[2] = jnp.zeros((CLAT, C), bf16)
            self.to_diag[3] = jnp.zeros((CLAT, C), bf16)


def vector_encode(spec_t, owner, cell, w_in, w_out, preact, hidden, emb, route, table):
    pre = dot(spec_t[...], w_in[...], ((0,), (0,)))
    preact[...] = pre
    hid = (pre * (1.0 / (1.0 + jnp.exp(-pre)))).astype(bf16)
    hidden[...] = hid
    emb[:, :C] = dot(hid, w_out[...], ((1,), (0,))).astype(bf16)
    places = cell[...]
    values = jnp.concatenate(
        [owner[...], places // 16, places % 16, jnp.zeros((13, OBS), i32)], axis=0
    ).astype(f32).astype(bf16)
    down = lax.broadcasted_iota(i32, (OBS, OBS), 0)
    across = lax.broadcasted_iota(i32, (OBS, OBS), 1)
    eye = (down == across).astype(f32).astype(bf16)
    columns = dot(eye, values, ((1,), (1,)))
    tile_col, high_col, low_col = columns[:, 0:1], columns[:, 1:2], columns[:, 2:3]
    tile_row = values[0:1, :].astype(f32)
    tiles = N_LAT * N_LON
    hits = (tile_col == lax.broadcasted_iota(i32, (OBS, tiles), 1).astype(f32)).astype(f32)
    lower = (across <= down).astype(f32).astype(bf16)
    count = dot(lower, hits.astype(bf16), ((1,), (0,)))
    pos_col = (jnp.sum(count * hits, axis=1, keepdims=True) - 1.0).astype(i32)
    hits_t = (tile_row == lax.broadcasted_iota(i32, (tiles, OBS), 0).astype(f32)).astype(f32)
    upper = (down <= across).astype(f32).astype(bf16)
    count_t = dot(hits_t.astype(bf16), upper, ((1,), (0,)))
    pos_row = (jnp.sum(count_t * hits_t, axis=0, keepdims=True) - 1.0).astype(i32)
    lane = lax.broadcasted_iota(i32, (OBS, META), 1)
    kind = lane // CAP
    value = jnp.where(kind == 0, high_col, jnp.where(kind == 1, low_col, 1.0))
    keep = (lane % CAP == pos_col) & (kind < 3)
    tile_at = tile_col.astype(i32)
    lat_at = tile_at // N_LON
    chip_at = lat_at // 2 * N_LON + tile_at % N_LON
    about = jnp.where(lane == 24, chip_at, jnp.where(lane == 25, pos_col, lat_at % 2)).astype(f32)
    about = jnp.where((lane >= 24) & (lane < 27), about, 0.0)
    emb[:, C:] = jnp.where(keep, value, about).astype(bf16)
    table[...] = dot(hits_t.astype(bf16), emb[:, C:], ((1,), (0,))).reshape(N_LAT, N_LON, META)
    tile = tile_row.astype(i32)
    lat, lon = tile // N_LON, tile % N_LON
    chip = lat // 2 * N_LON + lon
    route[...] = jnp.concatenate(
        [chip * SLOT + pos_row, lat % 2, chip, jnp.zeros((5, OBS), i32)], axis=0
    )


def slot_keys(route, mine, core):
    return jnp.where(route[1:2, :] == mine, route[0:1, :] + CAP * core, -1)


class Round:
    def __init__(self, number, axis, first, quarter, width):
        self.axis, self.first, self.quarter, self.width = axis, first, quarter, width
        self.half = 4 * quarter
        self.base = first // 2
        self.across = C // width
        self.count = quarter // 16 * self.across
        self.sems = range(7 + 6 * number, 13 + 6 * number)

    def line(self, place):
        x, z, y, core = place.x, place.lon // SIDE, place.lon % SIDE, place.core
        if self.axis == "x":
            return x, lambda q: (2 * q + core, place.lon)
        if self.axis == "y":
            return y, lambda q: (place.lat, z * SIDE + q)
        return z, lambda q: (place.lat, q * SIDE + y)

    def plane(self, place):
        x, z, y, core = place.x, place.lon // SIDE, place.lon % SIDE, place.core
        if self.axis == "x":
            return place.lon, lambda m: (place.lat, m)
        if self.axis == "y":
            return x * SIDE + z, lambda m: (2 * (m // SIDE) + core, m % SIDE * SIDE + y)
        return x * SIDE + y, lambda m: (2 * (m // SIDE) + core, z * SIDE + m % SIDE)


IN = Round(0, "z", 0, 80, 256)
OUT = Round(1, "y", 640, 64, 128)
POINT = Round(2, "x", 1152, 64, 128)
PARTS = 1664
DEPTH = 624

SIB_EMB, SIB_ROUTE, MARK_LAT, MARK_LON, DATA, BACK, SIB_PART = range(7)
SEMS = 7 + 18


def block(ref, chip, size=SLOT):
    return ref.at[pl.ds(pl.multiple_of(chip * size, size), size)]


def keep_ends(ends, row, values):
    for r in range(values.shape[0] // CLON):
        at = r * CLON
        ends[0, row + r, 0:1, :] = values[at : at + 1]
        ends[1, row + r, 0:1, :] = values[at + CLON - 1 : at + CLON]


def edge_columns(ends, cols):
    for side in range(2):
        cols[side] = ends[side, :, 0, :].astype(bf16)


def side_columns(to_cols, to_diag, west, east):
    for side, (into, above, below) in enumerate(((west, 0, 2), (east, 1, 3))):
        into[0:1, :] = to_diag[above].astype(f32)[CLAT - 1 : CLAT]
        into[1 : CLAT + 1, :] = to_cols[side].astype(f32)
        into[CLAT + 1 : CLAT + 2, :] = to_diag[below].astype(f32)[0:1]


def side_totals(west, east, weight):
    return [
        weight(b) * ref[0:CLAT, :]
        + weight(3 + b) * ref[1 : CLAT + 1, :]
        + weight(6 + b) * ref[2 : CLAT + 2, :]
        for b, ref in ((0, west), (2, east))
    ]


def side_sums(west, east, weight, sides):
    for side, total in enumerate(side_totals(west, east, weight)):
        for i in range(CLAT):
            sides[side, i, 0:1, :] = total[i : i + 1, :]


def conv_part(rows, first, last, weight):
    columns = [
        weight(b) * rows[0] + weight(3 + b) * rows[1] + weight(6 + b) * rows[2] for b in range(3)
    ]
    index = lax.broadcasted_iota(i32, (CLON, CHUNK), 0)
    left = jnp.where(index == 0, first, pltpu.roll(columns[0], 1, 0))
    right = jnp.where(index == CLON - 1, last, pltpu.roll(columns[2], CLON - 1, 0))
    return columns[1] + left + right


def kernel(
    spec_in,
    owner,
    cell,
    w_in_in,
    w_out_in,
    w_point_in,
    w_depth,
    cot_in,
    latent,
    sums_out,
    spec_t,
    w_in,
    w_out,
    w_point,
    cot,
    preact,
    hidden,
    emb,
    emb_sib,
    route,
    route_sib,
    outgoing,
    arrived,
    table,
    table_lat,
    marks,
    places,
    gm_ext,
    grid_ext,
    cols,
    to_cols,
    to_diag,
    cols_x,
    to_cols_x,
    to_diag_x,
    west,
    east,
    sides,
    ends,
    depth_sums,
    g_grid,
    g_arrived,
    returned,
    part,
    part_sib,
    g_emb,
    mixed,
    parts,
    swap_out,
    swap_in,
    chip_sum,
    lines_in,
    lines_out,
    lines_point,
    quarter_in,
    quarter_out,
    quarter_point,
    gather_in,
    gather_out,
    gather_point,
    latent_here,
    result,
    out_sem,
    load_sem,
    local_sem,
    send_sem,
    recv_sem,
    halo_send,
    halo_recv,
):
    place = Place()
    core, me = place.core, place.chip
    loads = [
        pltpu.make_async_copy(src, dst, load_sem.at[i])
        for i, (src, dst) in enumerate(
            (
                (spec_in, spec_t),
                (w_in_in, w_in),
                (w_out_in, w_out),
                (w_point_in, w_point),
                (cot_in, cot),
            )
        )
    ]
    for copy in loads:
        copy.start()
    barrier, count = greet(place)

    def cross(src, dst, index, device):
        return remote(src, dst, send_sem.at[index], recv_sem.at[index], device)

    halo_g = Halo(place, gm_ext, cols, to_cols, to_diag, halo_send.at[0], halo_recv.at[0])
    halo_x = Halo(place, grid_ext, cols_x, to_cols_x, to_diag_x, halo_send.at[1], halo_recv.at[1])
    halo_g.clear_outside()
    halo_x.clear_outside()
    for copy in loads[:3]:
        copy.wait()
    vector_encode(spec_t, owner, cell, w_in, w_out, preact, hidden, emb, route, table)
    pl.semaphore_wait(barrier, count)

    swaps = [
        cross(emb, emb_sib, SIB_EMB, place.sibling),
        cross(route, route_sib, SIB_ROUTE, place.sibling),
    ]
    for copy in swaps:
        copy.start()
    keep_lat = pltpu.make_async_copy(
        table.at[place.lat], table_lat.at[place.lat], local_sem.at[5]
    )
    keep_lat.start()
    for step in range(1, N_LAT):
        lat = (place.lat + step) % N_LAT
        cross(table.at[lat], table_lat.at[place.lat], MARK_LAT, (lat, place.lon)).start()
    def spread(key, values, more):
        def one(i, carry):
            at = pl.multiple_of(i * PART, PART)
            index = lax.broadcasted_iota(i32, (PART, OBS), 0) + at
            pick = (index == key).astype(f32).astype(bf16)
            new = dot(pick, values[:, :C], ((1,), (0,)))
            if more:
                new = new + outgoing[pl.ds(at, PART), :].astype(f32)
            outgoing[pl.ds(at, PART), :] = new.astype(bf16)
            return carry

        lax.fori_loop(0, SLOTS // PART, one, 0)

    spread(slot_keys(route[...], core, core), emb, False)
    for copy in loads[3:]:
        copy.wait()

    def mix_back(i, carry):
        rows4 = cot[pl.ds(pl.multiple_of(i * 512, 512), 512), :]
        gm = dot(rows4, w_point[...], ((1,), (1,)))
        gm_ext[pl.ds(1 + 4 * i, 4)] = gm.astype(bf16).reshape(4, CLON, C)
        keep_ends(ends, 4 * i, gm)
        return carry

    lax.fori_loop(0, CLAT // 4, mix_back, 0)
    edge_columns(ends, cols)
    halo_g.start()
    keep_lat.wait()
    lat_row = pl.ds(0, N_LAT - 1)
    lat_marks = cross(table.at[lat_row], table_lat.at[lat_row], MARK_LAT, place.sibling)
    lat_marks.wait_recv()
    for lon in range(N_LON):
        marks[lon] = table_lat[:, lon, :]
    keep_lon = pltpu.make_async_copy(marks.at[place.lon], places.at[place.lon], local_sem.at[0])
    keep_lon.start()
    for step in range(1, N_LON):
        lon = (place.lon + step) % N_LON
        cross(marks.at[lon], places.at[place.lon], MARK_LON, (place.lat, lon)).start()
    for copy in swaps:
        copy.wait()
    spread(slot_keys(route_sib[...], core, 1 - core), emb_sib, True)
    keep = pltpu.make_async_copy(block(outgoing, me), block(arrived, me), local_sem.at[1])
    keep.start()

    def send_data(step, carry):
        chip, device = place.peer(step)
        cross(block(outgoing, chip), block(arrived, me), DATA, device).start()
        return carry

    lax.fori_loop(1, CHIPS, send_data, 0)
    some = pl.ds(0, (CHIPS - 1) * SLOT)
    few = pl.ds(0, CHIPS - 1)

    halo_g.wait()
    side_columns(to_cols, to_diag, west, east)
    side_sums(west, east, lambda k: w_depth[8 - k : 9 - k, :], sides)

    def conv_back(i, carry):
        for chunk in range(C // CHUNK):
            lanes = slice(chunk * CHUNK, (chunk + 1) * CHUNK)
            three = [gm_ext[i + a, :, lanes].astype(f32) for a in range(3)]
            first, last = sides[0, i, 0:1, lanes], sides[1, i, 0:1, lanes]
            acc = conv_part(three, first, last, lambda k: w_depth[8 - k : 9 - k, lanes])
            at = pl.ds(pl.multiple_of(i * CLON, CLON), CLON)
            g_grid[at, lanes] = (cot[at, lanes].astype(f32) + acc).astype(bf16)
        return carry

    lax.fori_loop(0, CLAT, conv_back, 0)

    keep_lon.wait()
    lon_row = pl.ds(0, N_LON - 1)
    lon_marks = cross(marks.at[lon_row], places.at[lon_row], MARK_LON, place.sibling)
    lon_marks.wait_recv()
    tiles = N_LAT * N_LON
    known = places[...].reshape(tiles, META).astype(bf16)

    def sender(slot):
        chip = slot // SLOT
        return chip % N_LON * N_LAT + chip // N_LON * 2 + slot // CAP % 2

    def cells_of(axis):
        shape = (SLOTS, tiles) if axis == 0 else (tiles, SLOTS)
        slot = lax.broadcasted_iota(i32, shape, axis)
        other = lax.broadcasted_iota(i32, shape, 1 - axis)
        expand = (sender(slot) == other).astype(f32).astype(bf16)
        if axis == 0:
            wide = dot(expand, known, ((1,), (0,)))
        else:
            wide = dot(known, expand, ((0,), (0,)))
        value = jnp.where(other < CAP, 16.0, 1.0) * wide
        keep = jnp.where((other % CAP == slot % CAP) & (other < 3 * CAP), value, 0.0)
        return (jnp.sum(keep, axis=1 - axis, keepdims=True) - 1.0).astype(i32)

    place_col, place_row = cells_of(0), cells_of(1)
    cells = lax.broadcasted_iota(i32, (PART, CELLS), 1)
    for at in range(0, SLOTS, PART):
        pick = (place_col[at : at + PART] == cells).astype(f32).astype(bf16)
        g_arrived[at : at + PART, :] = dot(pick, g_grid[...], ((1,), (0,))).astype(bf16)
    keep_back = pltpu.make_async_copy(block(g_arrived, me), block(returned, me), local_sem.at[2])
    keep_back.start()

    def send_back(step, carry):
        chip, device = place.peer(step)
        cross(block(g_arrived, chip), block(returned, me), BACK, device).start()
        return carry

    lax.fori_loop(1, CHIPS, send_back, 0)

    all_data = cross(outgoing.at[some], arrived.at[some], DATA, place.sibling)
    all_data.wait_recv()
    keep.wait()

    def bin_rows(i, carry):
        index = lax.broadcasted_iota(i32, (PART, SLOTS), 0) + i * PART
        pick = (index == place_row).astype(f32).astype(bf16)
        cells_here = dot(pick, arrived[...], ((1,), (0,)))
        grid_ext[pl.ds(1 + 2 * i, 2)] = cells_here.astype(bf16).reshape(2, CLON, C)
        keep_ends(ends, 2 * i, cells_here)
        return carry

    lax.fori_loop(0, CELLS // PART, bin_rows, 0)
    edge_columns(ends, cols_x)
    halo_x.start()

    def conv_rows(low, high, chunk, sums):
        lanes = slice(chunk * CHUNK, (chunk + 1) * CHUNK)

        def one(i, sums):
            three = [grid_ext[i + a, :, lanes].astype(f32) for a in range(3)]
            acc = conv_part(three, 0.0, 0.0, lambda k: w_depth[k : k + 1, lanes])
            at = pl.ds(pl.multiple_of(i * CLON, CLON), CLON)
            mixed[at, lanes] = acc.astype(bf16)
            ends[0, i, 0:1, lanes] = acc[0:1]
            ends[1, i, 0:1, lanes] = acc[CLON - 1 : CLON]
            middle = gm_ext[i + 1, :, lanes].astype(f32)
            index = lax.broadcasted_iota(i32, (CLON, CHUNK), 0)
            shifted = [
                jnp.where(index == CLON - 1, 0.0, pltpu.roll(middle, CLON - 1, 0)),
                middle,
                jnp.where(index == 0, 0.0, pltpu.roll(middle, 1, 0)),
            ]
            return tuple(
                sums[3 * a + b] + jnp.sum((shifted[b] * three[a]).reshape(16, 8, CHUNK), axis=0)
                for a in range(3)
                for b in range(3)
            )

        return lax.fori_loop(low, high, one, sums)

    for chunk in range(C // CHUNK):
        sums = conv_rows(1, CLAT - 1, chunk, tuple(jnp.zeros((8, CHUNK), f32) for _ in range(9)))
        for k in range(9):
            depth_sums[chunk, k] = sums[k]
    halo_x.wait()
    side_columns(to_cols_x, to_diag_x, west, east)
    for chunk in range(C // CHUNK):
        lanes = slice(chunk * CHUNK, (chunk + 1) * CHUNK)
        sums = conv_rows(0, 1, chunk, tuple(depth_sums[chunk, k] for k in range(9)))
        sums = conv_rows(CLAT - 1, CLAT, chunk, sums)
        for k, (a, b) in enumerate(offsets):
            total = jnp.sum(sums[k], axis=0, keepdims=True)
            if b:
                side = (west if b < 0 else east)[1 + a : 1 + a + CLAT, lanes]
                edge = cols[0 if b < 0 else 1, :, lanes].astype(f32)
                total = total + jnp.sum(side * edge, axis=0, keepdims=True)
            parts[DEPTH + k : DEPTH + k + 1, lanes] = total

    index = lax.broadcasted_iota(i32, (16, C), 0)
    for side, beside in enumerate(side_totals(west, east, lambda k: w_depth[k : k + 1, :])):
        for i in range(CLAT):
            at = i * CLON + side * (CLON - 16)
            whole = (ends[side, i, 0:1, :] + beside[i : i + 1]).astype(bf16).astype(f32)
            old = mixed[at : at + 16, :].astype(f32)
            mixed[at : at + 16, :] = jnp.where(index == 15 * side, whole, old).astype(bf16)
    parts[SPEC:DEPTH, :] = jnp.zeros((DEPTH - SPEC, C), f32)
    parts[DEPTH + 9 : ROWS_IN, :] = jnp.zeros((ROWS_IN - DEPTH - 9, C), f32)

    lines = {IN: lines_in, OUT: lines_out, POINT: lines_point}
    quarter = {IN: quarter_in, OUT: quarter_out, POINT: quarter_point}
    gathers = {IN: gather_in, OUT: gather_out, POINT: gather_point}

    def half_of(r, which):
        return pl.ds(pl.multiple_of(r.first + which * r.half, 16), r.half)

    def local_half(r):
        return pl.ds(r.base, r.half)

    def swap_halves(r):
        swap_out[local_half(r), :] = parts[half_of(r, 1 - core), :].astype(bf16)
        copy = cross(swap_out.at[local_half(r)], swap_in.at[local_half(r)], r.sems[0], place.sibling)
        copy.start()
        return copy

    def rows_at(start, size):
        return pl.ds(pl.multiple_of(start, 16), size)

    def send_line(r):
        here = local_half(r)
        chip_sum[here, :] = (
            parts[half_of(r, core), :] + swap_in[here, :].astype(f32)
        ).astype(bf16)
        at, device = r.line(place)
        for step in range(1, 4):
            q = (at + step) % 4
            src = chip_sum.at[rows_at(r.base + q * r.quarter, r.quarter)]
            cross(src, lines[r].at[at], r.sems[1], device(q)).start()

    def piece(r, start, index):
        rows_here = rows_at(start + index // r.across * 16, 16)
        return rows_here, pl.ds(pl.multiple_of(index % r.across * r.width, 128), r.width)

    def waiting(r, size, sem):
        some = gathers[r].at[pl.ds(0, size)]
        return cross(some, some, r.sems[sem], place.sibling)

    def waiting_line(r, sem):
        some = lines[r].at[pl.ds(0, 3)]
        return cross(some, some, r.sems[sem], place.sibling)

    def send_plane(r):
        waiting_line(r, 1).wait_recv()
        at, _ = r.line(place)
        total = chip_sum[rows_at(r.base + at * r.quarter, r.quarter), :].astype(f32)
        for step in range(1, 4):
            total = total + lines[r][(at + step) % 4].astype(f32)
        quarter[r][...] = total.astype(bf16)
        me_here, device = r.plane(place)

        def send(step, carry):
            index = (me_here + step) % 16

            @pl.when(index < r.count)
            def _():
                where = piece(r, 0, index)
                cross(quarter[r].at[where], gathers[r].at[me_here], r.sems[2], device(index)).start()

            return carry

        lax.fori_loop(1, 16, send, 0)

    def result_rows(r):
        return r.first + core * r.half + r.line(place)[0] * r.quarter

    def share_plane(r):
        me_here, device = r.plane(place)

        @pl.when(me_here < r.count)
        def _():
            waiting(r, 15, 2).wait_recv()
            total = quarter[r][piece(r, 0, me_here)].astype(f32)
            for step in range(1, 16):
                total = total + gathers[r][(me_here + step) % 16].astype(f32)
            where = piece(r, result_rows(r), me_here)
            result[where] = total.astype(bf16)

            def share(step, carry):
                index = (me_here + step) % 16
                cross(result.at[where], result.at[where], r.sems[3], device(index)).start()
                return carry

            lax.fori_loop(1, 16, share, 0)

    def share_line(r):
        me_here, _ = r.plane(place)
        if r.count == 16:
            waiting(r, 15, 3).wait_recv()
        else:
            pl.when(me_here < r.count)(lambda: waiting(r, r.count - 1, 3).wait_recv())
            pl.when(me_here >= r.count)(lambda: waiting(r, r.count, 3).wait_recv())
        at, device = r.line(place)
        here = result.at[rows_at(result_rows(r), r.quarter)]
        for step in range(1, 4):
            cross(here, here, r.sems[4], device((at + step) % 4)).start()

    def last_swap(r):
        waiting_line(r, 4).wait_recv()
        half = result.at[half_of(r, core)]
        copy = cross(half, half, r.sems[5], place.sibling)
        copy.start()
        return copy

    def sent(r):
        waiting_line(r, 1).wait_send()
        waiting_line(r, 4).wait_send()
        me_here, _ = r.plane(place)

        def owner():
            waiting(r, r.count - 1, 2).wait_send()
            waiting(r, 15, 3).wait_send()

        if r.count == 16:
            owner()
        else:
            pl.when(me_here < r.count)(owner)
            pl.when(me_here >= r.count)(lambda: waiting(r, r.count, 2).wait_send())

    def point(i):
        at = slice(i * 512, (i + 1) * 512)
        here = grid_ext[1 + 4 * i : 5 + 4 * i].astype(f32).reshape(512, C)
        latent_here[at, :] = (here + dot(mixed[at, :], w_point[...], ((1,), (0,)))).astype(bf16)


    keep_back.wait()
    all_back = cross(g_arrived.at[some], returned.at[some], BACK, place.sibling)
    all_back.wait_recv()

    def gathered(info, which):
        about = info[:, C:].astype(f32)
        slot = about[:, 24:25] * SLOT + about[:, 25:26] + (CAP * which).astype(f32)
        key = jnp.where(about[:, 26:27] == core.astype(f32), slot, -1.0)
        total = jnp.zeros((OBS, C), f32)
        for at in range(0, SLOTS, 512):
            index = (lax.broadcasted_iota(i32, (OBS, 512), 1) + at).astype(f32)
            pick = (index == key).astype(f32).astype(bf16)
            total = total + dot(pick, returned[at : at + 512, :], ((1,), (0,)))
        return total

    part[...] = gathered(emb_sib, 1 - core).astype(bf16)
    swap = cross(part, part_sib, SIB_PART, place.sibling)
    swap.start()
    parts[POINT.first : PARTS, :] = dot(mixed[...], cot[...], ((0,), (0,)))
    point_swap = swap_halves(POINT)
    own = gathered(emb, core)
    swap.wait()
    g_emb[...] = (own + part_sib[...].astype(f32)).astype(bf16)
    parts[OUT.first : OUT.first + C, :] = dot(hidden[...], g_emb[...], ((0,), (0,)))
    out_swap = swap_halves(OUT)
    g_hidden = dot(g_emb[...], w_out[...], ((1,), (1,)))
    pre = preact[...]
    sig = 1.0 / (1.0 + jnp.exp(-pre))
    g_pre = (g_hidden * sig * (1.0 + pre * (1.0 - sig))).astype(bf16)
    parts[0:SPEC, :] = dot(spec_t[...], g_pre, ((1,), (0,)))
    in_swap = swap_halves(IN)
    point_swap.wait()
    send_line(POINT)
    out_swap.wait()
    send_line(OUT)
    in_swap.wait()
    send_line(IN)
    point(0)
    send_plane(POINT)
    send_plane(OUT)
    send_plane(IN)
    point(1)
    share_plane(POINT)
    share_plane(OUT)
    share_plane(IN)
    point(2)
    share_line(POINT)
    share_line(OUT)
    share_line(IN)
    point(3)
    store = pltpu.make_async_copy(latent_here, latent, local_sem.at[6])
    store.start()
    rounds = (POINT, OUT, IN)

    def leave(r, which, index):
        half = half_of(r, which)
        return pltpu.make_async_copy(result.at[half], sums_out.at[half], out_sem.at[index])

    last, leaving = [], []
    for i, r in enumerate(rounds):
        last.append(last_swap(r))
        leaving.append(leave(r, core, i))
        leaving[-1].start()
    for r in rounds:
        sent(r)
    store.wait()
    for copy in (lat_marks, lon_marks, all_data, all_back):
        copy.wait_send()
    for i, r in enumerate(rounds):
        last[i].wait()
        leaving.append(leave(r, 1 - core, 3 + i))
        leaving[-1].start()
    for copy in leaving:
        copy.wait()


def run(spec_t, owner, cell, w_in, w_out, w_point, w_depth, cot):
    dma = pltpu.SemaphoreType.DMA
    anywhere = pl.BlockSpec(memory_space=pl.ANY)
    field = VMEM((CLAT + 2, CLON, C), bf16)
    half = VMEM((PARTS // 2, C), bf16)
    return pl.pallas_call(
        kernel,
        out_shape=[
            pltpu.VMEM((CELLS, C), bf16),
            pltpu.VMEM((PARTS, C), bf16),
        ],
        in_specs=[anywhere, vmem(), vmem(), anywhere, anywhere, anywhere, vmem(), anywhere],
        out_specs=[anywhere, anywhere],
        scratch_shapes=[
            VMEM((SPEC, OBS), bf16),
            VMEM((SPEC, C), bf16),
            VMEM((C, C), bf16),
            VMEM((C, C), bf16),
            VMEM((CELLS, C), bf16),
            VMEM((OBS, C), f32),
            VMEM((OBS, C), bf16),
            VMEM((OBS, C + META), bf16),
            VMEM((OBS, C + META), bf16),
            VMEM((8, OBS), i32),
            VMEM((8, OBS), i32),
            VMEM((SLOTS, C), bf16),
            VMEM((SLOTS, C), bf16),
            VMEM((N_LAT, N_LON, META), f32),
            VMEM((N_LAT, N_LON, META), f32),
            VMEM((N_LON, N_LAT, META), f32),
            VMEM((N_LON, N_LAT, META), f32),
            field,
            field,
            VMEM((2, CLAT, C), bf16),
            VMEM((2, CLAT, C), bf16),
            VMEM((4, CLAT, C), bf16),
            VMEM((2, CLAT, C), bf16),
            VMEM((2, CLAT, C), bf16),
            VMEM((4, CLAT, C), bf16),
            VMEM((24, C), f32),
            VMEM((24, C), f32),
            VMEM((2, CLAT, 8, C), f32),
            VMEM((2, CLAT, 8, C), f32),
            VMEM((C // CHUNK, 9, 8, CHUNK), f32),
            VMEM((CELLS, C), bf16),
            VMEM((SLOTS, C), bf16),
            VMEM((SLOTS, C), bf16),
            VMEM((OBS, C), bf16),
            VMEM((OBS, C), bf16),
            VMEM((OBS, C), bf16),
            VMEM((CELLS, C), bf16),
            VMEM((PARTS, C), f32),
            half,
            half,
            half,
        ]
        + [VMEM((4, r.quarter, C), bf16) for r in (IN, OUT, POINT)]
        + [VMEM((r.quarter, C), bf16) for r in (IN, OUT, POINT)]
        + [VMEM((16, 16, r.width), bf16) for r in (IN, OUT, POINT)]
        + [
            VMEM((CELLS, C), bf16),
            VMEM((PARTS, C), bf16),
            dma((6,)),
            dma((5,)),
            dma((7,)),
            dma((SEMS,)),
            dma((SEMS,)),
            dma((2, 8)),
            dma((2, 8)),
        ],
        compiler_params=pltpu.CompilerParams(
            collective_id=0, has_side_effects=True, vmem_limit_bytes=51 << 20
        ),
    )(spec_t, owner, cell, w_in, w_out, w_point, w_depth, cot)


def finish_kernel(latent_in, total, latent, g_in, g_out, g_point, g_depth, in_f, out_f, point_f, sem):
    obs_scale = 1.0 / math.sqrt(OBS * N_LAT * N_LON)
    cell_scale = 1.0 / math.sqrt(CELLS * N_LAT * N_LON)
    copies = [pltpu.make_async_copy(latent_in, latent, sem.at[3])]
    copies[0].start()
    plan = (
        (in_f, g_in, IN.first, obs_scale),
        (out_f, g_out, OUT.first, obs_scale),
        (point_f, g_point, POINT.first, cell_scale),
    )
    for i, (values, target, first, scale) in enumerate(plan):
        values[...] = total[first : first + values.shape[0], :].astype(f32) * scale
        copies.append(pltpu.make_async_copy(values, target, sem.at[i]))
        copies[-1].start()
    g_depth[...] = total[DEPTH : DEPTH + 16, :].astype(f32)[0:9] * cell_scale
    for copy in copies:
        copy.wait()


def finish(latent, total):
    anywhere = pl.BlockSpec(memory_space=pl.ANY)
    shapes = [(SPEC, C), (C, C), (C, C), (9, C)]
    return pl.pallas_call(
        finish_kernel,
        out_shape=[jax.ShapeDtypeStruct((CELLS, C), bf16)]
        + [jax.ShapeDtypeStruct(shape, f32) for shape in shapes],
        in_specs=[vmem(), vmem()],
        out_specs=[anywhere] * 4 + [vmem()],
        scratch_shapes=[VMEM(shape, f32) for shape in shapes[:3]] + [pltpu.SemaphoreType.DMA((4,))],
        compiler_params=pltpu.CompilerParams(vmem_limit_bytes=12 << 20),
    )(latent, total)


def on_device(spectra, owner, cell, w_in, w_out, w_point, w_depth, cotangent):
    latent, total = run(
        spectra.T,
        owner.reshape(1, OBS),
        cell.reshape(1, OBS),
        w_in,
        w_out,
        w_point,
        w_depth,
        cotangent.reshape(CELLS, C),
    )
    latent, *grads = finish(latent, total)
    return (latent.reshape(CLAT, CLON, C), *grads)


def solution(mesh):
    in_specs = (
        P(("lat", "lon"), None),
        P(("lat", "lon"), None),
        P(("lat", "lon")),
        P(),
        P(),
        P(),
        P(),
        P("lat", "lon", None),
    )
    out_specs = (P("lat", "lon", None), P(), P(), P(), P())
    return jax.shard_map(
        on_device, mesh=mesh, in_specs=in_specs, out_specs=out_specs, check_vma=False
    )
```

```python
import math

import jax
import jax.numpy as jnp
from jax import lax
from jax.experimental import pallas as pl
from jax.experimental.pallas import tpu as pltpu
from jax.sharding import PartitionSpec as P

offsets = [(a, b) for a in (-1, 0, 1) for b in (-1, 0, 1)]
f32, bf16, i32 = jnp.float32, jnp.bfloat16, jnp.int32

N_LAT, N_LON, SIDE = 8, 16, 4
CHIPS = N_LAT // 2 * N_LON
CAP = 8
SLOT = 2 * CAP
SLOTS = CHIPS * SLOT
OBS = 512
C = 512
CLAT, CLON = 16, 128
CELLS = CLAT * CLON
SPEC = 616
META = 128
ROWS_IN = 640
PART = 256
CHUNK = 128

VMEM = pltpu.VMEM


def vmem():
    return pl.BlockSpec(memory_space=pltpu.VMEM)


def dot(a, b, dims):
    return lax.dot_general(a, b, (dims, ((), ())), preferred_element_type=f32)


class Place:
    def __init__(self):
        self.lat = lax.axis_index("lat")
        self.lon = lax.axis_index("lon")
        self.core = self.lat % 2
        self.x = self.lat // 2
        self.chip = self.x * N_LON + self.lon
        self.sibling = (self.x * 2 + 1 - self.core, self.lon)

    def peer(self, step):
        step = (step * 37) % CHIPS
        x = (self.x + step // N_LON) % (N_LAT // 2)
        z = (self.lon // SIDE + step // SIDE) % SIDE
        y = (self.lon + step) % SIDE
        lon = z * SIDE + y
        return x * N_LON + lon, (x * 2 + self.core, lon)

    def of_chip(self, chip):
        return (chip // N_LON * 2 + self.core, chip % N_LON)


def remote(src, dst, send, recv, device):
    return pltpu.make_async_remote_copy(
        src_ref=src,
        dst_ref=dst,
        send_sem=send,
        recv_sem=recv,
        device_id=device,
        device_id_type=pl.DeviceIdType.MESH,
    )


def greet(place):
    barrier = pltpu.get_barrier_semaphore()

    def hello(device):
        pl.semaphore_signal(
            barrier, inc=1, device_id=device, device_id_type=pl.DeviceIdType.MESH
        )

    def one(step, carry):
        hello(place.peer(step)[1])
        return carry

    lax.fori_loop(1, CHIPS, one, 0)
    others = N_LAT // 2
    for x in range(others):
        hello((2 * x + 1 - place.core, place.lon))
    for side in (-1, 1):
        inside = (place.lat + side >= 0) & (place.lat + side < N_LAT)

        @pl.when(inside)
        def _(side=side):
            for turn in (-1, 1):
                hello((place.lat + side, (place.lon + turn + N_LON) % N_LON))

    edges = (place.lat > 0).astype(i32) + (place.lat < N_LAT - 1).astype(i32)
    return barrier, CHIPS - 1 + others + 2 * edges


class Halo:
    def __init__(self, place, ext, cols, to_cols, to_diag, send, recv):
        self.place = place
        self.ext, self.to_diag = ext, to_diag
        lat, lon = place.lat, place.lon
        east, west = (lon + 1) % N_LON, (lon + N_LON - 1) % N_LON
        has_north, has_south = lat > 0, lat < N_LAT - 1
        south, north = jnp.minimum(lat + 1, N_LAT - 1), jnp.maximum(lat - 1, 0)
        plan = [
            (ext.at[CLAT], ext.at[0], (south, lon), has_south, has_north),
            (ext.at[1], ext.at[CLAT + 1], (north, lon), has_north, has_south),
            (cols.at[1], to_cols.at[0], (lat, east), None, None),
            (cols.at[0], to_cols.at[1], (lat, west), None, None),
            (cols.at[1], to_diag.at[0], (south, east), has_south, has_north),
            (cols.at[0], to_diag.at[1], (south, west), has_south, has_north),
            (cols.at[1], to_diag.at[2], (north, east), has_north, has_south),
            (cols.at[0], to_diag.at[3], (north, west), has_north, has_south),
        ]
        self.plan = [
            (remote(src, dst, send.at[i], recv.at[i], device), sends, receives)
            for i, (src, dst, device, sends, receives) in enumerate(plan)
        ]

    def start(self):
        for copy, sends, _ in self.plan:
            if sends is None:
                copy.start()
            else:
                pl.when(sends)(copy.start)

    def wait(self):
        for copy, sends, receives in self.plan:
            if sends is None:
                copy.wait_send()
                copy.wait_recv()
            else:
                pl.when(sends)(copy.wait_send)
                pl.when(receives)(copy.wait_recv)

    def clear_outside(self):
        @pl.when(self.place.lat == 0)
        def _():
            self.ext[0] = jnp.zeros((CLON, C), bf16)
            self.to_diag[0] = jnp.zeros((CLAT, C), bf16)
            self.to_diag[1] = jnp.zeros((CLAT, C), bf16)

        @pl.when(self.place.lat == N_LAT - 1)
        def _():
            self.ext[CLAT + 1] = jnp.zeros((CLON, C), bf16)
            self.to_diag[2] = jnp.zeros((CLAT, C), bf16)
            self.to_diag[3] = jnp.zeros((CLAT, C), bf16)


def vector_encode(spec_t, owner, cell, w_in, w_out, preact, hidden, emb, route, table):
    pre = dot(spec_t[...], w_in[...], ((0,), (0,)))
    preact[...] = pre
    hid = (pre * (1.0 / (1.0 + jnp.exp(-pre)))).astype(bf16)
    hidden[...] = hid
    emb[:, :C] = dot(hid, w_out[...], ((1,), (0,))).astype(bf16)
    places = cell[...]
    values = jnp.concatenate(
        [owner[...], places // 16, places % 16, jnp.zeros((13, OBS), i32)], axis=0
    ).astype(f32).astype(bf16)
    down = lax.broadcasted_iota(i32, (OBS, OBS), 0)
    across = lax.broadcasted_iota(i32, (OBS, OBS), 1)
    eye = (down == across).astype(f32).astype(bf16)
    columns = dot(eye, values, ((1,), (1,)))
    tile_col, high_col, low_col = columns[:, 0:1], columns[:, 1:2], columns[:, 2:3]
    tile_row = values[0:1, :].astype(f32)
    tiles = N_LAT * N_LON
    hits = (tile_col == lax.broadcasted_iota(i32, (OBS, tiles), 1).astype(f32)).astype(f32)
    lower = (across <= down).astype(f32).astype(bf16)
    count = dot(lower, hits.astype(bf16), ((1,), (0,)))
    pos_col = (jnp.sum(count * hits, axis=1, keepdims=True) - 1.0).astype(i32)
    hits_t = (tile_row == lax.broadcasted_iota(i32, (tiles, OBS), 0).astype(f32)).astype(f32)
    upper = (down <= across).astype(f32).astype(bf16)
    count_t = dot(hits_t.astype(bf16), upper, ((1,), (0,)))
    pos_row = (jnp.sum(count_t * hits_t, axis=0, keepdims=True) - 1.0).astype(i32)
    lane = lax.broadcasted_iota(i32, (OBS, META), 1)
    kind = lane // CAP
    value = jnp.where(kind == 0, high_col, jnp.where(kind == 1, low_col, 1.0))
    keep = (lane % CAP == pos_col) & (kind < 3)
    emb[:, C:] = jnp.where(keep, value, 0.0).astype(bf16)
    table[...] = dot(hits_t.astype(bf16), emb[:, C:], ((1,), (0,))).reshape(N_LAT, N_LON, META)
    tile = tile_row.astype(i32)
    lat, lon = tile // N_LON, tile % N_LON
    chip = lat // 2 * N_LON + lon
    route[...] = jnp.concatenate(
        [chip * SLOT + pos_row, lat % 2, chip, jnp.zeros((5, OBS), i32)], axis=0
    )


def slot_keys(route, mine, core):
    return jnp.where(route[1:2, :] == mine, route[0:1, :] + CAP * core, -1)


class Round:
    def __init__(self, number, axis, first, quarter, width):
        self.axis, self.first, self.quarter, self.width = axis, first, quarter, width
        self.half = 4 * quarter
        self.base = first // 2
        self.across = C // width
        self.count = quarter // 16 * self.across
        self.sems = range(7 + 6 * number, 13 + 6 * number)

    def line(self, place):
        x, z, y, core = place.x, place.lon // SIDE, place.lon % SIDE, place.core
        if self.axis == "x":
            return x, lambda q: (2 * q + core, place.lon)
        if self.axis == "y":
            return y, lambda q: (place.lat, z * SIDE + q)
        return z, lambda q: (place.lat, q * SIDE + y)

    def plane(self, place):
        x, z, y, core = place.x, place.lon // SIDE, place.lon % SIDE, place.core
        if self.axis == "x":
            return place.lon, lambda m: (place.lat, m)
        if self.axis == "y":
            return x * SIDE + z, lambda m: (2 * (m // SIDE) + core, m % SIDE * SIDE + y)
        return x * SIDE + y, lambda m: (2 * (m // SIDE) + core, z * SIDE + m % SIDE)


IN = Round(0, "z", 0, 80, 256)
OUT = Round(1, "y", 640, 64, 128)
POINT = Round(2, "x", 1152, 64, 128)
PARTS = 1664
DEPTH = 624

SIB_EMB, SIB_ROUTE, MARK_LAT, MARK_LON, DATA, BACK, SIB_PART = range(7)
SEMS = 7 + 18


def block(ref, chip, size=SLOT):
    return ref.at[pl.ds(pl.multiple_of(chip * size, size), size)]


def keep_ends(ends, row, values):
    for r in range(values.shape[0] // CLON):
        at = r * CLON
        ends[0, row + r, 0:1, :] = values[at : at + 1]
        ends[1, row + r, 0:1, :] = values[at + CLON - 1 : at + CLON]


def edge_columns(ends, cols):
    for side in range(2):
        cols[side] = ends[side, :, 0, :].astype(bf16)


def side_columns(to_cols, to_diag, west, east):
    for side, (into, above, below) in enumerate(((west, 0, 2), (east, 1, 3))):
        into[0:1, :] = to_diag[above].astype(f32)[CLAT - 1 : CLAT]
        into[1 : CLAT + 1, :] = to_cols[side].astype(f32)
        into[CLAT + 1 : CLAT + 2, :] = to_diag[below].astype(f32)[0:1]


def side_sums(west, east, weight, sides):
    for side, ref in ((0, west), (1, east)):
        b = 2 * side
        total = (
            weight(b) * ref[0:CLAT, :]
            + weight(3 + b) * ref[1 : CLAT + 1, :]
            + weight(6 + b) * ref[2 : CLAT + 2, :]
        )
        for i in range(CLAT):
            sides[side, i, 0:1, :] = total[i : i + 1, :]


def conv_part(rows, first, last, weight):
    columns = [
        weight(b) * rows[0] + weight(3 + b) * rows[1] + weight(6 + b) * rows[2] for b in range(3)
    ]
    index = lax.broadcasted_iota(i32, (CLON, CHUNK), 0)
    left = jnp.where(index == 0, first, pltpu.roll(columns[0], 1, 0))
    right = jnp.where(index == CLON - 1, last, pltpu.roll(columns[2], CLON - 1, 0))
    return columns[1] + left + right


def kernel(
    spec_in,
    owner,
    cell,
    w_in_in,
    w_out_in,
    w_point_in,
    w_depth,
    cot_in,
    latent,
    sums_out,
    spec_t,
    w_in,
    w_out,
    w_point,
    cot,
    preact,
    hidden,
    emb,
    emb_sib,
    route,
    route_sib,
    outgoing,
    arrived,
    table,
    table_lat,
    marks,
    places,
    gm_ext,
    grid_ext,
    cols,
    to_cols,
    to_diag,
    cols_x,
    to_cols_x,
    to_diag_x,
    west,
    east,
    sides,
    ends,
    depth_sums,
    g_grid,
    g_arrived,
    returned,
    part,
    part_sib,
    g_emb,
    mixed,
    parts,
    swap_out,
    swap_in,
    chip_sum,
    lines_in,
    lines_out,
    lines_point,
    quarter_in,
    quarter_out,
    quarter_point,
    gather_in,
    gather_out,
    gather_point,
    latent_here,
    result,
    out_sem,
    load_sem,
    local_sem,
    send_sem,
    recv_sem,
    halo_send,
    halo_recv,
):
    place = Place()
    core, me = place.core, place.chip
    loads = [
        pltpu.make_async_copy(src, dst, load_sem.at[i])
        for i, (src, dst) in enumerate(
            (
                (spec_in, spec_t),
                (w_in_in, w_in),
                (w_out_in, w_out),
                (w_point_in, w_point),
                (cot_in, cot),
            )
        )
    ]
    for copy in loads[:3]:
        copy.start()
    barrier, count = greet(place)

    def cross(src, dst, index, device):
        return remote(src, dst, send_sem.at[index], recv_sem.at[index], device)

    halo_g = Halo(place, gm_ext, cols, to_cols, to_diag, halo_send.at[0], halo_recv.at[0])
    halo_x = Halo(place, grid_ext, cols_x, to_cols_x, to_diag_x, halo_send.at[1], halo_recv.at[1])
    halo_g.clear_outside()
    halo_x.clear_outside()
    for copy in loads[:3]:
        copy.wait()
    for copy in loads[3:]:
        copy.start()
    vector_encode(spec_t, owner, cell, w_in, w_out, preact, hidden, emb, route, table)
    pl.semaphore_wait(barrier, count)

    swaps = [
        cross(emb, emb_sib, SIB_EMB, place.sibling),
        cross(route, route_sib, SIB_ROUTE, place.sibling),
    ]
    for copy in swaps:
        copy.start()
    keep_lat = pltpu.make_async_copy(
        table.at[place.lat], table_lat.at[place.lat], local_sem.at[5]
    )
    keep_lat.start()
    for step in range(1, N_LAT):
        lat = (place.lat + step) % N_LAT
        cross(table.at[lat], table_lat.at[place.lat], MARK_LAT, (lat, place.lon)).start()
    def spread(key, values, more):
        def one(i, carry):
            at = pl.multiple_of(i * PART, PART)
            index = lax.broadcasted_iota(i32, (PART, OBS), 0) + at
            pick = (index == key).astype(f32).astype(bf16)
            new = dot(pick, values[:, :C], ((1,), (0,)))
            if more:
                new = new + outgoing[pl.ds(at, PART), :].astype(f32)
            outgoing[pl.ds(at, PART), :] = new.astype(bf16)
            return carry

        lax.fori_loop(0, SLOTS // PART, one, 0)

    spread(slot_keys(route[...], core, core), emb, False)
    for copy in loads[3:]:
        copy.wait()

    def mix_back(i, carry):
        rows4 = cot[pl.ds(pl.multiple_of(i * 512, 512), 512), :]
        gm = dot(rows4, w_point[...], ((1,), (1,)))
        gm_ext[pl.ds(1 + 4 * i, 4)] = gm.astype(bf16).reshape(4, CLON, C)
        keep_ends(ends, 4 * i, gm)
        return carry

    lax.fori_loop(0, CLAT // 4, mix_back, 0)
    edge_columns(ends, cols)
    halo_g.start()
    keep_lat.wait()
    lat_row = pl.ds(0, N_LAT - 1)
    lat_marks = cross(table.at[lat_row], table_lat.at[lat_row], MARK_LAT, place.sibling)
    lat_marks.wait_recv()
    for lon in range(N_LON):
        marks[lon] = table_lat[:, lon, :]
    keep_lon = pltpu.make_async_copy(marks.at[place.lon], places.at[place.lon], local_sem.at[0])
    keep_lon.start()
    for step in range(1, N_LON):
        lon = (place.lon + step) % N_LON
        cross(marks.at[lon], places.at[place.lon], MARK_LON, (place.lat, lon)).start()
    for copy in swaps:
        copy.wait()
    spread(slot_keys(route_sib[...], core, 1 - core), emb_sib, True)
    keep = pltpu.make_async_copy(block(outgoing, me), block(arrived, me), local_sem.at[1])
    keep.start()

    def send_data(step, carry):
        chip, device = place.peer(step)
        cross(block(outgoing, chip), block(arrived, me), DATA, device).start()
        return carry

    lax.fori_loop(1, CHIPS, send_data, 0)
    some = pl.ds(0, (CHIPS - 1) * SLOT)
    few = pl.ds(0, CHIPS - 1)

    halo_g.wait()
    side_columns(to_cols, to_diag, west, east)
    side_sums(west, east, lambda k: w_depth[8 - k : 9 - k, :], sides)

    def conv_back(i, carry):
        for chunk in range(C // CHUNK):
            lanes = slice(chunk * CHUNK, (chunk + 1) * CHUNK)
            three = [gm_ext[i + a, :, lanes].astype(f32) for a in range(3)]
            first, last = sides[0, i, 0:1, lanes], sides[1, i, 0:1, lanes]
            acc = conv_part(three, first, last, lambda k: w_depth[8 - k : 9 - k, lanes])
            at = pl.ds(pl.multiple_of(i * CLON, CLON), CLON)
            g_grid[at, lanes] = (cot[at, lanes].astype(f32) + acc).astype(bf16)
        return carry

    lax.fori_loop(0, CLAT, conv_back, 0)

    keep_lon.wait()
    lon_row = pl.ds(0, N_LON - 1)
    lon_marks = cross(marks.at[lon_row], places.at[lon_row], MARK_LON, place.sibling)
    lon_marks.wait_recv()
    tiles = N_LAT * N_LON
    known = places[...].reshape(tiles, META).astype(bf16)

    def sender(slot):
        chip = slot // SLOT
        return chip % N_LON * N_LAT + chip // N_LON * 2 + slot // CAP % 2

    def cells_of(axis):
        shape = (SLOTS, tiles) if axis == 0 else (tiles, SLOTS)
        slot = lax.broadcasted_iota(i32, shape, axis)
        other = lax.broadcasted_iota(i32, shape, 1 - axis)
        expand = (sender(slot) == other).astype(f32).astype(bf16)
        if axis == 0:
            wide = dot(expand, known, ((1,), (0,)))
        else:
            wide = dot(known, expand, ((0,), (0,)))
        value = jnp.where(other < CAP, 16.0, 1.0) * wide
        keep = jnp.where(other % CAP == slot % CAP, value, 0.0)
        return (jnp.sum(keep, axis=1 - axis, keepdims=True) - 1.0).astype(i32)

    place_col, place_row = cells_of(0), cells_of(1)
    cells = lax.broadcasted_iota(i32, (PART, CELLS), 1)
    for at in range(0, SLOTS, PART):
        pick = (place_col[at : at + PART] == cells).astype(f32).astype(bf16)
        g_arrived[at : at + PART, :] = dot(pick, g_grid[...], ((1,), (0,))).astype(bf16)
    keep_back = pltpu.make_async_copy(block(g_arrived, me), block(returned, me), local_sem.at[2])
    keep_back.start()

    def send_back(step, carry):
        chip, device = place.peer(step)
        cross(block(g_arrived, chip), block(returned, me), BACK, device).start()
        return carry

    lax.fori_loop(1, CHIPS, send_back, 0)

    all_data = cross(outgoing.at[some], arrived.at[some], DATA, place.sibling)
    all_data.wait_recv()
    keep.wait()

    def bin_rows(i, carry):
        index = lax.broadcasted_iota(i32, (PART, SLOTS), 0) + i * PART
        pick = (index == place_row).astype(f32).astype(bf16)
        cells_here = dot(pick, arrived[...], ((1,), (0,)))
        grid_ext[pl.ds(1 + 2 * i, 2)] = cells_here.astype(bf16).reshape(2, CLON, C)
        keep_ends(ends, 2 * i, cells_here)
        return carry

    lax.fori_loop(0, CELLS // PART, bin_rows, 0)
    edge_columns(ends, cols_x)
    halo_x.start()

    def conv_rows(low, high, chunk, sums):
        lanes = slice(chunk * CHUNK, (chunk + 1) * CHUNK)

        def one(i, sums):
            three = [grid_ext[i + a, :, lanes].astype(f32) for a in range(3)]
            acc = conv_part(three, 0.0, 0.0, lambda k: w_depth[k : k + 1, lanes])
            at = pl.ds(pl.multiple_of(i * CLON, CLON), CLON)
            mixed[at, lanes] = acc.astype(bf16)
            ends[0, i, 0:1, lanes] = acc[0:1]
            ends[1, i, 0:1, lanes] = acc[CLON - 1 : CLON]
            middle = gm_ext[i + 1, :, lanes].astype(f32)
            index = lax.broadcasted_iota(i32, (CLON, CHUNK), 0)
            shifted = [
                jnp.where(index == CLON - 1, 0.0, pltpu.roll(middle, CLON - 1, 0)),
                middle,
                jnp.where(index == 0, 0.0, pltpu.roll(middle, 1, 0)),
            ]
            return tuple(
                sums[3 * a + b] + jnp.sum((shifted[b] * three[a]).reshape(16, 8, CHUNK), axis=0)
                for a in range(3)
                for b in range(3)
            )

        return lax.fori_loop(low, high, one, sums)

    for chunk in range(C // CHUNK):
        sums = conv_rows(1, CLAT - 1, chunk, tuple(jnp.zeros((8, CHUNK), f32) for _ in range(9)))
        for k in range(9):
            depth_sums[chunk, k] = sums[k]
    halo_x.wait()
    side_columns(to_cols_x, to_diag_x, west, east)
    side_sums(west, east, lambda k: w_depth[k : k + 1, :], sides)
    for chunk in range(C // CHUNK):
        lanes = slice(chunk * CHUNK, (chunk + 1) * CHUNK)
        sums = conv_rows(0, 1, chunk, tuple(depth_sums[chunk, k] for k in range(9)))
        sums = conv_rows(CLAT - 1, CLAT, chunk, sums)
        for k, (a, b) in enumerate(offsets):
            total = jnp.sum(sums[k], axis=0, keepdims=True)
            if b:
                side = (west if b < 0 else east)[1 + a : 1 + a + CLAT, lanes]
                edge = cols[0 if b < 0 else 1, :, lanes].astype(f32)
                total = total + jnp.sum(side * edge, axis=0, keepdims=True)
            parts[DEPTH + k : DEPTH + k + 1, lanes] = total

    def side_rows(i, carry):
        index = lax.broadcasted_iota(i32, (16, C), 0)
        for side, row in ((0, 0), (1, CLON - 16)):
            at = pl.ds(pl.multiple_of(i * CLON + row, 16), 16)
            whole = (ends[side, i, 0:1, :] + sides[side, i, 0:1, :]).astype(bf16).astype(f32)
            old = mixed[at, :].astype(f32)
            mixed[at, :] = jnp.where(index == 15 * side, whole, old).astype(bf16)
        return carry

    lax.fori_loop(0, CLAT, side_rows, 0)
    parts[SPEC:DEPTH, :] = jnp.zeros((DEPTH - SPEC, C), f32)
    parts[DEPTH + 9 : ROWS_IN, :] = jnp.zeros((ROWS_IN - DEPTH - 9, C), f32)

    lines = {IN: lines_in, OUT: lines_out, POINT: lines_point}
    quarter = {IN: quarter_in, OUT: quarter_out, POINT: quarter_point}
    gathers = {IN: gather_in, OUT: gather_out, POINT: gather_point}

    def half_of(r, which):
        return pl.ds(pl.multiple_of(r.first + which * r.half, 16), r.half)

    def local_half(r):
        return pl.ds(r.base, r.half)

    def swap_halves(r):
        swap_out[local_half(r), :] = parts[half_of(r, 1 - core), :].astype(bf16)
        copy = cross(swap_out.at[local_half(r)], swap_in.at[local_half(r)], r.sems[0], place.sibling)
        copy.start()
        return copy

    def rows_at(start, size):
        return pl.ds(pl.multiple_of(start, 16), size)

    def send_line(r):
        here = local_half(r)
        chip_sum[here, :] = (
            parts[half_of(r, core), :] + swap_in[here, :].astype(f32)
        ).astype(bf16)
        at, device = r.line(place)
        for step in range(1, 4):
            q = (at + step) % 4
            src = chip_sum.at[rows_at(r.base + q * r.quarter, r.quarter)]
            cross(src, lines[r].at[at], r.sems[1], device(q)).start()

    def piece(r, start, index):
        rows_here = rows_at(start + index // r.across * 16, 16)
        return rows_here, pl.ds(pl.multiple_of(index % r.across * r.width, 128), r.width)

    def waiting(r, size, sem):
        some = gathers[r].at[pl.ds(0, size)]
        return cross(some, some, r.sems[sem], place.sibling)

    def waiting_line(r, sem):
        some = lines[r].at[pl.ds(0, 3)]
        return cross(some, some, r.sems[sem], place.sibling)

    def send_plane(r):
        waiting_line(r, 1).wait_recv()
        at, _ = r.line(place)
        total = chip_sum[rows_at(r.base + at * r.quarter, r.quarter), :].astype(f32)
        for step in range(1, 4):
            total = total + lines[r][(at + step) % 4].astype(f32)
        quarter[r][...] = total.astype(bf16)
        me_here, device = r.plane(place)

        def send(step, carry):
            index = (me_here + step) % 16

            @pl.when(index < r.count)
            def _():
                where = piece(r, 0, index)
                cross(quarter[r].at[where], gathers[r].at[me_here], r.sems[2], device(index)).start()

            return carry

        lax.fori_loop(1, 16, send, 0)

    def result_rows(r):
        return r.first + core * r.half + r.line(place)[0] * r.quarter

    def share_plane(r):
        me_here, device = r.plane(place)

        @pl.when(me_here < r.count)
        def _():
            waiting(r, 15, 2).wait_recv()
            total = quarter[r][piece(r, 0, me_here)].astype(f32)
            for step in range(1, 16):
                total = total + gathers[r][(me_here + step) % 16].astype(f32)
            where = piece(r, result_rows(r), me_here)
            result[where] = total.astype(bf16)

            def share(step, carry):
                index = (me_here + step) % 16
                cross(result.at[where], result.at[where], r.sems[3], device(index)).start()
                return carry

            lax.fori_loop(1, 16, share, 0)

    def share_line(r):
        me_here, _ = r.plane(place)
        if r.count == 16:
            waiting(r, 15, 3).wait_recv()
        else:
            pl.when(me_here < r.count)(lambda: waiting(r, r.count - 1, 3).wait_recv())
            pl.when(me_here >= r.count)(lambda: waiting(r, r.count, 3).wait_recv())
        at, device = r.line(place)
        here = result.at[rows_at(result_rows(r), r.quarter)]
        for step in range(1, 4):
            cross(here, here, r.sems[4], device((at + step) % 4)).start()

    def last_swap(r):
        waiting_line(r, 4).wait_recv()
        half = result.at[half_of(r, core)]
        copy = cross(half, half, r.sems[5], place.sibling)
        copy.start()
        return copy

    def sent(r):
        waiting_line(r, 1).wait_send()
        waiting_line(r, 4).wait_send()
        me_here, _ = r.plane(place)

        def owner():
            waiting(r, r.count - 1, 2).wait_send()
            waiting(r, 15, 3).wait_send()

        if r.count == 16:
            owner()
        else:
            pl.when(me_here < r.count)(owner)
            pl.when(me_here >= r.count)(lambda: waiting(r, r.count, 2).wait_send())

    def point(i):
        at = slice(i * 512, (i + 1) * 512)
        here = grid_ext[1 + 4 * i : 5 + 4 * i].astype(f32).reshape(512, C)
        latent_here[at, :] = (here + dot(mixed[at, :], w_point[...], ((1,), (0,)))).astype(bf16)


    keep_back.wait()
    all_back = cross(g_arrived.at[some], returned.at[some], BACK, place.sibling)
    all_back.wait_recv()

    def gathered(key):
        total = jnp.zeros((OBS, C), f32)
        for at in range(0, SLOTS, PART):
            index = lax.broadcasted_iota(i32, (PART, OBS), 0) + at
            pick = (index == key).astype(f32).astype(bf16)
            total = total + dot(pick, returned[at : at + PART, :], ((0,), (0,)))
        return total

    part[...] = gathered(slot_keys(route_sib[...], core, 1 - core)).astype(bf16)
    swap = cross(part, part_sib, SIB_PART, place.sibling)
    swap.start()
    parts[POINT.first : PARTS, :] = dot(mixed[...], cot[...], ((0,), (0,)))
    point_swap = swap_halves(POINT)
    own = gathered(slot_keys(route[...], core, core))
    swap.wait()
    g_emb[...] = (own + part_sib[...].astype(f32)).astype(bf16)
    parts[OUT.first : OUT.first + C, :] = dot(hidden[...], g_emb[...], ((0,), (0,)))
    out_swap = swap_halves(OUT)
    g_hidden = dot(g_emb[...], w_out[...], ((1,), (1,)))
    pre = preact[...]
    sig = 1.0 / (1.0 + jnp.exp(-pre))
    g_pre = (g_hidden * sig * (1.0 + pre * (1.0 - sig))).astype(bf16)
    parts[0:SPEC, :] = dot(spec_t[...], g_pre, ((1,), (0,)))
    in_swap = swap_halves(IN)
    point_swap.wait()
    send_line(POINT)
    out_swap.wait()
    send_line(OUT)
    in_swap.wait()
    send_line(IN)
    point(0)
    send_plane(POINT)
    send_plane(OUT)
    send_plane(IN)
    point(1)
    share_plane(POINT)
    share_plane(OUT)
    share_plane(IN)
    point(2)
    share_line(POINT)
    share_line(OUT)
    share_line(IN)
    point(3)
    store = pltpu.make_async_copy(latent_here, latent, local_sem.at[6])
    store.start()
    rounds = (POINT, OUT, IN)

    def leave(r, which, index):
        half = half_of(r, which)
        return pltpu.make_async_copy(result.at[half], sums_out.at[half], out_sem.at[index])

    last, leaving = [], []
    for i, r in enumerate(rounds):
        last.append(last_swap(r))
        leaving.append(leave(r, core, i))
        leaving[-1].start()
    for r in rounds:
        sent(r)
    store.wait()
    for copy in (lat_marks, lon_marks, all_data, all_back):
        copy.wait_send()
    for i, r in enumerate(rounds):
        last[i].wait()
        leaving.append(leave(r, 1 - core, 3 + i))
        leaving[-1].start()
    for copy in leaving:
        copy.wait()


def run(spec_t, owner, cell, w_in, w_out, w_point, w_depth, cot):
    dma = pltpu.SemaphoreType.DMA
    anywhere = pl.BlockSpec(memory_space=pl.ANY)
    field = VMEM((CLAT + 2, CLON, C), bf16)
    half = VMEM((PARTS // 2, C), bf16)
    return pl.pallas_call(
        kernel,
        out_shape=[
            pltpu.VMEM((CELLS, C), bf16),
            pltpu.VMEM((PARTS, C), bf16),
        ],
        in_specs=[anywhere, vmem(), vmem(), anywhere, anywhere, anywhere, vmem(), anywhere],
        out_specs=[anywhere, anywhere],
        scratch_shapes=[
            VMEM((SPEC, OBS), bf16),
            VMEM((SPEC, C), bf16),
            VMEM((C, C), bf16),
            VMEM((C, C), bf16),
            VMEM((CELLS, C), bf16),
            VMEM((OBS, C), f32),
            VMEM((OBS, C), bf16),
            VMEM((OBS, C + META), bf16),
            VMEM((OBS, C + META), bf16),
            VMEM((8, OBS), i32),
            VMEM((8, OBS), i32),
            VMEM((SLOTS, C), bf16),
            VMEM((SLOTS, C), bf16),
            VMEM((N_LAT, N_LON, META), f32),
            VMEM((N_LAT, N_LON, META), f32),
            VMEM((N_LON, N_LAT, META), f32),
            VMEM((N_LON, N_LAT, META), f32),
            field,
            field,
            VMEM((2, CLAT, C), bf16),
            VMEM((2, CLAT, C), bf16),
            VMEM((4, CLAT, C), bf16),
            VMEM((2, CLAT, C), bf16),
            VMEM((2, CLAT, C), bf16),
            VMEM((4, CLAT, C), bf16),
            VMEM((24, C), f32),
            VMEM((24, C), f32),
            VMEM((2, CLAT, 8, C), f32),
            VMEM((2, CLAT, 8, C), f32),
            VMEM((C // CHUNK, 9, 8, CHUNK), f32),
            VMEM((CELLS, C), bf16),
            VMEM((SLOTS, C), bf16),
            VMEM((SLOTS, C), bf16),
            VMEM((OBS, C), bf16),
            VMEM((OBS, C), bf16),
            VMEM((OBS, C), bf16),
            VMEM((CELLS, C), bf16),
            VMEM((PARTS, C), f32),
            half,
            half,
            half,
        ]
        + [VMEM((4, r.quarter, C), bf16) for r in (IN, OUT, POINT)]
        + [VMEM((r.quarter, C), bf16) for r in (IN, OUT, POINT)]
        + [VMEM((16, 16, r.width), bf16) for r in (IN, OUT, POINT)]
        + [
            VMEM((CELLS, C), bf16),
            VMEM((PARTS, C), bf16),
            dma((6,)),
            dma((5,)),
            dma((7,)),
            dma((SEMS,)),
            dma((SEMS,)),
            dma((2, 8)),
            dma((2, 8)),
        ],
        compiler_params=pltpu.CompilerParams(
            collective_id=0, has_side_effects=True, vmem_limit_bytes=51 << 20
        ),
    )(spec_t, owner, cell, w_in, w_out, w_point, w_depth, cot)


def finish_kernel(latent_in, total, latent, g_in, g_out, g_point, g_depth, in_f, out_f, point_f, sem):
    obs_scale = 1.0 / math.sqrt(OBS * N_LAT * N_LON)
    cell_scale = 1.0 / math.sqrt(CELLS * N_LAT * N_LON)
    copies = [pltpu.make_async_copy(latent_in, latent, sem.at[3])]
    copies[0].start()
    plan = (
        (in_f, g_in, IN.first, obs_scale),
        (out_f, g_out, OUT.first, obs_scale),
        (point_f, g_point, POINT.first, cell_scale),
    )
    for i, (values, target, first, scale) in enumerate(plan):
        values[...] = total[first : first + values.shape[0], :].astype(f32) * scale
        copies.append(pltpu.make_async_copy(values, target, sem.at[i]))
        copies[-1].start()
    g_depth[...] = total[DEPTH : DEPTH + 16, :].astype(f32)[0:9] * cell_scale
    for copy in copies:
        copy.wait()


def finish(latent, total):
    anywhere = pl.BlockSpec(memory_space=pl.ANY)
    shapes = [(SPEC, C), (C, C), (C, C), (9, C)]
    return pl.pallas_call(
        finish_kernel,
        out_shape=[jax.ShapeDtypeStruct((CELLS, C), bf16)]
        + [jax.ShapeDtypeStruct(shape, f32) for shape in shapes],
        in_specs=[vmem(), vmem()],
        out_specs=[anywhere] * 4 + [vmem()],
        scratch_shapes=[VMEM(shape, f32) for shape in shapes[:3]] + [pltpu.SemaphoreType.DMA((4,))],
        compiler_params=pltpu.CompilerParams(vmem_limit_bytes=12 << 20),
    )(latent, total)


def on_device(spectra, owner, cell, w_in, w_out, w_point, w_depth, cotangent):
    latent, total = run(
        spectra.T,
        owner.reshape(1, OBS),
        cell.reshape(1, OBS),
        w_in,
        w_out,
        w_point,
        w_depth,
        cotangent.reshape(CELLS, C),
    )
    latent, *grads = finish(latent, total)
    return (latent.reshape(CLAT, CLON, C), *grads)


def solution(mesh):
    in_specs = (
        P(("lat", "lon"), None),
        P(("lat", "lon"), None),
        P(("lat", "lon")),
        P(),
        P(),
        P(),
        P(),
        P("lat", "lon", None),
    )
    out_specs = (P("lat", "lon", None), P(), P(), P(), P())
    return jax.shard_map(
        on_device, mesh=mesh, in_specs=in_specs, out_specs=out_specs, check_vma=False
    )
```
